32 devices in a mesh: dp: 8 (over z, y), seq: 4 (over x, core).
Axes of the slice: x: 2, y: 2, z: 4, core: 2. Of those that a mesh axis runs over, the one named last changes fastest.
Arguments:
- tokens: float32 [8, 4096, 512], P('dp', 'seq'), may hold values from -6 to 6
- cotangent: float32 [8, 4096, 512], P('dp', 'seq'), may hold values from -6 to 6
- lengths: int32 [8, 6], P('dp'), may hold values from 1 to 4091, as said below
- routes: int32 [8, 4096, 2], P('dp', 'seq'), may hold values from 0 to 7, all different within a row
- router_weight: float32 [512, 8], P(('dp', 'seq')), may hold values from -0.1875 to 0.1875
- query_weight: float32 [512, 512], P(('dp', 'seq')), may hold values from -0.375 to 0.375
- out_weight: float32 [512, 512], P(('dp', 'seq')), may hold values from -3 to 3
- kv_weight: float32 [512, 128], P(('dp', 'seq')), may hold values from -0.375 to 0.375
- up_weight: float32 [512, 2048], P(('dp', 'seq')), may hold values from -0.25 to 0.25
- up_bias: float32 [2048], P(('dp', 'seq')), may hold values from -2 to 2
- down_weight: float32 [2048, 512], P(('dp', 'seq')), may hold values from -0.125 to 0.125
- vectors: float32 [5, 512], P(None, ('dp', 'seq'))
- router_moment: float32 [512, 8], P(('dp', 'seq')), may hold values from -2 to 2
- query_moment: float32 [512, 512], P(('dp', 'seq')), may hold values from -2 to 2
- out_moment: float32 [512, 512], P(('dp', 'seq')), may hold values from -2 to 2
- kv_moment: float32 [512, 128], P(('dp', 'seq')), may hold values from -2 to 2
- up_moment: float32 [512, 2048], P(('dp', 'seq')), may hold values from -2 to 2
- bias_moment: float32 [2048], P(('dp', 'seq')), may hold values from -2 to 2
- down_moment: float32 [2048, 512], P(('dp', 'seq')), may hold values from -2 to 2
- vector_moment: float32 [5, 512], P(None, ('dp', 'seq')), may hold values from -2 to 2
- router_average: float32 [512, 8], P(('dp', 'seq')), may hold values from -0.1875 to 0.1875
- query_average: float32 [512, 512], P(('dp', 'seq')), may hold values from -0.375 to 0.375
- out_average: float32 [512, 512], P(('dp', 'seq')), may hold values from -3 to 3
- kv_average: float32 [512, 128], P(('dp', 'seq')), may hold values from -0.375 to 0.375
- up_average: float32 [512, 2048], P(('dp', 'seq')), may hold values from -0.25 to 0.25
- bias_average: float32 [2048], P(('dp', 'seq')), may hold values from -2 to 2
- down_average: float32 [2048, 512], P(('dp', 'seq')), may hold values from -0.125 to 0.125
- vector_average: float32 [5, 512], P(None, ('dp', 'seq')), may hold values from -3 to 3
Outputs:
- output: float32 [8, 4096, 512], P('dp', 'seq')
- input_grad: float32 [8, 4096, 512], P('dp', 'seq')
- new_router: float32 [512, 8], P(('dp', 'seq'))
- new_query: float32 [512, 512], P(('dp', 'seq'))
- new_out: float32 [512, 512], P(('dp', 'seq'))
- new_kv: float32 [512, 128], P(('dp', 'seq'))
- new_up: float32 [512, 2048], P(('dp', 'seq'))
- new_bias: float32 [2048], P(('dp', 'seq'))
- new_down: float32 [2048, 512], P(('dp', 'seq'))
- new_vectors: float32 [5, 512], P(None, ('dp', 'seq'))
- new_router_moment: float32 [512, 8], P(('dp', 'seq'))
- new_query_moment: float32 [512, 512], P(('dp', 'seq'))
- new_out_moment: float32 [512, 512], P(('dp', 'seq'))
- new_kv_moment: float32 [512, 128], P(('dp', 'seq'))
- new_up_moment: float32 [512, 2048], P(('dp', 'seq'))
- new_bias_moment: float32 [2048], P(('dp', 'seq'))
- new_down_moment: float32 [2048, 512], P(('dp', 'seq'))
- new_vector_moment: float32 [5, 512], P(None, ('dp', 'seq'))
- new_router_average: float32 [512, 8], P(('dp', 'seq'))
- new_query_average: float32 [512, 512], P(('dp', 'seq'))
- new_out_average: float32 [512, 512], P(('dp', 'seq'))
- new_kv_average: float32 [512, 128], P(('dp', 'seq'))
- new_up_average: float32 [512, 2048], P(('dp', 'seq'))
- new_bias_average: float32 [2048], P(('dp', 'seq'))
- new_down_average: float32 [2048, 512], P(('dp', 'seq'))
- new_vector_average: float32 [5, 512], P(None, ('dp', 'seq'))
The draws below stay inside these ranges and needn't reach their ends.
Inputs may be any that keep to these rules, and one draw needn't show every extreme that they name: Each row's 6 lengths sum to 4096; in every row one sentence starts among the first 1024 positions and ends among the last 1024. `routes`: the 2 experts of one token differ from each other; across the positions of a row the same experts repeat, and every expert is chosen somewhere.
All inputs are finite; a program needn't handle non-finite values.
Results may differ from the reference program's by a relative error of at most 0.0003.
Values sent between devices are 32-bit elements; how exact they have to be, the bound alone decides.
A program may use at most 320 MiB of HBM per device.

```python
import math
import jax
import jax.numpy as jnp
from jax import lax

D = 512
HD = 64
EXPERTS = 8
FF = 2048
TOP = 2
SENTS = 6
SEQ_DEV = 1024
LENGTH = 4096
ROWS = 8
TOKENS = 32768


def draw_lengths(key, part):
    key = jax.random.fold_in(key, 7)
    pick_key, size_key = jax.random.split(key)
    longest = jax.random.randint(pick_key, (ROWS, 1), 0, SENTS)
    most_short = max(1, (SEQ_DEV - 1) // (SENTS - 1))
    shorts = jax.random.randint(size_key, (ROWS, SENTS), 1, most_short + 1)
    places = jnp.arange(SENTS, dtype=jnp.int32)[None, :]
    shorts = jnp.where(places == longest, 0, shorts)
    remain = LENGTH - jnp.sum(shorts, axis=1, keepdims=True)
    return jnp.where(places == longest, remain, shorts).astype(jnp.int32)


def draw_vectors(key, part):
    key = jax.random.fold_in(key, 11)
    gain_key, shift_key = jax.random.split(key)
    gains = jax.random.uniform(gain_key, (5, D), jnp.float32, 0.6, 1.4)
    shifts = 0.3 * jax.random.normal(shift_key, (5, D), jnp.float32)
    places = jnp.arange(5)[:, None]
    return jnp.where((places == 0) | (places == 2), gains, shifts)


def levels(own_key, dims, cuts, smallest, top_value):
    def one(dim, shards_of):
        draws = jax.random.uniform(jax.random.fold_in(jax.random.fold_in(own_key, 6), dim), (shards_of,), jnp.float32, smallest / len(cuts), top_value / len(cuts))
        return jnp.repeat(jnp.exp(draws), dims[dim] // shards_of).reshape((-1,) + (1,) * (len(dims) - dim - 1))

    level = one(*cuts[0])
    for cut in cuts[1:]:
        level = level * one(*cut)
    return level


def distinct(key, rows, count, top, lift):
    sequence = jax.random.permutation(jax.random.fold_in(key, 1), count)
    boost = sequence
    for power in range(3):
        boost = boost * boost // count
    boost = boost * lift // count
    lots = jax.random.randint(jax.random.fold_in(key, 2), (rows, count), 0, 4096) + boost
    sure = jax.random.permutation(jax.random.fold_in(key, 3), rows)[jnp.arange(count) % rows]
    lots = jnp.where(jnp.arange(rows)[:, None] == sure[None, :], 1 << 14, lots)
    score = lots * count + jnp.arange(count)
    return lax.top_k(score.astype(jnp.int32), top)[1].astype(jnp.int32)


def bell_draw(rng, extent, width, reach, pieces=(), held_as=jnp.bfloat16):
    values = jax.random.normal(rng, extent, jnp.float32) * width
    if len(pieces) > 0:
        values = levels(rng, extent, pieces, -0.22, 0.18) * values
    return jnp.clip(values, min=-reach, max=reach).astype(held_as)


def setup_inputs(seed: int = 0) -> dict:
    arg_keys = jax.random.split(jax.random.key(seed), 29)
    tokens = bell_draw(arg_keys[0], (ROWS, LENGTH, D), 1.0, 6.0, ((0, 8), (1, 4)), jnp.float32)
    cotangent = bell_draw(arg_keys[1], (ROWS, LENGTH, D), 1.0, 6.0, ((0, 8), (1, 4)), jnp.float32)
    lengths = draw_lengths(jax.random.fold_in(arg_keys[28], 71), 0)
    routes = distinct(arg_keys[3], ROWS * LENGTH, EXPERTS, TOP, 0).reshape((ROWS, LENGTH, TOP))
    router_weight = bell_draw(arg_keys[4], (D, EXPERTS), (2 * D) ** -0.5, 0.1875, ((0, 32),), jnp.float32)
    query_weight = bell_draw(arg_keys[5], (D, EXPERTS * HD), (D // 2) ** -0.5, 0.375, ((0, 32),), jnp.float32)
    out_weight = bell_draw(arg_keys[6], (EXPERTS * HD, D), 0.5, 3.0, ((0, 32),), jnp.float32)
    kv_weight = bell_draw(arg_keys[7], (D, 2 * HD), (D // 2) ** -0.5, 0.375, ((0, 32),), jnp.float32)
    up_weight = bell_draw(arg_keys[8], (D, FF), D ** -0.5, 0.25, ((0, 32),), jnp.float32)
    up_bias = bell_draw(arg_keys[9], (FF,), 0.3, 2.0, ((0, 32),), jnp.float32)
    down_weight = bell_draw(arg_keys[10], (FF, D), FF ** -0.5, 0.125, ((0, 32),), jnp.float32)
    vectors = draw_vectors(jax.random.fold_in(arg_keys[28], 71), 0)
    router_moment = bell_draw(arg_keys[12], (D, EXPERTS), 0.3, 2.0, ((0, 32),), jnp.float32)
    query_moment = bell_draw(arg_keys[13], (D, EXPERTS * HD), 0.3, 2.0, ((0, 32),), jnp.float32)
    out_moment = bell_draw(arg_keys[14], (EXPERTS * HD, D), 0.3, 2.0, ((0, 32),), jnp.float32)
    kv_moment = bell_draw(arg_keys[15], (D, 2 * HD), 0.3, 2.0, ((0, 32),), jnp.float32)
    up_moment = bell_draw(arg_keys[16], (D, FF), 0.3, 2.0, ((0, 32),), jnp.float32)
    bias_moment = bell_draw(arg_keys[17], (FF,), 0.3, 2.0, ((0, 32),), jnp.float32)
    down_moment = bell_draw(arg_keys[18], (FF, D), 0.3, 2.0, ((0, 32),), jnp.float32)
    vector_moment = bell_draw(arg_keys[19], (5, D), 0.3, 2.0, ((1, 32),), jnp.float32)
    router_average = bell_draw(arg_keys[20], (D, EXPERTS), (2 * D) ** -0.5, 0.1875, ((0, 32),), jnp.float32)
    query_average = bell_draw(arg_keys[21], (D, EXPERTS * HD), (D // 2) ** -0.5, 0.375, ((0, 32),), jnp.float32)
    out_average = bell_draw(arg_keys[22], (EXPERTS * HD, D), 0.5, 3.0, ((0, 32),), jnp.float32)
    kv_average = bell_draw(arg_keys[23], (D, 2 * HD), (D // 2) ** -0.5, 0.375, ((0, 32),), jnp.float32)
    up_average = bell_draw(arg_keys[24], (D, FF), D ** -0.5, 0.25, ((0, 32),), jnp.float32)
    bias_average = bell_draw(arg_keys[25], (FF,), 0.3, 2.0, ((0, 32),), jnp.float32)
    down_average = bell_draw(arg_keys[26], (FF, D), FF ** -0.5, 0.125, ((0, 32),), jnp.float32)
    vector_average = bell_draw(arg_keys[27], (5, D), 0.5, 3.0, ((1, 32),), jnp.float32)
    return {"tokens": tokens, "cotangent": cotangent, "lengths": lengths, "routes": routes, "router_weight": router_weight, "query_weight": query_weight, "out_weight": out_weight, "kv_weight": kv_weight, "up_weight": up_weight, "up_bias": up_bias, "down_weight": down_weight, "vectors": vectors, "router_moment": router_moment, "query_moment": query_moment, "out_moment": out_moment, "kv_moment": kv_moment, "up_moment": up_moment, "bias_moment": bias_moment, "down_moment": down_moment, "vector_moment": vector_moment, "router_average": router_average, "query_average": query_average, "out_average": out_average, "kv_average": kv_average, "up_average": up_average, "bias_average": bias_average, "down_average": down_average, "vector_average": vector_average}


highest = lax.Precision.HIGHEST
norm_eps = 1e-05
step_rate = 0.02
moment_decay = 0.9
average_decay = 0.99

@jax.custom_vjp
def low(v):
    return lax.optimization_barrier(v.astype(jnp.bfloat16)).astype(jnp.float32)

@jax.custom_vjp
def low_back(v):
    return v

def low_keep(v):
    return (low(v), None)

def low_pass(kept, grad):
    return (grad,)

def back_keep(v):
    return (v, None)

def back_low(kept, grad):
    return (low(grad),)
low.defvjp(low_keep, low_pass)
low_back.defvjp(back_keep, back_low)

def matmul(left, right):
    return jnp.dot(left, right, precision=highest, preferred_element_type=jnp.float32)

def layer_norm(values, gain, shift):
    centre = values - lax.optimization_barrier(jnp.mean(values, axis=-1, keepdims=True))
    spread = lax.optimization_barrier(jnp.mean(centre * centre, axis=-1, keepdims=True))
    return centre * lax.rsqrt(spread + norm_eps) * gain + shift

def segment_ids(row_lengths, total):
    ends = jnp.cumsum(row_lengths)
    positions = jnp.arange(total, dtype=jnp.int32)
    return lax.optimization_barrier(jnp.sum((positions[:, None] >= ends[None, :]).astype(jnp.int32), axis=1))

def project_in(row_tokens, vectors, router_weight, query_weight, kv_weight, onehot):
    normed = layer_norm(row_tokens, vectors[0], vectors[1])
    logits = matmul(normed, router_weight)
    chosen = jnp.einsum('tke,te->tk', onehot, logits, precision=highest)
    gates = jax.nn.softmax(chosen, axis=-1)
    experts = onehot.shape[2]
    all_queries = matmul(normed, query_weight).reshape(normed.shape[0], experts, -1)
    queries = jnp.einsum('tke,ted->tkd', onehot, all_queries, precision=highest)
    keyval = matmul(normed, kv_weight)
    return (queries, keyval, gates)

def project_out(row_tokens, heads, gates, onehot, vectors, out_weight, up_weight, up_bias, down_weight):
    mixed = jnp.einsum('tk,tke,tkd->ted', gates, onehot, heads, precision=highest)
    mixed = mixed.reshape(row_tokens.shape[0], -1)
    middle = row_tokens + matmul(mixed, out_weight)
    normed = layer_norm(middle, vectors[2], vectors[3])
    hidden = jax.nn.gelu(matmul(normed, up_weight) + up_bias)
    return middle + matmul(hidden, down_weight) + vectors[4]

def attend_block(block_queries, block_segment, keys, values, key_segment):
    score_scale = block_queries.shape[-1] ** (-0.5)
    scores = jnp.einsum('tkd,sd->tks', block_queries, keys, precision=highest) * score_scale
    same_sent = block_segment[:, None, None] == key_segment[None, None, :]
    scores = jnp.where(same_sent, scores, -1e+30)
    weights_soft = jax.nn.softmax(scores, axis=-1)
    return jnp.einsum('tks,sd->tkd', weights_soft, values, precision=highest)

def row_forward(params, row_tokens, row_lengths, row_routes):
    router_weight, query_weight, out_weight, kv_weight, up_weight, up_bias, down_weight, vectors = params
    onehot = (row_routes[:, :, None] == jnp.arange(EXPERTS, dtype=jnp.int32)[None, None, :]).astype(jnp.float32)
    queries, keyval, gates = project_in(row_tokens, vectors, router_weight, query_weight, kv_weight, onehot)
    segment = segment_ids(row_lengths, LENGTH)
    keys = keyval[:, :HD]
    values = keyval[:, HD:]
    block = min(512, LENGTH)
    query_blocks = queries.reshape(LENGTH // block, block, TOP, HD)
    segment_blocks = segment.reshape(LENGTH // block, block)

    def one_block(pair):
        return attend_block(pair[0], pair[1], keys, values, segment)
    heads = lax.map(jax.checkpoint(one_block), (query_blocks, segment_blocks)).reshape(LENGTH, TOP, HD)
    return project_out(row_tokens, heads, gates, onehot, vectors, out_weight, up_weight, up_bias, down_weight)

def update(weight, gradient, moment, average):
    scaled = gradient * (1.0 / math.sqrt(TOKENS))
    moment_new = moment_decay * moment + scaled
    weight_new = weight - step_rate * (scaled + moment_decay * moment_new)
    average_new = average_decay * average + (1.0 - average_decay) * weight_new
    return (weight_new, moment_new, average_new)

def reference(tokens, cotangent, lengths, routes, router_weight, query_weight, out_weight, kv_weight, up_weight, up_bias, down_weight, vectors, router_moment, query_moment, out_moment, kv_moment, up_moment, bias_moment, down_moment, vector_moment, router_average, query_average, out_average, kv_average, up_average, bias_average, down_average, vector_average):
    params = (router_weight, query_weight, out_weight, kv_weight, up_weight, up_bias, down_weight, vectors)

    def step_row(totals, row_items):
        row_tokens, row_cotangent, row_lengths, row_routes = row_items

        def forward_of(weights_in, tokens_in):
            return row_forward(weights_in, tokens_in, row_lengths, row_routes)
        row_output, pull_back = jax.vjp(forward_of, params, row_tokens)
        weight_grads, token_grad = pull_back(row_cotangent)
        totals = jax.tree.map(jnp.add, totals, weight_grads)
        return (totals, (row_output, token_grad))
    zero_grads = jax.tree.map(jnp.zeros_like, params)
    gradients, (output, input_grad) = lax.scan(step_row, zero_grads, (tokens, cotangent, lengths, routes))
    new_router, new_router_moment, new_router_average = update(router_weight, gradients[0], router_moment, router_average)
    new_query, new_query_moment, new_query_average = update(query_weight, gradients[1], query_moment, query_average)
    new_out, new_out_moment, new_out_average = update(out_weight, gradients[2], out_moment, out_average)
    new_kv, new_kv_moment, new_kv_average = update(kv_weight, gradients[3], kv_moment, kv_average)
    new_up, new_up_moment, new_up_average = update(up_weight, gradients[4], up_moment, up_average)
    new_bias, new_bias_moment, new_bias_average = update(up_bias, gradients[5], bias_moment, bias_average)
    new_down, new_down_moment, new_down_average = update(down_weight, gradients[6], down_moment, down_average)
    new_vectors, new_vector_moment, new_vector_average = update(vectors, gradients[7], vector_moment, vector_average)
    return (output, input_grad, new_router, new_query, new_out, new_kv, new_up, new_bias, new_down, new_vectors, new_router_moment, new_query_moment, new_out_moment, new_kv_moment, new_up_moment, new_bias_moment, new_down_moment, new_vector_moment, new_router_average, new_query_average, new_out_average, new_kv_average, new_up_average, new_bias_average, new_down_average, new_vector_average)
```

```python
import functools
import math

import jax
import jax.numpy as jnp
from jax import lax
from jax.experimental import pallas as pl
from jax.experimental.pallas import tpu as pltpu
from jax.sharding import PartitionSpec as P

highest = lax.Precision.HIGHEST
norm_eps = 1e-05
step_rate = 0.02
moment_decay = 0.9
average_decay = 0.99


def matmul(left, right):
    return jnp.dot(left, right, precision=highest, preferred_element_type=jnp.float32)


def layer_norm(values, gain, shift):
    centre = values - jnp.mean(values, axis=-1, keepdims=True)
    spread = jnp.mean(centre * centre, axis=-1, keepdims=True)
    return centre * lax.rsqrt(spread + norm_eps) * gain + shift


def project_in(row_tokens, vectors, router_weight, query_weight, kv_weight, onehot):
    normed = layer_norm(row_tokens, vectors[0], vectors[1])
    logits = matmul(normed, router_weight)
    chosen = jnp.einsum("tke,te->tk", onehot, logits, precision=highest)
    gates = jax.nn.softmax(chosen, axis=-1)
    experts = onehot.shape[2]
    all_queries = matmul(normed, query_weight).reshape(normed.shape[0], experts, -1)
    queries = jnp.einsum("tke,ted->tkd", onehot, all_queries, precision=highest)
    keyval = matmul(normed, kv_weight)
    return (queries, keyval, gates)


def project_out(
    row_tokens, heads, gates, onehot, vectors, out_weight, up_weight, up_bias, down_weight
):
    mixed = jnp.einsum("tk,tke,tkd->ted", gates, onehot, heads, precision=highest)
    mixed = mixed.reshape(row_tokens.shape[0], -1)
    middle = row_tokens + matmul(mixed, out_weight)
    normed = layer_norm(middle, vectors[2], vectors[3])
    hidden = jax.nn.gelu(matmul(normed, up_weight) + up_bias)
    return middle + matmul(hidden, down_weight) + vectors[4]


def update(weight, gradient, moment, average, factor):
    scaled = gradient * factor
    moment_new = moment_decay * moment + scaled
    weight_new = weight - step_rate * (scaled + moment_decay * moment_new)
    average_new = average_decay * average + (1.0 - average_decay) * weight_new
    return (weight_new, moment_new, average_new)


def general_step(
    tokens,
    cotangent,
    lengths,
    routes,
    router_weight,
    query_weight,
    out_weight,
    kv_weight,
    up_weight,
    up_bias,
    down_weight,
    vectors,
    router_moment,
    query_moment,
    out_moment,
    kv_moment,
    up_moment,
    bias_moment,
    down_moment,
    vector_moment,
    router_average,
    query_average,
    out_average,
    kv_average,
    up_average,
    bias_average,
    down_average,
    vector_average,
):
    full_router, full_query, full_out, full_kv, full_up, full_bias, full_down, full_vectors = (
        lax.all_gather(router_weight, ("dp", "seq"), axis=0, tiled=True),
        lax.all_gather(query_weight, ("dp", "seq"), axis=0, tiled=True),
        lax.all_gather(out_weight, ("dp", "seq"), axis=0, tiled=True),
        lax.all_gather(kv_weight, ("dp", "seq"), axis=0, tiled=True),
        lax.all_gather(up_weight, ("dp", "seq"), axis=0, tiled=True),
        lax.all_gather(up_bias, ("dp", "seq"), axis=0, tiled=True),
        lax.all_gather(down_weight, ("dp", "seq"), axis=0, tiled=True),
        lax.all_gather(vectors, ("dp", "seq"), axis=1, tiled=True),
    )
    local_tokens = tokens[0]
    local_cotangent = cotangent[0]
    span = local_tokens.shape[0]
    row_length = span * lax.axis_size("seq")
    offset = lax.axis_index("seq") * span
    ends = jnp.cumsum(lengths[0])
    positions = jnp.arange(row_length, dtype=jnp.int32)
    segment_all = jnp.sum((positions[:, None] >= ends[None, :]).astype(jnp.int32), axis=1)
    segment_local = lax.dynamic_slice_in_dim(segment_all, offset, span)
    experts = full_router.shape[1]
    onehot = (routes[0][:, :, None] == jnp.arange(experts, dtype=jnp.int32)[None, None, :]).astype(
        jnp.float32
    )

    def front(tokens_in, vectors_in, router_in, query_in, kv_in):
        return project_in(tokens_in, vectors_in, router_in, query_in, kv_in, onehot)

    (queries, keyval, gates), front_pull = jax.vjp(
        front, local_tokens, full_vectors, full_router, full_query, full_kv
    )
    head_width = queries.shape[-1]
    choices_count = queries.shape[1]
    score_scale = head_width ** (-0.5)
    kv_piece = lax.all_gather(keyval, "seq", axis=0, tiled=True)
    best = jnp.full((span, choices_count), -1e30, jnp.float32)
    keys = kv_piece[:, :head_width]
    values = kv_piece[:, head_width:]
    key_segment = segment_all
    scores = jnp.einsum("tkd,sd->tks", queries, keys, precision=highest) * score_scale
    same_sent = segment_local[:, None, None] == key_segment[None, None, :]
    peak = jnp.maximum(best, jnp.max(jnp.where(same_sent, scores, -1e30), axis=-1))
    weights_soft = jnp.where(same_sent, jnp.exp(scores - peak[..., None]), 0.0)
    total = jnp.sum(weights_soft, axis=-1)
    accum = jnp.einsum("tks,sd->tkd", weights_soft, values, precision=highest)
    best, total, accum = (peak, total, accum)
    heads = accum / total[..., None]
    logsum = best + jnp.log(total)

    def tail(tokens_in, heads_in, gates_in, vectors_in, out_in, up_in, bias_in, down_in):
        return project_out(
            tokens_in, heads_in, gates_in, onehot, vectors_in, out_in, up_in, bias_in, down_in
        )

    output, tail_pull = jax.vjp(
        tail, local_tokens, heads, gates, full_vectors, full_out, full_up, full_bias, full_down
    )
    (
        tokens_grad_tail,
        heads_grad,
        gates_grad,
        vectors_grad_tail,
        out_grad,
        up_grad,
        bias_grad,
        down_grad,
    ) = tail_pull(local_cotangent)
    row_delta = jnp.sum(heads_grad * heads, axis=-1)
    kv_piece = lax.all_gather(keyval, "seq", axis=0, tiled=True)
    keys = kv_piece[:, :head_width]
    values = kv_piece[:, head_width:]
    key_segment = segment_all
    scores = jnp.einsum("tkd,sd->tks", queries, keys, precision=highest) * score_scale
    same_sent = segment_local[:, None, None] == key_segment[None, None, :]
    weights_soft = jnp.where(same_sent, jnp.exp(scores - logsum[..., None]), 0.0)
    weights_grad = jnp.einsum("tkd,sd->tks", heads_grad, values, precision=highest)
    scores_grad = weights_soft * (weights_grad - row_delta[..., None]) * score_scale
    query_grad = jnp.einsum("tks,sd->tkd", scores_grad, keys, precision=highest)
    keys_grad = jnp.einsum("tks,tkd->sd", scores_grad, queries, precision=highest)
    values_grad = jnp.einsum("tks,tkd->sd", weights_soft, heads_grad, precision=highest)
    joined = jnp.concatenate([keys_grad, values_grad], axis=1)
    keyval_grad = joined
    query_grad, keyval_partial = (query_grad, keyval_grad)
    keyval_grad = lax.psum_scatter(keyval_partial, "seq", scatter_dimension=0, tiled=True)
    tokens_grad_front, vectors_grad_front, router_grad, query_weight_grad, kv_grad = front_pull(
        (query_grad, keyval_grad, gates_grad)
    )
    input_grad = tokens_grad_tail + tokens_grad_front
    vectors_grad = vectors_grad_tail + vectors_grad_front
    shards = (
        router_weight,
        query_weight,
        out_weight,
        kv_weight,
        up_weight,
        up_bias,
        down_weight,
        vectors,
    )
    shard_dims = (0, 0, 0, 0, 0, 0, 0, 1)
    summed = lax.psum(
        (
            router_grad,
            query_weight_grad,
            out_grad,
            kv_grad,
            up_grad,
            bias_grad,
            down_grad,
            vectors_grad,
        ),
        ("dp", "seq"),
    )
    place = lax.axis_index(("dp", "seq"))
    reduced = tuple(
        (
            lax.dynamic_slice_in_dim(
                whole_grad, place * shard.shape[shard_dim], shard.shape[shard_dim], shard_dim
            )
            for whole_grad, shard, shard_dim in zip(summed, shards, shard_dims)
        )
    )
    all_tokens = span * lax.axis_size("seq") * tokens.shape[0] * lax.axis_size("dp")
    factor = 1.0 / math.sqrt(all_tokens)
    new_router, new_router_moment, new_router_average = update(
        router_weight, reduced[0], router_moment, router_average, factor
    )
    new_query, new_query_moment, new_query_average = update(
        query_weight, reduced[1], query_moment, query_average, factor
    )
    new_out, new_out_moment, new_out_average = update(
        out_weight, reduced[2], out_moment, out_average, factor
    )
    new_kv, new_kv_moment, new_kv_average = update(
        kv_weight, reduced[3], kv_moment, kv_average, factor
    )
    new_up, new_up_moment, new_up_average = update(
        up_weight, reduced[4], up_moment, up_average, factor
    )
    new_bias, new_bias_moment, new_bias_average = update(
        up_bias, reduced[5], bias_moment, bias_average, factor
    )
    new_down, new_down_moment, new_down_average = update(
        down_weight, reduced[6], down_moment, down_average, factor
    )
    new_vectors, new_vector_moment, new_vector_average = update(
        vectors, reduced[7], vector_moment, vector_average, factor
    )
    return (
        output[None],
        input_grad[None],
        new_router,
        new_query,
        new_out,
        new_kv,
        new_up,
        new_bias,
        new_down,
        new_vectors,
        new_router_moment,
        new_query_moment,
        new_out_moment,
        new_kv_moment,
        new_up_moment,
        new_bias_moment,
        new_down_moment,
        new_vector_moment,
        new_router_average,
        new_query_average,
        new_out_average,
        new_kv_average,
        new_up_average,
        new_bias_average,
        new_down_average,
        new_vector_average,
    )


f32 = jnp.float32
bf16 = jnp.bfloat16
MESH = pl.DeviceIdType.MESH
log2e = math.log2(math.e)
far = 2.0**100
vmem_limit = 60 * 2**20
NN = (((1,), (0,)), ((), ()))
NT = (((1,), (1,)), ((), ()))
TN = (((0,), (0,)), ((), ()))


def dot(left, right, dims=NN):
    return lax.dot_general(left, right, dims, preferred_element_type=f32)


def split(values):
    high = values.astype(bf16)
    return high, (values - high.astype(f32)).astype(bf16)


def split_wide(values):
    high = values.astype(bf16).astype(f32)
    return high, values - high


def cat(parts, axis):
    return jnp.concatenate(parts, axis=axis)


def dot_nn(left, right):
    return dot(cat([left[0], left[1], left[0]], 1), cat([right[0], right[0], right[1]], 0))


def dot_nt(left, right):
    return dot(cat([left[0], left[1], left[0]], 1), cat([right[0], right[0], right[1]], 1), NT)


def dot_tn(left, right):
    return dot(cat([left[0], left[1], left[0]], 0), cat([right[0], right[0], right[1]], 0), TN)


def iota(shape, dim):
    return lax.broadcasted_iota(jnp.int32, shape, dim)


def rows_at(index, count):
    return pl.ds(pl.multiple_of(index * count, count), count)


class Grid:
    def __init__(self, mesh):
        dp, seq = mesh.shape["dp"], mesh.shape["seq"]
        self.x = max(seq // 2, 1)
        self.y = self.x if dp % self.x == 0 else 1
        self.z = dp // self.y
        self.count = dp * seq
        self.lead = (self.z, self.y, self.x, 2)

    def here(self):
        dp, seq = lax.axis_index("dp"), lax.axis_index("seq")
        return dp // self.y, dp % self.y, seq // 2, seq % 2

    def device(self, z, y, x, core):
        return (z * self.y + y, x * 2 + core)

    def others(self, axis):
        z, y, x, core = self.here()
        if axis == "z":
            return [self.device((z + i) % self.z, y, x, core) for i in range(1, self.z)]
        if axis == "y":
            return [self.device(z, (y + i) % self.y, x, core) for i in range(1, self.y)]
        if axis == "x":
            return [self.device(z, y, (x + i) % self.x, core) for i in range(1, self.x)]
        return [self.device(z, y, x, 1 - core)]

    def copies(self):
        return self.z + self.y + self.x - 2

    def barrier(self):
        barrier = pltpu.get_barrier_semaphore()
        count = 0
        for axis in "zyxc":
            for device in self.others(axis):
                pl.semaphore_signal(barrier, inc=1, device_id=device, device_id_type=MESH)
                count += 1
        pl.semaphore_wait(barrier, count)


class Sends:
    def __init__(self, send, recv):
        self.send, self.recv, self.used, self.started = send, recv, 0, []

    def start(self, source, target, device):
        copy = pltpu.make_async_remote_copy(
            src_ref=source,
            dst_ref=target,
            send_sem=self.send.at[self.used],
            recv_sem=self.recv.at[self.used],
            device_id=device,
            device_id_type=MESH,
        )
        self.used += 1
        copy.start()
        self.started.append(copy)
        return copy

    def finish(self):
        for copy in self.started:
            copy.wait_send()


class Gather:
    def __init__(self, grid, source, target, order, local, send, recv):
        self.grid, self.source, self.target, self.order = grid, source, target, order
        self.local, self.sends, self.current = local, Sends(send, recv), []

    def start(self):
        z, y, x, core = self.grid.here()
        mine = self.target.at[z, y, x, core]
        self.own = pltpu.make_async_copy(self.source, mine, self.local)
        self.own.start()
        self.current = [
            self.sends.start(self.source, mine, device) for device in self.grid.others("z")
        ]

    def wait(self):
        for copy in self.current:
            copy.wait_recv()
        self.current = []

    def step(self, number):
        z, y, x, core = self.grid.here()
        self.wait()
        if number == 0:
            self.own.wait()
            view = self.target.at[:, y, x, core]
        elif number == 1:
            view = self.target.at[:, :, x, core] if self.order[0] == "y" else self.target.at[:, y, :, core]
        else:
            view = self.target.at[:, :, :, core]
        axis = (self.order + "c")[number]
        self.current = [self.sends.start(view, view, device) for device in self.grid.others(axis)]

    def finish(self):
        self.wait()
        self.sends.finish()


class Reduce:
    def __init__(self, grid, source, order, held, parts, local, send, recv):
        self.grid, self.source, self.order, self.held = grid, source, order, held
        self.parts, self.local, self.sends, self.current = parts, local, Sends(send, recv), []

    def start(self):
        z, y, x, core = self.grid.here()
        self.own = pltpu.make_async_copy(self.source.at[:, :, :, core], self.held, self.local)
        self.own.start()
        device = self.grid.others("c")[0]
        self.current = [
            self.sends.start(self.source.at[:, :, :, 1 - core], self.parts[0].at[0], device)
        ]

    def take(self, view, parts):
        for copy in self.current:
            copy.wait_recv()
        for i in range(len(self.current)):
            view[...] += parts[i]

    def step(self, number):
        z, y, x, core = self.grid.here()
        held, first = self.held, self.order[0]
        if number == 0:
            self.own.wait()
            view = held
        elif number == 1:
            view = held.at[:, y] if first == "y" else held.at[:, :, x]
        else:
            view = held.at[:, y, x]
        self.take(view, self.parts[number])
        axis = (self.order + "z")[number]
        devices = self.grid.others(axis)
        self.current = []
        for i, device in enumerate(devices):
            if axis == "z":
                part = held.at[(z + i + 1) % self.grid.z, y, x]
            elif axis == "y":
                other = (y + i + 1) % self.grid.y
                part = held.at[:, other] if number == 0 else held.at[:, other, x]
            else:
                other = (x + i + 1) % self.grid.x
                part = held.at[:, :, other] if number == 0 else held.at[:, y, other]
            self.current.append(self.sends.start(part, self.parts[number + 1].at[i], device))

    def result(self):
        z, y, x, core = self.grid.here()
        for copy in self.current:
            copy.wait_recv()
        total = self.held[z, y, x]
        for i in range(len(self.current)):
            total = total + self.parts[3][i]
        return total

    def finish(self):
        self.sends.finish()


def reduce_scratch(grid, shape, order):
    z, y, x = grid.z, grid.y, grid.x
    first = y if order[0] == "y" else x
    second = x if order[0] == "y" else y
    return [
        pltpu.VMEM((z, y, x) + shape, f32),
        pltpu.VMEM((1, z, y, x) + shape, f32),
        pltpu.VMEM((first - 1, z, second) + shape, f32),
        pltpu.VMEM((second - 1, z) + shape, f32),
        pltpu.VMEM((z - 1,) + shape, f32),
    ]


def vmem_specs(count):
    return [pl.BlockSpec(memory_space=pltpu.VMEM)] * count


def any_specs(count):
    return [pl.BlockSpec(memory_space=pl.ANY)] * count


def sentence_bounds(lengths, marks, first):
    start = jnp.zeros(marks.shape, jnp.int32)
    end = jnp.zeros(marks.shape, jnp.int32)
    at = jnp.int32(0)
    for e in range(lengths.shape[1]):
        after = at + lengths[0, e]
        start = jnp.where(marks == first + e, at, start)
        end = jnp.where(marks == first + e, after, end)
        at = after
    return start, end


def in_sentence(positions, start, end):
    return jnp.logical_and(positions >= start, positions < end).astype(f32)


def query_pack(transposed, extra):
    high, low = split(transposed[: transposed.shape[0] // 2])
    return cat([high, low, high, extra.astype(bf16)], 0)


def key_pack(doubled, extra):
    lanes = iota(doubled.shape, 1)
    half = doubled.shape[1] // 2
    high, low = split_wide(doubled)
    return cat([high.astype(bf16), jnp.where(lanes < half, low, extra).astype(bf16)], 1)


def half_split(doubled, axis):
    half = doubled.shape[axis] // 2
    high, low = split_wide(doubled)
    return jnp.where(iota(doubled.shape, axis) < half, high, low).astype(bf16)


def twice(pair):
    half = pair.shape[1] // 2
    turned = pltpu.roll(pair, half, 1)
    lanes = iota(pair.shape, 1)
    return jnp.where(lanes < half, pair, turned), jnp.where(lanes < half, turned, pair)


def pick(wide, route, head):
    lanes = iota((wide.shape[0], 2 * head), 1) // head
    total = None
    for group in range(wide.shape[1] // (2 * head)):
        part = jnp.where(lanes + 2 * group == route, wide[:, group * 2 * head : (group + 1) * 2 * head], 0.0)
        total = part if total is None else total + part
    return total + pltpu.roll(total, head, 1)


def spread(doubled, route, experts):
    head = doubled.shape[1] // 2
    lanes = iota(doubled.shape, 1) // head
    return cat([jnp.where(lanes + 2 * group == route, doubled, 0.0) for group in range(experts // 2)], 1)


def normalise(values):
    centre = values - jnp.mean(values, axis=-1, keepdims=True)
    scale = lax.rsqrt(jnp.mean(centre * centre, axis=-1, keepdims=True) + norm_eps)
    return centre * scale, scale


def norm_back(grad, unit, scale, gain):
    inner = grad * gain
    mean = jnp.mean(inner, axis=-1, keepdims=True)
    along = jnp.mean(inner * unit, axis=-1, keepdims=True)
    return scale * (inner - mean - unit * along)


def forward_kernel(
    grid, head, experts,
    lengths, tokens, routes, packed, out_shard, up_shard, down_shard,
    front_all, vectors, bias, heads_out, queries, logsum, gates, keyval, out_all, up_all, down_all,
    high_w, low_w, query_t, key_p, value_t, scores, accum, peak, total, extra, even, odd,
    local, send, recv, kv_send, kv_recv,
):
    span, width = tokens.shape
    z, y, x, core = grid.here()
    grid.barrier()
    columns = packed.shape[1]
    half = columns // 2
    items = [
        (packed.at[:, :half], front_all.at[:, :, :, :, :, :half], "yx"),
        (packed.at[:, half:], front_all.at[:, :, :, :, :, half:], "xy"),
        (out_shard, out_all, "yx"),
        (up_shard.at[:, : up_shard.shape[1] // 2], up_all.at[:, :, :, :, :, : up_shard.shape[1] // 2], "yx"),
        (up_shard.at[:, up_shard.shape[1] // 2 :], up_all.at[:, :, :, :, :, up_shard.shape[1] // 2 :], "xy"),
        (down_shard.at[: down_shard.shape[0] // 2], down_all.at[:, :, :, :, : down_shard.shape[0] // 2], "yx"),
        (down_shard.at[down_shard.shape[0] // 2 :], down_all.at[:, :, :, :, down_shard.shape[0] // 2 :], "xy"),
    ]
    gathers = [
        Gather(grid, source, target, order, local.at[i], send.at[i], recv.at[i])
        for i, (source, target, order) in enumerate(items)
    ]
    front, rest = gathers[:2], gathers[2:]
    for item in front:
        item.start()
    for number in range(3):
        for item in front:
            item.step(number)
        if number == 0:
            for item in rest[:3]:
                item.start()
    for item in front:
        item.wait()
    for item in rest[3:]:
        item.start()
    whole = front_all[...].reshape(width, columns)
    high_w[...], low_w[...] = split(whole)
    wide = experts * head
    tail = whole[:, wide + 2 * head :]
    extra[...] = tail
    turned = tail.T
    vectors[...] = turned[8:16]
    shard = width // grid.count
    piece = bias.shape[1] // grid.count
    per_tile = 128 // piece
    pieces = extra[pl.ds(0, grid.count, stride=shard), :]
    even[...] = pltpu.roll(pieces, piece, 1)
    odd[...] = pieces
    lanes = iota((1, 128), 1)
    for q in range(bias.shape[1] // 128):
        bias[0:1, q * 128 : (q + 1) * 128] = jnp.where(
            lanes < piece, even[per_tile * q : per_tile * q + 1], odd[per_tile * q + 1 : per_tile * q + 2]
        )
    gain, shift = vectors[0:1], vectors[1:2]
    seq_at = (x * 2 + core) * span
    block = min(256, span)

    def project(i, carry):
        rows = rows_at(i, block)
        normed = normalise(tokens[rows])[0] * gain + shift
        result = dot_nn(split(normed), (high_w[...], low_w[...]))
        lane = iota((block, 2 * head), 1)
        picked_routes = [routes[rows, k : k + 1] for k in range(2)]
        logits = result[:, wide + 2 * head :]
        chosen = [
            jnp.sum(jnp.where(lane == route, logits, 0.0), axis=1, keepdims=True) for route in picked_routes
        ]
        top = jnp.maximum(chosen[0], chosen[1])
        raw = [jnp.exp(c - top) for c in chosen]
        norm = raw[0] + raw[1]
        gates[rows] = jnp.where(lane < head, raw[0] / norm, raw[1] / norm)
        keyval[x, core, rows] = result[:, wide : wide + 2 * head]
        marks = iota((head, 1), 0)
        start, end = sentence_bounds(lengths, marks, 0)
        positions = seq_at + i * block + iota((1, block), 1)
        inside = in_sentence(positions, start, end)
        for k in range(2):
            query = pick(result[:, :wide], picked_routes[k], head) * (log2e * head**-0.5)
            queries[rows_at(k * (span // block) + i, block)] = query
            query_t[:, rows_at(k * (span // block) + i, block)] = query_pack(query.T, inside)
        return carry

    lax.fori_loop(0, span // block, project, 0)
    moves = Sends(kv_send, kv_recv)
    mine = keyval.at[x, core]
    sibling = grid.others("c")[0]
    to_sibling = moves.start(mine, mine, sibling)
    across = [moves.start(mine, mine, device) for device in grid.others("x")]
    for item in rest[:3]:
        item.step(0)

    accum[...] = jnp.zeros_like(accum)
    peak[...] = jnp.full_like(peak, -3e38)
    total[...] = jnp.zeros_like(total)
    s_tile, t_tile = min(512, span), min(1024, 2 * span)
    s_count, t_count = span // s_tile, 2 * span // t_tile

    def attend(chunk_x, chunk_core):
        at = (chunk_x * 2 + chunk_core) * span

        def prepare(i, carry):
            rows = rows_at(i, block)
            keys, values = twice(keyval[chunk_x, chunk_core, rows])
            marks = iota((1, 2 * head), 1)
            start, end = sentence_bounds(lengths, marks, head)
            positions = at + i * block + iota((block, 1), 0)
            outside = jnp.where(marks - head < lengths.shape[1], (in_sentence(positions, start, end) - 1.0) * far, 0.0)
            key_p[rows] = key_pack(keys, outside)
            value_t[:, rows] = half_split(values.T, 0)
            return carry

        lax.fori_loop(0, span // block, prepare, 0)

        def tile(i, carry):
            s_rows = rows_at(i // t_count, s_tile)
            t_cols = rows_at(i % t_count, t_tile)
            scores[...] = dot(key_p[s_rows], query_t[:, t_cols])
            old = peak[0:1, t_cols]
            new = jnp.maximum(old, jnp.max(scores[...], axis=0, keepdims=True))
            fade = jnp.exp2(old - new)
            probs = jnp.exp2(scores[...] - new)
            high, low = split(probs)
            weights = value_t[:, s_rows]
            add = dot(cat([weights, weights], 1), cat([high, low], 0))
            total[0:1, t_cols] = total[0:1, t_cols] * fade + jnp.sum(probs, axis=0, keepdims=True)
            accum[:, t_cols] = accum[:, t_cols] * fade + add
            peak[0:1, t_cols] = new
            return carry

        lax.fori_loop(0, s_count * t_count, tile, 0)

    attend(x, core)
    to_sibling.wait_recv()
    for item in rest[:3]:
        item.step(1)
    forwards = []
    attend(x, 1 - core)
    for i in range(1, grid.x):
        across[i - 1].wait_recv()
        view = keyval.at[(x - i + grid.x) % grid.x, core]
        forward = moves.start(view, view, sibling)
        if i == 1:
            for item in rest[3:]:
                item.step(0)
        attend((x - i + grid.x) % grid.x, core)
        forward.wait_recv()
        if i == 1:
            for item in rest[:3]:
                item.step(2)
            for item in rest[3:]:
                item.step(1)
        attend((x - i + grid.x) % grid.x, 1 - core)
    for item in rest[3:]:
        item.step(2)

    def finish(i, carry):
        cols = rows_at(i, block)
        norm = total[0:1, cols]
        result = (accum[:head, cols] + accum[head:, cols]) / norm
        heads_out[cols] = cat([result, result], 0).T
        logsum[0:1, cols] = peak[0:1, cols] + jnp.log2(norm)
        return carry

    lax.fori_loop(0, 2 * span // block, finish, 0)
    for item in gathers:
        item.finish()
    moves.finish()


def forward(grid, experts, head, lengths, tokens, routes, packed, out_shard, up_shard, down_shard):
    span, width = tokens.shape
    columns = packed.shape[1]
    ff = up_shard.shape[1]
    lead = grid.lead
    shapes = [
        lead + packed.shape,
        (8, width),
        (1, ff),
        (2 * span, 2 * head),
        (2 * span, 2 * head),
        (1, 2 * span),
        (span, 2 * head),
        (grid.x, 2, span, 2 * head),
        lead + out_shard.shape,
        lead + up_shard.shape,
        lead + down_shard.shape,
    ]
    items = 7
    return pl.pallas_call(
        functools.partial(forward_kernel, grid, head, experts),
        out_shape=[jax.ShapeDtypeStruct(shape, f32) for shape in shapes],
        in_specs=[pl.BlockSpec(memory_space=pltpu.SMEM)] + vmem_specs(3) + any_specs(3),
        out_specs=vmem_specs(8) + any_specs(3),
        scratch_shapes=[
            pltpu.VMEM((width, columns), bf16),
            pltpu.VMEM((width, columns), bf16),
            pltpu.VMEM((4 * head, 2 * span), bf16),
            pltpu.VMEM((span, 4 * head), bf16),
            pltpu.VMEM((2 * head, span), bf16),
            pltpu.VMEM((min(512, span), min(1024, 2 * span)), f32),
            pltpu.VMEM((2 * head, 2 * span), f32),
            pltpu.VMEM((1, 2 * span), f32),
            pltpu.VMEM((1, 2 * span), f32),
            pltpu.VMEM((width, 128), f32),
            pltpu.VMEM((grid.count, 128), f32),
            pltpu.VMEM((grid.count, 128), f32),
            pltpu.SemaphoreType.DMA((items,)),
            pltpu.SemaphoreType.DMA((items, grid.copies())),
            pltpu.SemaphoreType.DMA((items, grid.copies())),
            pltpu.SemaphoreType.DMA((2 * grid.x - 1,)),
            pltpu.SemaphoreType.DMA((2 * grid.x - 1,)),
        ],
        compiler_params=pltpu.CompilerParams(
            collective_id=0, has_side_effects=True, vmem_limit_bytes=vmem_limit
        ),
        name="front_and_attention",
    )(lengths, tokens, routes, packed, out_shard, up_shard, down_shard)


def middle_kernel(
    head, experts,
    tokens, cotangent, heads, gates, routes, vectors, bias, out_w, up_w, down_w,
    output, middle_grad, up_grad, down_grad, out_grad, vector_grad, bias_grad, heads_grad, chosen_grad,
    out_h, out_l, up_h, up_l, down_h, down_l, norm_h, norm_l, cot_h, cot_l, unit, scale_ref, norm_grad,
):
    span, width = tokens.shape
    ff = up_w.shape[1]
    block, part = min(512, span), 512
    out_h[...], out_l[...] = split(out_w[...])

    def halve(i, carry):
        rows = rows_at(i, width // 4)
        up_h[rows], up_l[rows] = split(up_w[rows])
        rows = rows_at(i, ff // 4)
        down_h[rows], down_l[rows] = split(down_w[rows])
        return carry

    lax.fori_loop(0, 4, halve, 0)
    up_grad[...] = jnp.zeros_like(up_grad)
    down_grad[...] = jnp.zeros_like(down_grad)
    out_grad[...] = jnp.zeros_like(out_grad)
    vector_grad[...] = jnp.zeros_like(vector_grad)
    bias_grad[...] = jnp.zeros_like(bias_grad)
    gain, shift, last = vectors[2:3], vectors[3:4], vectors[4:5]

    def tokens_block(i, carry):
        rows = rows_at(i, block)
        second = rows_at(span // block + i, block)
        gate = gates[rows]
        turned = pltpu.roll(gate, head, 1)
        lane = iota(gate.shape, 1)
        gate_k = [jnp.where(lane < head, gate, turned), jnp.where(lane < head, turned, gate)]
        route = [routes[rows, k : k + 1] for k in range(2)]
        own = [heads[rows], heads[second]]
        mixed = sum(spread(gate_k[k] * own[k], route[k], experts) for k in range(2))
        mixed_s = split(mixed)
        middle = tokens[rows] + dot_nn(mixed_s, (out_h[...], out_l[...]))
        unit_v, scale = normalise(middle)
        unit[...] = unit_v
        scale_ref[...] = jnp.broadcast_to(scale, scale_ref.shape)
        norm_h[...], norm_l[...] = split(unit_v * gain + shift)
        cot = cotangent[rows]
        cot_h[...], cot_l[...] = split(cot)
        output[rows] = middle + last
        norm_grad[...] = jnp.zeros_like(norm_grad)

        def hidden_part(j, carry):
            cols = rows_at(j, part)
            cot_s = (cot_h[...], cot_l[...])
            norm_s = (norm_h[...], norm_l[...])
            up_s = (up_h[:, cols], up_l[:, cols])
            down_s = (down_h[cols], down_l[cols])
            pre = dot_nn(norm_s, up_s) + bias[0:1, cols]
            back = dot_nt(cot_s, down_s)
            square = pre * pre
            wave = jnp.tanh(math.sqrt(2.0 / math.pi) * (pre + 0.044715 * (square * pre)))
            half = 0.5 * (1.0 + wave)
            hidden_s = split(pre * half)
            slope = half + (0.5 * math.sqrt(2.0 / math.pi)) * pre * (1.0 - wave * wave) * (
                1.0 + (3.0 * 0.044715) * square
            )
            pre_grad = back * slope
            pre_s = split(pre_grad)
            output[rows] += dot_nn(hidden_s, down_s)
            norm_grad[...] += dot_nt(pre_s, up_s)
            down_grad[cols] += dot_tn(hidden_s, cot_s)
            up_grad[:, cols] += dot_tn(norm_s, pre_s)
            bias_grad[0:1, cols] += jnp.sum(pre_grad, axis=0, keepdims=True)
            return carry

        lax.fori_loop(0, ff // part, hidden_part, 0)
        grad = norm_grad[...]
        unit_v = unit[...]
        vector_grad[2:3] += jnp.sum(grad * unit_v, axis=0, keepdims=True)
        vector_grad[3:4] += jnp.sum(grad, axis=0, keepdims=True)
        vector_grad[4:5] += jnp.sum(cot, axis=0, keepdims=True)
        mid = cot + norm_back(grad, unit_v, scale_ref[:, 0:1], gain)
        middle_grad[rows] = mid
        mid_s = split(mid)
        out_grad[...] += dot_tn(mixed_s, mid_s)
        grad_mixed = dot_nt(mid_s, (out_h[...], out_l[...]))
        gates_grad = []
        for k in range(2):
            picked = pick(grad_mixed, route[k], head)
            gate_grad = jnp.sum(jnp.where(lane < head, picked * own[k], 0.0), axis=1, keepdims=True)
            gates_grad.append(gate_grad)
            delta = gate_grad * gate_k[k]
            heads_grad[rows_at(k * (span // block) + i, block)] = jnp.where(
                lane < head, gate_k[k] * picked, jnp.where(lane == head, delta, 0.0)
            )
        both = gate_k[0] * gates_grad[0] + gate_k[1] * gates_grad[1]
        chosen_grad[rows] = jnp.where(
            lane == 0, gate_k[0] * (gates_grad[0] - both), gate_k[1] * (gates_grad[1] - both)
        )
        return carry

    lax.fori_loop(0, span // block, tokens_block, 0)


def middle(experts, head, tokens, cotangent, heads, gates, routes, vectors, bias, out_w, up_w, down_w):
    span, width = tokens.shape
    ff = up_w.shape[1]
    block = min(512, span)
    shapes = [
        (span, width),
        (span, width),
        (width, ff),
        (ff, width),
        (experts * head, width),
        (8, width),
        (1, ff),
        (2 * span, 2 * head),
        (span, 2 * head),
    ]
    return pl.pallas_call(
        functools.partial(middle_kernel, head, experts),
        out_shape=[jax.ShapeDtypeStruct(shape, f32) for shape in shapes],
        in_specs=vmem_specs(10),
        out_specs=vmem_specs(9),
        scratch_shapes=[
            pltpu.VMEM(out_w.shape, bf16),
            pltpu.VMEM(out_w.shape, bf16),
            pltpu.VMEM(up_w.shape, bf16),
            pltpu.VMEM(up_w.shape, bf16),
            pltpu.VMEM(down_w.shape, bf16),
            pltpu.VMEM(down_w.shape, bf16),
            pltpu.VMEM((block, width), bf16),
            pltpu.VMEM((block, width), bf16),
            pltpu.VMEM((block, width), bf16),
            pltpu.VMEM((block, width), bf16),
            pltpu.VMEM((block, width), f32),
            pltpu.VMEM((block, 128), f32),
            pltpu.VMEM((block, width), f32),
        ],
        compiler_params=pltpu.CompilerParams(vmem_limit_bytes=vmem_limit),
        name="feed_forward",
    )(tokens, cotangent, heads, gates, routes, vectors, bias, out_w, up_w, down_w)


def backward_kernel(
    grid, head, experts,
    lengths, tokens, middle_grad, routes, front_all, keyval, queries, logsum, heads_grad, chosen_grad,
    vectors, vector_grad, bias_grad, up_grad, down_grad, out_grad,
    input_grad, front_sum, up_sum, down_sum, out_sum,
    query_t, query_n, grad_t, grad_n, key_p, value_p, key_t, query_grad, tile_k, tile_v,
    chunk_grad, chunk_in, cross_in, front_grad, high_w, low_w, extra, even, *rest,
):
    reduces, sems = rest[:25], rest[25:]
    local, send, recv, kv_send, kv_recv = sems
    span, width = tokens.shape
    z, y, x, core = grid.here()
    grid.barrier()
    columns = front_all.shape[-1]
    half = columns // 2
    wide = experts * head
    sources = [
        (up_grad, "yx"),
        (down_grad, "xy"),
        (out_grad, "yx"),
        (front_grad.at[:, :, :, :, :, :half], "yx"),
        (front_grad.at[:, :, :, :, :, half:], "xy"),
    ]
    items = [
        Reduce(grid, source, order, reduces[5 * i], reduces[5 * i + 1 : 5 * i + 5], local.at[i], send.at[i], recv.at[i])
        for i, (source, order) in enumerate(sources)
    ]
    early, late = items[:3], items[3:]
    for item in early:
        item.start()
    block = min(256, span)
    blocks = span // block
    seq_at = (x * 2 + core) * span

    def prepare_queries(i, carry):
        rows = rows_at(i, block)
        marks = iota((head, 1), 0)
        start, end = sentence_bounds(lengths, marks, 0)
        positions = seq_at + (i % blocks) * block + iota((1, block), 1)
        rest_ls = -logsum[0:1, rows]
        one = rest_ls.astype(bf16).astype(f32)
        two = (rest_ls - one).astype(bf16).astype(f32)
        three = rest_ls - one - two
        inside = in_sentence(positions, start, end)
        inside = jnp.where(marks == 8, one, jnp.where(marks == 9, two, jnp.where(marks == 10, three, inside)))
        query = queries[rows]
        query_t[:, rows] = query_pack(query.T, inside)
        query_n[rows] = half_split(query, 1)
        grad = heads_grad[rows]
        turned = grad.T
        rest_d = -turned[head : head + 1]
        one = rest_d.astype(bf16).astype(f32)
        two = (rest_d - one).astype(bf16).astype(f32)
        three = rest_d - one - two
        terms = jnp.where(marks == 0, one, jnp.where(marks == 1, two, jnp.where(marks == 2, three, 0.0)))
        grad_t[:, rows] = query_pack(turned, terms)
        grad_n[rows] = half_split(twice(grad)[0], 1)
        return carry

    lax.fori_loop(0, 2 * blocks, prepare_queries, 0)
    query_grad[...] = jnp.zeros_like(query_grad)
    s_tile, t_tile = min(512, span), min(512, span)
    t_count = 2 * span // t_tile

    def chunk(chunk_x, chunk_core, target):
        at = (chunk_x * 2 + chunk_core) * span

        def prepare(i, carry):
            rows = rows_at(i, block)
            keys, values = twice(keyval[chunk_x, chunk_core, rows])
            marks = iota((1, 2 * head), 1)
            start, end = sentence_bounds(lengths, marks, head)
            positions = at + i * block + iota((block, 1), 0)
            outside = jnp.where(marks - head < lengths.shape[1], (in_sentence(positions, start, end) - 1.0) * far, 0.0)
            ones = jnp.logical_and(marks - head >= 8, marks - head < 11)
            key_p[rows] = key_pack(keys, jnp.where(ones, 1.0, outside))
            few = jnp.logical_and(marks - head >= 0, marks - head < 3).astype(f32)
            value_p[rows] = key_pack(values, jnp.broadcast_to(few, values.shape))
            key_t[:, rows] = half_split(keys.T, 0)
            return carry

        lax.fori_loop(0, blocks, prepare, 0)

        def key_rows(i, carry):
            s_rows = rows_at(i, s_tile)
            tile_k[...] = jnp.zeros_like(tile_k)
            tile_v[...] = jnp.zeros_like(tile_v)

            def tile(j, carry):
                t_cols = rows_at(j, t_tile)
                probs = jnp.exp2(dot(key_p[s_rows], query_t[:, t_cols]))
                probs_h, probs_l = split(probs)
                grads = probs * dot(value_p[s_rows], grad_t[:, t_cols])
                grads_h, grads_l = split(grads)
                grad_rows, query_rows = grad_n[t_cols], query_n[t_cols]
                tile_v[...] += dot(cat([probs_h, probs_l], 1), cat([grad_rows, grad_rows], 0))
                tile_k[...] += dot(cat([grads_h, grads_l], 1), cat([query_rows, query_rows], 0))
                keys = key_t[:, s_rows]
                query_grad[:, t_cols] += dot(cat([keys, keys], 1), cat([grads_h, grads_l], 0))
                return carry

            lax.fori_loop(0, t_count, tile, 0)
            lane = iota((s_tile, 2 * head), 1)
            k_part, v_part = tile_k[...], tile_v[...]
            target[s_rows] = jnp.where(
                lane < head,
                (k_part + pltpu.roll(k_part, head, 1)) * (1.0 / log2e),
                v_part + pltpu.roll(v_part, head, 1),
            )
            return carry

        lax.fori_loop(0, span // s_tile, key_rows, 0)

    moves = Sends(kv_send, kv_recv)
    sibling = grid.others("c")[0]
    step = 0
    crossing = []
    for i in range(1, grid.x):
        there = (x + i) % grid.x
        chunk(there, 1 - core, chunk_grad.at[2 * i])
        over = moves.start(chunk_grad.at[2 * i], chunk_in.at[i], sibling)
        if i == 1:
            for item in early:
                item.step(0)
        chunk(there, core, chunk_grad.at[2 * i + 1])
        over.wait_recv()
        chunk_grad[2 * i + 1] += chunk_in[i]
        crossing.append(moves.start(chunk_grad.at[2 * i + 1], cross_in.at[i - 1], grid.others("x")[i - 1]))
    for item in early:
        item.step(1)
    chunk(x, 1 - core, chunk_grad.at[0])
    over = moves.start(chunk_grad.at[0], chunk_in.at[0], sibling)
    for item in early:
        item.step(2)
    chunk(x, core, chunk_grad.at[1])
    over.wait_recv()
    for copy in crossing:
        copy.wait_recv()
    own = chunk_grad.at[1]
    own[...] += chunk_in[0]
    for i in range(1, grid.x):
        own[...] += cross_in[i - 1]

    whole = front_all[...].reshape(width, columns)
    high_w[...], low_w[...] = split(whole)
    front_rows = front_grad.reshape(width, columns)
    front_rows[...] = jnp.zeros_like(front_rows)
    gain, shift = vectors[0:1], vectors[1:2]

    def project_back(i, carry):
        rows = rows_at(i, block)
        unit, scale = normalise(tokens[rows])
        normed_s = split(unit * gain + shift)
        parts = []
        lane = iota((block, 2 * head), 1)
        logits = jnp.zeros((block, 2 * head), f32)
        for k in range(2):
            cols = rows_at(k * blocks + i, block)
            grad = (query_grad[:head, cols] + query_grad[head:, cols]) * (head**-0.5)
            grad = cat([grad, grad], 0).T
            parts.append(spread(grad, routes[rows, k : k + 1], experts))
            logits = logits + jnp.where(lane == routes[rows, k : k + 1], chosen_grad[rows, k : k + 1], 0.0)
        all_s = split(cat([parts[0] + parts[1], own[rows], logits], 1))
        front_rows[...] += dot_tn(normed_s, all_s)
        grad = dot_nt(all_s, (high_w[...], low_w[...]))
        extra[0:1] += jnp.sum(grad * unit, axis=0, keepdims=True)
        extra[1:2] += jnp.sum(grad, axis=0, keepdims=True)
        input_grad[rows] = middle_grad[rows] + norm_back(grad, unit, scale, gain)
        return carry

    extra[...] = jnp.zeros_like(extra)
    extra[0:8] = vector_grad[...]
    lax.fori_loop(0, blocks, project_back, 0)
    shard = width // grid.count
    piece = bias_grad.shape[1] // grid.count
    per_tile = 128 // piece
    lanes = iota((1, 128), 1)
    for q in range(bias_grad.shape[1] // 128):
        both = bias_grad[0:1, q * 128 : (q + 1) * 128]
        even[per_tile * q : per_tile * q + 1] = jnp.where(lanes < piece, 0.0, pltpu.roll(both, piece, 1))
        even[per_tile * q + 1 : per_tile * q + 2] = jnp.where(lanes < piece, 0.0, both)
    lane = iota((width, 128), 1)
    columns_of = cat([jnp.zeros((8, width), f32), extra[0:8], jnp.zeros((112, width), f32)], 0).T
    place = (iota((width, grid.count), 0) == iota((width, grid.count), 1) * shard).astype(bf16)
    bias_h, bias_l = split(even[...])
    bias_m = (even[...] - bias_h.astype(f32) - bias_l.astype(f32)).astype(bf16)
    spread_bias = dot(cat([place, place, place], 1), cat([bias_h, bias_l, bias_m], 0))
    front_rows[:, wide + 2 * head :] += columns_of + spread_bias
    for item in late:
        item.start()
    up_sum[...] = early[0].result()
    down_sum[...] = early[1].result()
    out_sum[...] = early[2].result()
    for number in range(3):
        for item in late:
            item.step(number)
    front_sum[:, :half] = late[0].result()
    front_sum[:, half:] = late[1].result()
    for item in items:
        item.finish()
    moves.finish()


def backward(
    grid, experts, head, lengths, tokens, middle_grad, routes, front_all, keyval, queries, logsum, heads_grad,
    chosen_grad, vectors, vector_grad, bias_grad, up_grad, down_grad, out_grad,
):
    span, width = tokens.shape
    ff = up_grad.shape[1]
    columns = front_all.shape[-1]
    shard, ff_shard = width // grid.count, ff // grid.count
    lead = grid.lead
    up_grad = up_grad.reshape(lead + (shard, ff))
    down_grad = down_grad.reshape(lead + (ff_shard, width))
    out_grad = out_grad.reshape(lead + (out_grad.shape[0] // grid.count, width))
    out_shapes = [(span, width), (shard, columns), (shard, ff), (ff_shard, width), out_grad.shape[4:]]
    tile = min(512, span)
    reduce_shapes = [
        ((shard, ff), "yx"),
        ((ff_shard, width), "xy"),
        (out_grad.shape[4:], "yx"),
        ((shard, columns // 2), "yx"),
        ((shard, columns // 2), "xy"),
    ]
    items = len(reduce_shapes)
    scratch = [
        pltpu.VMEM((4 * head, 2 * span), bf16),
        pltpu.VMEM((2 * span, 2 * head), bf16),
        pltpu.VMEM((4 * head, 2 * span), bf16),
        pltpu.VMEM((2 * span, 2 * head), bf16),
        pltpu.VMEM((span, 4 * head), bf16),
        pltpu.VMEM((span, 4 * head), bf16),
        pltpu.VMEM((2 * head, span), bf16),
        pltpu.VMEM((2 * head, 2 * span), f32),
        pltpu.VMEM((tile, 2 * head), f32),
        pltpu.VMEM((tile, 2 * head), f32),
        pltpu.VMEM((2 * grid.x, span, 2 * head), f32),
        pltpu.VMEM((grid.x, span, 2 * head), f32),
        pltpu.VMEM((grid.x - 1, span, 2 * head), f32),
        pltpu.VMEM(lead + (shard, columns), f32),
        pltpu.VMEM((width, columns), bf16),
        pltpu.VMEM((width, columns), bf16),
        pltpu.VMEM((8, width), f32),
        pltpu.VMEM((grid.count, 128), f32),
    ]
    for shape, order in reduce_shapes:
        scratch += reduce_scratch(grid, tuple(shape), order)
    scratch += [
        pltpu.SemaphoreType.DMA((items,)),
        pltpu.SemaphoreType.DMA((items, grid.copies() + 1)),
        pltpu.SemaphoreType.DMA((items, grid.copies() + 1)),
        pltpu.SemaphoreType.DMA((2 * grid.x - 1,)),
        pltpu.SemaphoreType.DMA((2 * grid.x - 1,)),
    ]
    return pl.pallas_call(
        functools.partial(backward_kernel, grid, head, experts),
        out_shape=[jax.ShapeDtypeStruct(shape, f32) for shape in out_shapes],
        in_specs=[pl.BlockSpec(memory_space=pltpu.SMEM)] + vmem_specs(12) + any_specs(3),
        out_specs=vmem_specs(5),
        scratch_shapes=scratch,
        compiler_params=pltpu.CompilerParams(
            collective_id=1, has_side_effects=True, vmem_limit_bytes=vmem_limit
        ),
        name="attention_back",
    )(
        lengths, tokens, middle_grad, routes, front_all, keyval, queries, logsum, heads_grad, chosen_grad,
        vectors, vector_grad, bias_grad, up_grad, down_grad, out_grad,
    )


def update_kernel(factor, head, *refs):
    front, up, down, out = refs[:4]
    weights, moments, averages = refs[4:12], refs[12:20], refs[20:28]
    new_weights, new_moments, new_averages = refs[28:36], refs[36:44], refs[44:52]
    wide = out.shape[1]
    tail = front[:, wide + 2 * head :]
    experts = weights[0].shape[1]
    vector_rows = weights[7].shape
    square = cat([tail, jnp.zeros((128 - tail.shape[0], 128), f32)], 0).T
    piece = weights[5].shape[1]
    gradients = [
        tail[:, :experts],
        front[:, :wide],
        out[...],
        front[:, wide : wide + 2 * head],
        up[...],
        pltpu.roll(tail[0:8], piece, 1)[0:1, :piece],
        down[...],
        square[8 : 8 + vector_rows[0], : vector_rows[1]],
    ]
    for i, gradient in enumerate(gradients):
        scaled = gradient * factor
        moment = moment_decay * moments[i][...] + scaled
        weight = weights[i][...] - step_rate * (scaled + moment_decay * moment)
        new_moments[i][...] = moment
        new_weights[i][...] = weight
        new_averages[i][...] = average_decay * averages[i][...] + (1.0 - average_decay) * weight


def update_all(factor, head, front, up, down, out, weights, moments, averages):
    flat = lambda arrays: [a.reshape(1, -1) if a.ndim == 1 else a for a in arrays]
    shapes = [a.shape for a in weights]
    weights, moments, averages = flat(weights), flat(moments), flat(averages)
    results = pl.pallas_call(
        functools.partial(update_kernel, factor, head),
        out_shape=[jax.ShapeDtypeStruct(a.shape, f32) for a in weights] * 3,
        in_specs=vmem_specs(28),
        out_specs=vmem_specs(24),
        compiler_params=pltpu.CompilerParams(vmem_limit_bytes=vmem_limit),
        name="update",
    )(front, up, down, out, *weights, *moments, *averages)
    return tuple(r.reshape(shapes[i % 8]) for i, r in enumerate(results))


def fused_step(grid, tokens, cotangent, lengths, routes, *params):
    weights, moments, averages = params[:8], params[8:16], params[16:24]
    router_weight, query_weight, out_weight, kv_weight, up_weight, up_bias, down_weight, vectors = weights
    shard, experts = router_weight.shape
    head = kv_weight.shape[1] // 2
    piece = up_bias.shape[0]
    middle_pad = jnp.zeros((shard, 128 - piece - experts - vectors.shape[0]), f32)
    bias_rows = jnp.concatenate([up_bias[None], jnp.zeros((shard - 1, piece), f32)], axis=0)
    packed = jnp.concatenate([query_weight, kv_weight, router_weight, vectors.T, middle_pad, bias_rows], axis=1)
    tokens_in, cotangent_in, routes_in = tokens[0], cotangent[0], routes[0]
    (
        front_all, full_vectors, full_bias, heads, queries, logsum, gates, keyval, out_all, up_all, down_all
    ) = forward(grid, experts, head, lengths, tokens_in, routes_in, packed, out_weight, up_weight, down_weight)
    full = lambda a: a.reshape(-1, a.shape[-1])
    (
        output, middle_grad, up_grad, down_grad, out_grad, vector_grad, bias_grad, heads_grad, chosen_grad
    ) = middle(
        experts, head, tokens_in, cotangent_in, heads, gates, routes_in, full_vectors, full_bias,
        full(out_all), full(up_all), full(down_all),
    )
    input_grad, front_sum, up_sum, down_sum, out_sum = backward(
        grid, experts, head, lengths, tokens_in, middle_grad, routes_in, front_all, keyval, queries, logsum,
        heads_grad, chosen_grad, full_vectors, vector_grad, bias_grad, up_grad, down_grad, out_grad,
    )
    factor = 1.0 / math.sqrt(tokens.shape[0] * tokens.shape[1] * grid.count)
    updated = update_all(factor, head, front_sum, up_sum, down_sum, out_sum, weights, moments, averages)
    return (output[None], input_grad[None]) + updated


def step_for(mesh):
    grid = Grid(mesh)

    def step(*args):
        shard, span = args[4].shape[0], args[0].shape[1]
        if shard % 8 == 0 and span % 256 == 0 and grid.x > 1 and args[9].shape[0] == 64:
            return fused_step(grid, *args)
        return general_step(*args)

    return step


def solution(mesh):
    in_specs = (
        P("dp", "seq", None),
        P("dp", "seq", None),
        P("dp", None),
        P("dp", "seq", None),
        P(("dp", "seq"), None),
        P(("dp", "seq"), None),
        P(("dp", "seq"), None),
        P(("dp", "seq"), None),
        P(("dp", "seq"), None),
        P(("dp", "seq")),
        P(("dp", "seq"), None),
        P(None, ("dp", "seq")),
        P(("dp", "seq"), None),
        P(("dp", "seq"), None),
        P(("dp", "seq"), None),
        P(("dp", "seq"), None),
        P(("dp", "seq"), None),
        P(("dp", "seq")),
        P(("dp", "seq"), None),
        P(None, ("dp", "seq")),
        P(("dp", "seq"), None),
        P(("dp", "seq"), None),
        P(("dp", "seq"), None),
        P(("dp", "seq"), None),
        P(("dp", "seq"), None),
        P(("dp", "seq")),
        P(("dp", "seq"), None),
        P(None, ("dp", "seq")),
    )
    out_specs = (
        P("dp", "seq", None),
        P("dp", "seq", None),
        P(("dp", "seq"), None),
        P(("dp", "seq"), None),
        P(("dp", "seq"), None),
        P(("dp", "seq"), None),
        P(("dp", "seq"), None),
        P(("dp", "seq")),
        P(("dp", "seq"), None),
        P(None, ("dp", "seq")),
        P(("dp", "seq"), None),
        P(("dp", "seq"), None),
        P(("dp", "seq"), None),
        P(("dp", "seq"), None),
        P(("dp", "seq"), None),
        P(("dp", "seq")),
        P(("dp", "seq"), None),
        P(None, ("dp", "seq")),
        P(("dp", "seq"), None),
        P(("dp", "seq"), None),
        P(("dp", "seq"), None),
        P(("dp", "seq"), None),
        P(("dp", "seq"), None),
        P(("dp", "seq")),
        P(("dp", "seq"), None),
        P(None, ("dp", "seq")),
    )
    return jax.shard_map(
        step_for(mesh), mesh=mesh, in_specs=in_specs, out_specs=out_specs, check_vma=False
    )
```

```python
import functools
import math
import types

import jax
import jax.numpy as jnp
from jax import lax
from jax.experimental import pallas as pl
from jax.experimental.pallas import tpu as pltpu
from jax.sharding import PartitionSpec as P

highest = lax.Precision.HIGHEST
norm_eps = 1e-05
step_rate = 0.02
moment_decay = 0.9
average_decay = 0.99


def matmul(left, right):
    return jnp.dot(left, right, precision=highest, preferred_element_type=jnp.float32)


def layer_norm(values, gain, shift):
    centre = values - jnp.mean(values, axis=-1, keepdims=True)
    spread = jnp.mean(centre * centre, axis=-1, keepdims=True)
    return centre * lax.rsqrt(spread + norm_eps) * gain + shift


def project_in(row_tokens, vectors, router_weight, query_weight, kv_weight, onehot):
    normed = layer_norm(row_tokens, vectors[0], vectors[1])
    logits = matmul(normed, router_weight)
    chosen = jnp.einsum("tke,te->tk", onehot, logits, precision=highest)
    gates = jax.nn.softmax(chosen, axis=-1)
    experts = onehot.shape[2]
    all_queries = matmul(normed, query_weight).reshape(normed.shape[0], experts, -1)
    queries = jnp.einsum("tke,ted->tkd", onehot, all_queries, precision=highest)
    keyval = matmul(normed, kv_weight)
    return (queries, keyval, gates)


def project_out(
    row_tokens, heads, gates, onehot, vectors, out_weight, up_weight, up_bias, down_weight
):
    mixed = jnp.einsum("tk,tke,tkd->ted", gates, onehot, heads, precision=highest)
    mixed = mixed.reshape(row_tokens.shape[0], -1)
    middle = row_tokens + matmul(mixed, out_weight)
    normed = layer_norm(middle, vectors[2], vectors[3])
    hidden = jax.nn.gelu(matmul(normed, up_weight) + up_bias)
    return middle + matmul(hidden, down_weight) + vectors[4]


def update(weight, gradient, moment, average, factor):
    scaled = gradient * factor
    moment_new = moment_decay * moment + scaled
    weight_new = weight - step_rate * (scaled + moment_decay * moment_new)
    average_new = average_decay * average + (1.0 - average_decay) * weight_new
    return (weight_new, moment_new, average_new)


def general_step(
    tokens,
    cotangent,
    lengths,
    routes,
    router_weight,
    query_weight,
    out_weight,
    kv_weight,
    up_weight,
    up_bias,
    down_weight,
    vectors,
    router_moment,
    query_moment,
    out_moment,
    kv_moment,
    up_moment,
    bias_moment,
    down_moment,
    vector_moment,
    router_average,
    query_average,
    out_average,
    kv_average,
    up_average,
    bias_average,
    down_average,
    vector_average,
):
    full_router, full_query, full_out, full_kv, full_up, full_bias, full_down, full_vectors = (
        lax.all_gather(router_weight, ("dp", "seq"), axis=0, tiled=True),
        lax.all_gather(query_weight, ("dp", "seq"), axis=0, tiled=True),
        lax.all_gather(out_weight, ("dp", "seq"), axis=0, tiled=True),
        lax.all_gather(kv_weight, ("dp", "seq"), axis=0, tiled=True),
        lax.all_gather(up_weight, ("dp", "seq"), axis=0, tiled=True),
        lax.all_gather(up_bias, ("dp", "seq"), axis=0, tiled=True),
        lax.all_gather(down_weight, ("dp", "seq"), axis=0, tiled=True),
        lax.all_gather(vectors, ("dp", "seq"), axis=1, tiled=True),
    )
    local_tokens = tokens[0]
    local_cotangent = cotangent[0]
    span = local_tokens.shape[0]
    row_length = span * lax.axis_size("seq")
    offset = lax.axis_index("seq") * span
    ends = jnp.cumsum(lengths[0])
    positions = jnp.arange(row_length, dtype=jnp.int32)
    segment_all = jnp.sum((positions[:, None] >= ends[None, :]).astype(jnp.int32), axis=1)
    segment_local = lax.dynamic_slice_in_dim(segment_all, offset, span)
    experts = full_router.shape[1]
    onehot = (routes[0][:, :, None] == jnp.arange(experts, dtype=jnp.int32)[None, None, :]).astype(
        jnp.float32
    )

    def front(tokens_in, vectors_in, router_in, query_in, kv_in):
        return project_in(tokens_in, vectors_in, router_in, query_in, kv_in, onehot)

    (queries, keyval, gates), front_pull = jax.vjp(
        front, local_tokens, full_vectors, full_router, full_query, full_kv
    )
    head_width = queries.shape[-1]
    choices_count = queries.shape[1]
    score_scale = head_width ** (-0.5)
    kv_piece = lax.all_gather(keyval, "seq", axis=0, tiled=True)
    best = jnp.full((span, choices_count), -1e30, jnp.float32)
    keys = kv_piece[:, :head_width]
    values = kv_piece[:, head_width:]
    key_segment = segment_all
    scores = jnp.einsum("tkd,sd->tks", queries, keys, precision=highest) * score_scale
    same_sent = segment_local[:, None, None] == key_segment[None, None, :]
    peak = jnp.maximum(best, jnp.max(jnp.where(same_sent, scores, -1e30), axis=-1))
    weights_soft = jnp.where(same_sent, jnp.exp(scores - peak[..., None]), 0.0)
    total = jnp.sum(weights_soft, axis=-1)
    accum = jnp.einsum("tks,sd->tkd", weights_soft, values, precision=highest)
    best, total, accum = (peak, total, accum)
    heads = accum / total[..., None]
    logsum = best + jnp.log(total)

    def tail(tokens_in, heads_in, gates_in, vectors_in, out_in, up_in, bias_in, down_in):
        return project_out(
            tokens_in, heads_in, gates_in, onehot, vectors_in, out_in, up_in, bias_in, down_in
        )

    output, tail_pull = jax.vjp(
        tail, local_tokens, heads, gates, full_vectors, full_out, full_up, full_bias, full_down
    )
    (
        tokens_grad_tail,
        heads_grad,
        gates_grad,
        vectors_grad_tail,
        out_grad,
        up_grad,
        bias_grad,
        down_grad,
    ) = tail_pull(local_cotangent)
    row_delta = jnp.sum(heads_grad * heads, axis=-1)
    kv_piece = lax.all_gather(keyval, "seq", axis=0, tiled=True)
    keys = kv_piece[:, :head_width]
    values = kv_piece[:, head_width:]
    key_segment = segment_all
    scores = jnp.einsum("tkd,sd->tks", queries, keys, precision=highest) * score_scale
    same_sent = segment_local[:, None, None] == key_segment[None, None, :]
    weights_soft = jnp.where(same_sent, jnp.exp(scores - logsum[..., None]), 0.0)
    weights_grad = jnp.einsum("tkd,sd->tks", heads_grad, values, precision=highest)
    scores_grad = weights_soft * (weights_grad - row_delta[..., None]) * score_scale
    query_grad = jnp.einsum("tks,sd->tkd", scores_grad, keys, precision=highest)
    keys_grad = jnp.einsum("tks,tkd->sd", scores_grad, queries, precision=highest)
    values_grad = jnp.einsum("tks,tkd->sd", weights_soft, heads_grad, precision=highest)
    joined = jnp.concatenate([keys_grad, values_grad], axis=1)
    keyval_grad = joined
    query_grad, keyval_partial = (query_grad, keyval_grad)
    keyval_grad = lax.psum_scatter(keyval_partial, "seq", scatter_dimension=0, tiled=True)
    tokens_grad_front, vectors_grad_front, router_grad, query_weight_grad, kv_grad = front_pull(
        (query_grad, keyval_grad, gates_grad)
    )
    input_grad = tokens_grad_tail + tokens_grad_front
    vectors_grad = vectors_grad_tail + vectors_grad_front
    shards = (
        router_weight,
        query_weight,
        out_weight,
        kv_weight,
        up_weight,
        up_bias,
        down_weight,
        vectors,
    )
    shard_dims = (0, 0, 0, 0, 0, 0, 0, 1)
    summed = lax.psum(
        (
            router_grad,
            query_weight_grad,
            out_grad,
            kv_grad,
            up_grad,
            bias_grad,
            down_grad,
            vectors_grad,
        ),
        ("dp", "seq"),
    )
    place = lax.axis_index(("dp", "seq"))
    reduced = tuple(
        (
            lax.dynamic_slice_in_dim(
                whole_grad, place * shard.shape[shard_dim], shard.shape[shard_dim], shard_dim
            )
            for whole_grad, shard, shard_dim in zip(summed, shards, shard_dims)
        )
    )
    all_tokens = span * lax.axis_size("seq") * tokens.shape[0] * lax.axis_size("dp")
    factor = 1.0 / math.sqrt(all_tokens)
    new_router, new_router_moment, new_router_average = update(
        router_weight, reduced[0], router_moment, router_average, factor
    )
    new_query, new_query_moment, new_query_average = update(
        query_weight, reduced[1], query_moment, query_average, factor
    )
    new_out, new_out_moment, new_out_average = update(
        out_weight, reduced[2], out_moment, out_average, factor
    )
    new_kv, new_kv_moment, new_kv_average = update(
        kv_weight, reduced[3], kv_moment, kv_average, factor
    )
    new_up, new_up_moment, new_up_average = update(
        up_weight, reduced[4], up_moment, up_average, factor
    )
    new_bias, new_bias_moment, new_bias_average = update(
        up_bias, reduced[5], bias_moment, bias_average, factor
    )
    new_down, new_down_moment, new_down_average = update(
        down_weight, reduced[6], down_moment, down_average, factor
    )
    new_vectors, new_vector_moment, new_vector_average = update(
        vectors, reduced[7], vector_moment, vector_average, factor
    )
    return (
        output[None],
        input_grad[None],
        new_router,
        new_query,
        new_out,
        new_kv,
        new_up,
        new_bias,
        new_down,
        new_vectors,
        new_router_moment,
        new_query_moment,
        new_out_moment,
        new_kv_moment,
        new_up_moment,
        new_bias_moment,
        new_down_moment,
        new_vector_moment,
        new_router_average,
        new_query_average,
        new_out_average,
        new_kv_average,
        new_up_average,
        new_bias_average,
        new_down_average,
        new_vector_average,
    )


f32 = jnp.float32
bf16 = jnp.bfloat16
MESH = pl.DeviceIdType.MESH
log2e = math.log2(math.e)
far = 2.0**100
vmem_limit = 62 * 2**20
NN = (((1,), (0,)), ((), ()))
NT = (((1,), (1,)), ((), ()))
TN = (((0,), (0,)), ((), ()))


def dot(left, right, dims=NN):
    return lax.dot_general(left, right, dims, preferred_element_type=f32)


def split(values):
    high = values.astype(bf16)
    return high, (values - high.astype(f32)).astype(bf16)


def split_wide(values):
    high = values.astype(bf16).astype(f32)
    return high, values - high


def cat(parts, axis):
    return jnp.concatenate(parts, axis=axis)


def dot_nn(left, right):
    return dot(cat([left[0], left[1], left[0]], 1), cat([right[0], right[0], right[1]], 0))


def dot_nt(left, right):
    return dot(cat([left[0], left[1], left[0]], 1), cat([right[0], right[0], right[1]], 1), NT)


def dot_tn(left, right):
    return dot(cat([left[0], left[1], left[0]], 0), cat([right[0], right[0], right[1]], 0), TN)


def iota(shape, dim):
    return lax.broadcasted_iota(jnp.int32, shape, dim)


def rows_at(index, count):
    return pl.ds(pl.multiple_of(index * count, count), count)


class Grid:
    def __init__(self, mesh):
        dp, seq = mesh.shape["dp"], mesh.shape["seq"]
        self.x = max(seq // 2, 1)
        self.y = self.x if dp % self.x == 0 else 1
        self.z = dp // self.y
        self.count = dp * seq
        self.lead = (self.z, self.y, self.x, 2)

    def here(self):
        dp, seq = lax.axis_index("dp"), lax.axis_index("seq")
        return dp // self.y, dp % self.y, seq // 2, seq % 2

    def device(self, z, y, x, core):
        return (z * self.y + y, x * 2 + core)

    def others(self, axis):
        z, y, x, core = self.here()
        if axis == "z":
            return [self.device((z + i) % self.z, y, x, core) for i in range(1, self.z)]
        if axis == "y":
            return [self.device(z, (y + i) % self.y, x, core) for i in range(1, self.y)]
        if axis == "x":
            return [self.device(z, y, (x + i) % self.x, core) for i in range(1, self.x)]
        return [self.device(z, y, x, 1 - core)]

    def copies(self):
        return self.z + self.y + self.x - 2

    def barrier(self):
        barrier = pltpu.get_barrier_semaphore()
        count = 0
        for axis in "zyxc":
            for device in self.others(axis):
                pl.semaphore_signal(barrier, inc=1, device_id=device, device_id_type=MESH)
                count += 1
        pl.semaphore_wait(barrier, count)


class Sends:
    def __init__(self, send, recv):
        self.send, self.recv, self.used, self.started = send, recv, 0, []

    def start(self, source, target, device):
        copy = pltpu.make_async_remote_copy(
            src_ref=source,
            dst_ref=target,
            send_sem=self.send.at[self.used],
            recv_sem=self.recv.at[self.used],
            device_id=device,
            device_id_type=MESH,
        )
        self.used += 1
        copy.start()
        self.started.append(copy)
        return copy

    def finish(self):
        for copy in self.started:
            copy.wait_send()


def vmem_specs(count):
    return [pl.BlockSpec(memory_space=pltpu.VMEM)] * count


def any_specs(count):
    return [pl.BlockSpec(memory_space=pl.ANY)] * count


def sentence_bounds(lengths, marks, first):
    start = jnp.zeros(marks.shape, jnp.int32)
    end = jnp.zeros(marks.shape, jnp.int32)
    at = jnp.int32(0)
    for e in range(lengths.shape[1]):
        after = at + lengths[0, e]
        start = jnp.where(marks == first + e, at, start)
        end = jnp.where(marks == first + e, after, end)
        at = after
    return start, end


def in_sentence(positions, start, end):
    return jnp.logical_and(positions >= start, positions < end).astype(f32)


def query_pack(transposed, extra):
    high, low = split(transposed[: transposed.shape[0] // 2])
    return cat([high, low, high, extra.astype(bf16)], 0)


def key_pack(doubled, extra):
    lanes = iota(doubled.shape, 1)
    half = doubled.shape[1] // 2
    high, low = split_wide(doubled)
    return cat([high.astype(bf16), jnp.where(lanes < half, low, extra).astype(bf16)], 1)


def half_split(doubled, axis):
    half = doubled.shape[axis] // 2
    high, low = split_wide(doubled)
    return jnp.where(iota(doubled.shape, axis) < half, high, low).astype(bf16)


def twice(pair):
    half = pair.shape[1] // 2
    turned = pltpu.roll(pair, half, 1)
    lanes = iota(pair.shape, 1)
    return jnp.where(lanes < half, pair, turned), jnp.where(lanes < half, turned, pair)


def pick(wide, route, head):
    lanes = iota((wide.shape[0], 2 * head), 1) // head
    total = None
    for group in range(wide.shape[1] // (2 * head)):
        part = jnp.where(lanes + 2 * group == route, wide[:, group * 2 * head : (group + 1) * 2 * head], 0.0)
        total = part if total is None else total + part
    return total + pltpu.roll(total, head, 1)


def spread(doubled, route, experts):
    head = doubled.shape[1] // 2
    lanes = iota(doubled.shape, 1) // head
    return cat([jnp.where(lanes + 2 * group == route, doubled, 0.0) for group in range(experts // 2)], 1)


def normalise(values):
    centre = values - jnp.mean(values, axis=-1, keepdims=True)
    scale = lax.rsqrt(jnp.mean(centre * centre, axis=-1, keepdims=True) + norm_eps)
    return centre * scale, scale


def norm_back(grad, unit, scale, gain):
    inner = grad * gain
    mean = jnp.mean(inner, axis=-1, keepdims=True)
    along = jnp.mean(inner * unit, axis=-1, keepdims=True)
    return scale * (inner - mean - unit * along)


class Gather:
    def __init__(self, grid, source, target, axes, order, sems):
        self.grid, self.source, self.target, self.axes, self.order = grid, source, target, axes, order
        self.sends, self.local = Sends(*sems[:2]), sems[2]
        self.current, self.own = [], None

    def view(self, **fixed):
        fixed["c"] = self.grid.here()[3]
        return self.target.at[tuple(fixed.get(axis, slice(None)) for axis in self.axes + "c")]

    def start(self):
        z, y, x, core = self.grid.here()
        mine = self.view(z=z, y=y, x=x)
        self.own = pltpu.make_async_copy(self.source, mine, self.local)
        self.own.start()
        self.current = [self.sends.start(self.source, mine, device) for device in self.grid.others("z")]

    def wait(self):
        for copy in self.current:
            copy.wait_recv()
        self.current = []
        if self.own is not None:
            self.own.wait()
            self.own = None

    def step(self, number):
        z, y, x, core = self.grid.here()
        self.wait()
        if number == 0:
            view = self.view(y=y, x=x)
        elif number == 1:
            view = self.view(x=x) if self.order[0] == "y" else self.view(y=y)
        else:
            view = self.view()
        axis = (self.order + "c")[number]
        self.current = [self.sends.start(view, view, device) for device in self.grid.others(axis)]

    def finish(self):
        self.wait()
        self.sends.finish()


class Reduce:
    def __init__(self, grid, source, axes, order, parts, sems):
        self.grid, self.source, self.axes, self.order, self.parts = grid, source, axes, order, parts
        self.sends, self.current, self.done = Sends(*sems[:2]), [], {}

    def view(self, core, **fixed):
        fixed["c"] = core
        return self.source.at[tuple(fixed.get(axis, slice(None)) for axis in self.axes + "c")]

    def start(self):
        core = self.grid.here()[3]
        self.send("c", [self.view(1 - core)], 0)

    def send(self, axis, views, part):
        devices = self.grid.others(axis)
        self.current = [
            self.sends.start(view, self.parts[part].at[i], device)
            for i, (view, device) in enumerate(zip(views, devices))
        ]
        self.part = part

    def take(self):
        core = self.grid.here()[3]
        view = self.view(core, **self.done)
        for copy in self.current:
            copy.wait_recv()
        for i in range(len(self.current)):
            view[...] += self.parts[self.part][i]
        self.current = []

    def step(self, number):
        z, y, x, core = self.grid.here()
        self.take()
        axis = (self.order + "z")[number]
        if axis not in self.axes:
            return
        size, at = {"z": (self.grid.z, z), "y": (self.grid.y, y), "x": (self.grid.x, x)}[axis]
        views = [
            self.view(core, **{**self.done, axis: (at + i) % size}) for i in range(1, size)
        ]
        self.send(axis, views, number + 1)
        self.done = {**self.done, axis: at}

    def result(self):
        self.take()
        return self.view(self.grid.here()[3], **self.done)[...]

    def finish(self):
        self.sends.finish()


def reduce_scratch(grid, shape, axes, order):
    size = {"z": grid.z, "y": grid.y, "x": grid.x}
    dims = lambda names: tuple(size[axis] for axis in axes if axis in names)
    parts = [
        pltpu.VMEM((1,) + dims(axes) + shape, f32),
        pltpu.VMEM((size[order[0]] - 1,) + dims(axes.replace(order[0], "")) + shape, f32),
        pltpu.VMEM((size[order[1]] - 1,) + dims(axes.replace("x", "").replace("y", "")) + shape, f32),
    ]
    if "z" in axes:
        parts.append(pltpu.VMEM((grid.z - 1,) + shape, f32))
    return parts


def copy_sems(count):
    return [pltpu.SemaphoreType.DMA((count,)), pltpu.SemaphoreType.DMA((count,)), pltpu.SemaphoreType.DMA]


gather_orders = (
    ("keys", "yx"), ("query0", "yx"), ("query1", "yx"), ("out", "xy"), ("up0", "yx"), ("up1", "xy"), ("up2", "yx"),
    ("up3", "yx"), ("down", "yx"), ("down0", "yx"), ("down1", "yx"), ("down2", "xy"), ("down3", "xy"),
)
reduce_orders = (
    ("up0", "xy"), ("up1", "yx"), ("up2", "yx"), ("up3", "yx"), ("down0", "xy"), ("down1", "yx"), ("down2", "xy"),
    ("down3", "xy"), ("out", "xy"), ("keys", "xy"), ("query0", "yx"), ("query1", "xy"),
)
moves_at = {
    "queries": "+out0",
    "split": "+up00",
    "own_mid": "+out1 +up01",
    "near_mid": "hand +down +down00 +up10",
    "near_end": "+down20",
    "far_mid": "+out2 +up02 +down01 +down10",
    "far_end": "+up11",
    "last_mid": "+up20 +down21",
    "last_end": "+down11",
    "finish": "+down02 +up30",
    "mix": "+down30",
    "part00": "+up12 +down12 +up21 +down31",
    "part01": "+down22 +up31",
    "part10": "+up22 +down32",
    "part11": "+up32 -up00 -down00",
    "part21": "-up10 -down10",
    "part30": "-up01 -down01 -up20 -down20",
    "heads_mid": "-down21",
    "heads_end": "-up30 -down30",
    "back0_mid": "-up02 -down02 -up11 -down11 -out0",
    "back0_end": "-up21 -down22 -down31",
    "back1_mid": "-up31 -down32",
    "back1_end": "-up12 -down12 -up22 shards",
    "back2_mid": "-up32 -out1",
    "back3_mid": "-out2",
}


class Plan:
    def __init__(self, grid, span, width, ff, head, experts, columns):
        self.grid, self.span, self.width, self.ff = grid, span, width, ff
        self.head, self.experts, self.columns = head, experts, columns
        self.shard, self.ff_shard = width // grid.count, ff // grid.count
        self.chunks = grid.z
        self.part = ff // self.chunks
        self.pieces = {"keys": (experts * head, columns), "query0": (0, experts * head // 2)}
        self.pieces["query1"] = (experts * head // 2, experts * head)
        part, chunks = self.part, self.chunks
        shard = (self.shard, part)
        ff_shard = (self.ff_shard, width)
        self.gathers = [(name, "yx" if name[:-1] == "down" else "zyx", order) for name, order in gather_orders]
        shapes = {"out": (self.shard, width)}
        for name, (lo, hi) in self.pieces.items():
            shapes[name] = (self.shard, hi - lo)
        self.reduces = []
        for name, order in reduce_orders:
            shape = shapes.get(name, ff_shard if name.startswith("down") else shard)
            self.reduces.append((name, shape, "yx" if name.startswith("down") else "zyx", order))

    def scratch(self):
        grid, span, width, head = self.grid, self.span, self.width, self.head
        lead = grid.lead
        part = self.part
        b, f = lambda *shape: pltpu.VMEM(shape, bf16), lambda *shape: pltpu.VMEM(shape, f32)
        named = dict(
            tokens_v=f(span, width), cot_v=f(span, width), norm_grad=f(span, width),
            cot_h=b(span, width), cot_l=b(span, width), norm_h=b(span, width), norm_l=b(span, width),
            mixed_h=b(span, width), mixed_l=b(span, width), scale2=f(span, 128),
            routes=pltpu.VMEM((span, 128), jnp.int32), gates=f(span, 2 * head), heads=f(2 * span, 2 * head),
            packed=f(self.shard, self.columns), square=f(128, 128),
            front=pltpu.VMEM(lead + (self.shard, self.columns), f32),
            front_h=b(width, self.columns), front_l=b(width, self.columns),
            vectors=f(8, width), vector_grad=f(8, width), bias=f(1, self.ff), bias_grad=f(1, self.ff),
            even=f(grid.count, 128), odd=f(grid.count, 128),
            query_t=b(4 * head, 2 * span), query_n=b(2 * span, 2 * head),
            grad_t=b(4 * head, 2 * span), grad_n=b(2 * span, 2 * head),
            keyval=f(grid.x, 2, span, 2 * head),
            key_p=b(span, 4 * head), value_p=b(span, 4 * head), turned=b(2 * head, span),
            accum=f(2 * head, 2 * span), peak=f(1, 2 * span), total=f(1, 2 * span), logsum=f(1, 2 * span),
            tile_k=f(min(512, span), 2 * head), tile_v=f(min(512, span), 2 * head),
            chunk_grad=f(2 * grid.x, span, 2 * head), chunk_in=f(grid.x, span, 2 * head),
            cross_in=f(max(grid.x - 1, 1), span, 2 * head),
            out=pltpu.VMEM(lead + (self.shard, width), f32), out_h=b(width, width), out_l=b(width, width),
            up=pltpu.VMEM(lead + (self.shard, self.ff), f32), down=pltpu.VMEM(lead + (self.ff_shard, width), f32),
            up_h=b(width, part), up_l=b(width, part), down_h=b(part, width), down_l=b(part, width),
            down_z=f(grid.z - 1, self.ff_shard, width),
            kv_sems=copy_sems(2 * grid.x - 1), chunk_sems=copy_sems(2 * grid.x - 1), down_sems=copy_sems(grid.z - 1),
            io_sems=pltpu.SemaphoreType.DMA((5,)),
        )
        copies = grid.z + grid.y + grid.x
        named["gather_sems"] = [copy_sems(copies) for _ in self.gathers]
        named["reduce_sems"] = [copy_sems(copies) for _ in self.reduces]
        named["reduce_parts"] = [
            reduce_scratch(grid, shape, axes, order) for _, shape, axes, order in self.reduces
        ]
        return named


def attention_sides(plan, lengths, at, count, offset):
    marks = iota((1, 2 * plan.head), 1) - plan.head
    start, end = sentence_bounds(lengths, marks, 0)
    positions = at + offset + iota((count, 1), 0)
    outside = (in_sentence(positions, start, end) - 1.0) * far
    return marks, jnp.where(jnp.logical_and(marks >= 0, marks < lengths.shape[1]), outside, 0.0)


def three(values):
    one = values.astype(bf16).astype(f32)
    two = (values - one).astype(bf16).astype(f32)
    return one, two, values - one - two


def step_kernel(plan, tree, lengths, query_w, kv_w, router_t, vectors_w, bias_w, routes_t,
                tokens, cotangent, out_w, up_w, down_w,
                output, input_grad, front_sum, up_sum, down_sum, out_sum, *scratch):
    s = types.SimpleNamespace(**jax.tree.unflatten(tree, scratch))
    grid, span, width, head, experts = plan.grid, plan.span, plan.width, plan.head, plan.experts
    ff, part, chunks, columns = plan.ff, plan.part, plan.chunks, plan.columns
    wide = experts * head
    z, y, x, core = grid.here()
    seq_at = (x * 2 + core) * span
    block = min(256, span)
    blocks = span // block

    load_tokens = pltpu.make_async_copy(tokens, s.tokens_v, s.io_sems.at[0])
    load_tokens.start()
    load_cot = pltpu.make_async_copy(cotangent, s.cot_v, s.io_sems.at[1])
    load_cot.start()

    s.square[...] = jnp.zeros_like(s.square)
    s.square[0:experts, 0 : plan.shard] = router_t[...]
    s.square[experts : experts + vectors_w.shape[0], 0 : plan.shard] = vectors_w[...]
    s.packed[:, :wide] = query_w[...]
    s.packed[:, wide : wide + 2 * head] = kv_w[...]
    s.packed[:, wide + 2 * head :] = s.square[...].T[: plan.shard]
    piece = ff // grid.count
    s.packed[0:1, columns - piece :] = bias_w[...]

    sources = {"out": (out_w, s.out), "down": (down_w, s.down)}
    for name, (lo, hi) in plan.pieces.items():
        sources[name] = (s.packed.at[:, lo:hi], s.front.at[:, :, :, :, :, lo:hi])
    for j in range(chunks):
        cols = slice(j * part, (j + 1) * part)
        sources["up%d" % j] = (up_w.at[:, cols], s.up.at[:, :, :, :, :, cols])
        sources["down%d" % j] = (None, s.down.at[j])
    g = {
        name: Gather(grid, *sources[name], axes, order, sems)
        for (name, axes, order), sems in zip(plan.gathers, s.gather_sems)
    }
    targets = {name: target for name, (_, target) in sources.items()}
    r = {
        name: Reduce(grid, targets[name], axes, order, parts, sems)
        for (name, _, axes, order), parts, sems in zip(plan.reduces, s.reduce_parts, s.reduce_sems)
    }

    grid.barrier()
    g["keys"].start()

    def routes_block(i, carry):
        cols = rows_at(i, block)
        pair = routes_t[:, cols].astype(f32)
        tall = cat([pair, jnp.zeros((126, block), f32)], 0)
        s.routes[cols] = tall.T.astype(jnp.int32)
        return carry

    def unit_block(i, carry):
        rows = rows_at(i, block)
        s.norm_grad[rows] = normalise(s.tokens_v[rows])[0]
        return carry

    def cot_block(i, carry):
        rows = rows_at(i, block)
        s.cot_h[rows], s.cot_l[rows] = split(s.cot_v[rows])
        return carry

    keys, queries = g["keys"], [g["query0"], g["query1"]]
    lax.fori_loop(0, blocks, routes_block, 0)
    keys.step(0)
    for item in queries:
        item.start()
    load_tokens.wait()
    lax.fori_loop(0, blocks, unit_block, 0)
    keys.step(1)
    for item in queries:
        item.step(0)
    for name in ("out", "up0", "down"):
        g[name].start()
    load_cot.wait()
    lax.fori_loop(0, blocks, cot_block, 0)
    keys.step(2)
    for item in queries:
        item.step(1)
    keys.wait()

    def front_part(name):
        lo, hi = plan.pieces[name]
        part_w = s.front[:, :, :, :, :, lo:hi].reshape(width, hi - lo)
        s.front_h[:, lo:hi], s.front_l[:, lo:hi] = split(part_w)
        return part_w

    tail = front_part("keys")[:, 2 * head :]
    s.vectors[...] = tail.T[experts : experts + 8]
    gain, shift = s.vectors[0:1], s.vectors[1:2]

    def project_keys(i, carry):
        rows = rows_at(i, block)
        normed_s = split(s.norm_grad[rows] * gain + shift)
        s.norm_h[rows], s.norm_l[rows] = normed_s
        result = dot_nn(normed_s, (s.front_h[:, wide:], s.front_l[:, wide:]))
        s.keyval[x, core, rows] = result[:, : 2 * head]
        lane = iota((block, 2 * head), 1)
        route = s.routes[rows]
        logits = result[:, 2 * head :]
        chosen = [
            jnp.sum(jnp.where(lane == route[:, k : k + 1], logits, 0.0), axis=1, keepdims=True) for k in range(2)
        ]
        top = jnp.maximum(chosen[0], chosen[1])
        raw = [jnp.exp(c - top) for c in chosen]
        norm = raw[0] + raw[1]
        s.gates[rows] = jnp.where(lane < head, raw[0] / norm, raw[1] / norm)
        return carry

    lax.fori_loop(0, blocks, project_keys, 0)
    moves = Sends(*s.kv_sems[:2])
    mine = s.keyval.at[x, core]
    sibling = grid.others("c")[0]
    to_sibling = moves.start(mine, mine, sibling)
    across = [moves.start(mine, mine, device) for device in grid.others("x")]
    for item in queries:
        item.step(2)
    for j in range(1, chunks):
        g["up%d" % j].start()
    forwards = {}

    def hand_on(i):
        across[i - 1].wait_recv()
        view = s.keyval.at[(x - i + grid.x) % grid.x, core]
        forwards[i] = moves.start(view, view, sibling)

    down_moves = Sends(*s.down_sems[:2])
    down_last = []

    def tick(name):
        for move in moves_at.get(name, "").split():
            if move == "hand":
                hand_on(1)
            elif move == "+down":
                g["down"].wait()
            elif move == "shards":
                for i, device in enumerate(grid.others("z")):
                    source = s.down.at[(z + i + 1) % grid.z, y, x, core]
                    down_last.append(down_moves.start(source, s.down_z.at[i], device))
            else:
                (g if move[0] == "+" else r)[move[1:-1]].step(int(move[-1]))

    tick("queries")
    for item in queries:
        item.wait()
    front_part("query0")
    front_part("query1")
    lanes = iota((1, 128), 1)
    for p in range(grid.count):
        s.odd[p : p + 1] = tail[p * plan.shard : p * plan.shard + 1]
    s.even[...] = pltpu.roll(s.odd[...], piece, 1)
    per_tile = 128 // piece
    for q in range(ff // 128):
        s.bias[0:1, q * 128 : (q + 1) * 128] = jnp.where(
            lanes < piece, s.even[per_tile * q : per_tile * q + 1], s.odd[per_tile * q + 1 : per_tile * q + 2]
        )

    def project_queries(i, carry):
        rows = rows_at(i, block)
        result = dot_nn((s.norm_h[rows], s.norm_l[rows]), (s.front_h[:, :wide], s.front_l[:, :wide]))
        marks = iota((head, 1), 0)
        start, end = sentence_bounds(lengths, marks, 0)
        positions = seq_at + i * block + iota((1, block), 1)
        inside = in_sentence(positions, start, end)
        for k in range(2):
            query = pick(result, s.routes[rows, k : k + 1], head) * (log2e * head**-0.5)
            at = rows_at(k * blocks + i, block)
            s.query_n[at] = half_split(query, 1)
            s.query_t[:, at] = query_pack(query.T, inside)
        return carry

    tick("split")
    lax.fori_loop(0, blocks, project_queries, 0)
    for item in [keys] + queries:
        item.finish()

    s.accum[...] = jnp.zeros_like(s.accum)
    s.peak[...] = jnp.full_like(s.peak, -3e38)
    s.total[...] = jnp.zeros_like(s.total)
    t_tile = width
    t_count = 2 * span // t_tile

    def attend(chunk_x, chunk_core, name):
        at = (chunk_x * 2 + chunk_core) * span

        def prepare(i, carry):
            rows = rows_at(i, block)
            keys, values = twice(s.keyval[chunk_x, chunk_core, rows])
            _, outside = attention_sides(plan, lengths, at, block, i * block)
            s.key_p[rows] = key_pack(keys, outside)
            s.turned[:, rows] = half_split(values.T, 0)
            return carry

        lax.fori_loop(0, blocks, prepare, 0)

        def tile(i, carry):
            cols = rows_at(i, t_tile)
            s.norm_grad[...] = dot(s.key_p[...], s.query_t[:, cols])
            old = s.peak[0:1, cols]
            new = jnp.maximum(old, jnp.max(s.norm_grad[...], axis=0, keepdims=True))
            fade = jnp.exp2(old - new)
            probs = jnp.exp2(s.norm_grad[...] - new)
            high, low = split(probs)
            weights = s.turned[...]
            add = dot(cat([weights, weights], 1), cat([high, low], 0))
            s.total[0:1, cols] = s.total[0:1, cols] * fade + jnp.sum(probs, axis=0, keepdims=True)
            s.accum[:, cols] = s.accum[:, cols] * fade + add
            s.peak[0:1, cols] = new
            return carry

        lax.fori_loop(0, t_count // 2, tile, 0)
        tick(name + "_mid")
        lax.fori_loop(t_count // 2, t_count, tile, 0)
        tick(name + "_end")

    attend(x, core, "own")
    to_sibling.wait_recv()
    attend(x, 1 - core, "near")
    for i in range(1, grid.x):
        if i not in forwards:
            hand_on(i)
        attend((x - i + grid.x) % grid.x, core, "far" if i == 1 else "")
        forwards[i].wait_recv()
        attend((x - i + grid.x) % grid.x, 1 - core, "last" if i == 1 else "")

    def finish(i, carry):
        cols = rows_at(i, block)
        norm = s.total[0:1, cols]
        result = (s.accum[:head, cols] + s.accum[head:, cols]) / norm
        s.heads[cols] = cat([result, result], 0).T
        marks = iota((16, 1), 0)
        start, end = sentence_bounds(lengths, marks, 0)
        positions = seq_at + (i % blocks) * block + iota((1, block), 1)
        side = in_sentence(positions, start, end)
        for k, term in enumerate(three(-(s.peak[0:1, cols] + jnp.log2(norm)))):
            side = jnp.where(marks == 8 + k, term, side)
        s.query_t[3 * head : 3 * head + 16, cols] = side.astype(bf16)
        return carry

    lax.fori_loop(0, 2 * blocks, finish, 0)
    tick("finish")
    g["out"].finish()
    s.out_h[...], s.out_l[...] = split(s.out[...].reshape(width, width))
    gain2, shift2, last = s.vectors[2:3], s.vectors[3:4], s.vectors[4:5]

    def gate_pair(rows):
        gate = s.gates[rows]
        turned = pltpu.roll(gate, head, 1)
        lane = iota(gate.shape, 1)
        return [jnp.where(lane < head, gate, turned), jnp.where(lane < head, turned, gate)]

    def mix(i, carry):
        rows = rows_at(i, block)
        gate = gate_pair(rows)
        mixed = None
        for k in range(2):
            own = gate[k] * s.heads[rows_at(k * blocks + i, block)]
            wide_part = spread(own, s.routes[rows, k : k + 1], experts)
            mixed = wide_part if mixed is None else mixed + wide_part
        mixed_s = split(mixed)
        s.mixed_h[rows], s.mixed_l[rows] = mixed_s
        middle = s.tokens_v[rows] + dot_nn(mixed_s, (s.out_h[...], s.out_l[...]))
        unit, scale = normalise(middle)
        s.cot_v[rows] = unit
        s.scale2[rows] = jnp.broadcast_to(scale, (block, 128))
        s.norm_h[rows], s.norm_l[rows] = split(unit * gain2 + shift2)
        s.tokens_v[rows] = middle + last
        s.norm_grad[rows] = jnp.zeros((block, width), f32)
        return carry

    lax.fori_loop(0, blocks, mix, 0)
    tick("mix")

    up_rows, down_rows = s.up.reshape(width, ff), s.down.reshape(ff, width)
    row_block = min(512, span)

    def hidden_part(j, i):
        rows = slice(i * row_block, (i + 1) * row_block)
        cols = slice(j * part, (j + 1) * part)
        cot_s = (s.cot_h[rows], s.cot_l[rows])
        norm_s = (s.norm_h[rows], s.norm_l[rows])
        up_s = (s.up_h[...], s.up_l[...])
        down_s = (s.down_h[...], s.down_l[...])
        pre = dot_nn(norm_s, up_s) + s.bias[0:1, cols]
        back = dot_nt(cot_s, down_s)
        square = pre * pre
        wave = jnp.tanh(math.sqrt(2.0 / math.pi) * (pre + 0.044715 * (square * pre)))
        half_wave = 0.5 * (1.0 + wave)
        hidden_s = split(pre * half_wave)
        slope = half_wave + (0.5 * math.sqrt(2.0 / math.pi)) * pre * (1.0 - wave * wave) * (
            1.0 + (3.0 * 0.044715) * square
        )
        pre_grad = back * slope
        pre_s = split(pre_grad)
        s.tokens_v[rows] += dot_nn(hidden_s, down_s)
        s.norm_grad[rows] += dot_nt(pre_s, up_s)
        down_part = dot_tn(hidden_s, cot_s)
        up_part = dot_tn(norm_s, pre_s)
        bias_part = jnp.sum(pre_grad, axis=0, keepdims=True)
        if i == 0:
            down_rows[cols] = down_part
            up_rows[:, cols] = up_part
            s.bias_grad[0:1, cols] = bias_part
        else:
            down_rows[cols] += down_part
            up_rows[:, cols] += up_part
            s.bias_grad[0:1, cols] += bias_part

    for j in range(chunks):
        cols = slice(j * part, (j + 1) * part)
        if j == 0:
            g["down"].finish()
        g["up%d" % j].finish()
        g["down%d" % j].finish()
        s.up_h[...], s.up_l[...] = split(up_rows[:, cols])
        s.down_h[...], s.down_l[...] = split(down_rows[cols])
        for i in range(span // row_block):
            hidden_part(j, i)
            if i + 1 == span // row_block:
                r["up%d" % j].start()
                r["down%d" % j].start()
            tick("part%d%d" % (j, i))

    store_output = pltpu.make_async_copy(s.tokens_v, output, s.io_sems.at[2])
    store_output.start()
    s.vector_grad[...] = jnp.zeros_like(s.vector_grad)
    out_rows = s.out.reshape(width, width)

    def heads_block(i, carry):
        rows = rows_at(i, block)
        grad = s.norm_grad[rows]
        unit = s.cot_v[rows]
        cot = s.cot_h[rows].astype(f32) + s.cot_l[rows].astype(f32)
        s.vector_grad[2:3] += jnp.sum(grad * unit, axis=0, keepdims=True)
        s.vector_grad[3:4] += jnp.sum(grad, axis=0, keepdims=True)
        s.vector_grad[4:5] += jnp.sum(cot, axis=0, keepdims=True)
        mid = cot + norm_back(grad, unit, s.scale2[rows, 0:1], gain2)
        s.norm_grad[rows] = mid
        mid_s = split(mid)
        s.norm_h[rows], s.norm_l[rows] = mid_s
        grad_mixed = dot_nt(mid_s, (s.out_h[...], s.out_l[...]))
        gate = gate_pair(rows)
        lane = iota((block, 2 * head), 1)
        marks = iota((head, 1), 0)
        gates_grad = []
        for k in range(2):
            at = rows_at(k * blocks + i, block)
            picked = pick(grad_mixed, s.routes[rows, k : k + 1], head)
            gate_grad = jnp.sum(jnp.where(lane < head, picked * s.heads[at], 0.0), axis=1, keepdims=True)
            gates_grad.append(gate_grad)
            own = gate[k] * picked
            s.grad_n[at] = half_split(own, 1)
            turned = jnp.where(lane < head, own, gate_grad * gate[k]).T
            side = jnp.zeros((head, block), f32)
            for n, term in enumerate(three(-turned[head : head + 1])):
                side = jnp.where(marks == n, term, side)
            s.grad_t[:, at] = query_pack(turned, side)
        both = gate[0] * gates_grad[0] + gate[1] * gates_grad[1]
        s.gates[rows] = jnp.where(
            lane == 0, gate[0] * (gates_grad[0] - both), gate[1] * (gates_grad[1] - both)
        )
        return carry

    lax.fori_loop(0, blocks // 2, heads_block, 0)
    tick("heads_mid")
    lax.fori_loop(blocks // 2, blocks, heads_block, 0)
    out_rows[...] = dot_tn((s.mixed_h[...], s.mixed_l[...]), (s.norm_h[...], s.norm_l[...]))
    r["out"].start()
    tick("heads_end")
    store_output.wait()
    load_tokens = pltpu.make_async_copy(tokens, s.tokens_v, s.io_sems.at[3])
    load_tokens.start()

    s.accum[...] = jnp.zeros_like(s.accum)
    s_tile = min(512, span)

    def chunk(chunk_x, chunk_core, target, name):
        at = (chunk_x * 2 + chunk_core) * span

        def prepare(i, carry):
            rows = rows_at(i, block)
            keys, values = twice(s.keyval[chunk_x, chunk_core, rows])
            marks, outside = attention_sides(plan, lengths, at, block, i * block)
            ones = jnp.logical_and(marks >= 8, marks < 11)
            s.key_p[rows] = key_pack(keys, jnp.where(ones, 1.0, outside))
            few = jnp.logical_and(marks >= 0, marks < 3).astype(f32)
            s.value_p[rows] = key_pack(values, jnp.broadcast_to(few, values.shape))
            s.turned[:, rows] = half_split(keys.T, 0)
            return carry

        lax.fori_loop(0, blocks, prepare, 0)
        for i in range(span // s_tile):
            s_rows = slice(i * s_tile, (i + 1) * s_tile)
            s.tile_k[...] = jnp.zeros_like(s.tile_k)
            s.tile_v[...] = jnp.zeros_like(s.tile_v)

            def tile(j, carry):
                cols = rows_at(j, t_tile)
                probs = jnp.exp2(dot(s.key_p[s_rows], s.query_t[:, cols]))
                probs_h, probs_l = split(probs)
                grads = probs * dot(s.value_p[s_rows], s.grad_t[:, cols])
                grads_h, grads_l = split(grads)
                grad_rows, query_rows = s.grad_n[cols], s.query_n[cols]
                s.tile_v[...] += dot(cat([probs_h, probs_l], 1), cat([grad_rows, grad_rows], 0))
                s.tile_k[...] += dot(cat([grads_h, grads_l], 1), cat([query_rows, query_rows], 0))
                keys = s.turned[:, s_rows]
                s.accum[:, cols] += dot(cat([keys, keys], 1), cat([grads_h, grads_l], 0))
                return carry

            lax.fori_loop(0, t_count, tile, 0)
            lane = iota((s_tile, 2 * head), 1)
            k_part, v_part = s.tile_k[...], s.tile_v[...]
            target[s_rows] = jnp.where(
                lane < head,
                (k_part + pltpu.roll(k_part, head, 1)) * (1.0 / log2e),
                v_part + pltpu.roll(v_part, head, 1),
            )
            if i == 0:
                tick(name + "_mid")

    moves_back = Sends(*s.chunk_sems[:2])
    crossing = []
    for i in range(1, grid.x):
        there = (x + i) % grid.x
        chunk(there, 1 - core, s.chunk_grad.at[2 * i], "back0" if i == 1 else "")
        over = moves_back.start(s.chunk_grad.at[2 * i], s.chunk_in.at[i], sibling)
        if i == 1:
            tick("back0_end")
        chunk(there, core, s.chunk_grad.at[2 * i + 1], "back1" if i == 1 else "")
        over.wait_recv()
        s.chunk_grad[2 * i + 1] += s.chunk_in[i]
        crossing.append(
            moves_back.start(s.chunk_grad.at[2 * i + 1], s.cross_in.at[i - 1], grid.others("x")[i - 1])
        )
        if i == 1:
            tick("back1_end")
    chunk(x, 1 - core, s.chunk_grad.at[0], "back2")
    over = moves_back.start(s.chunk_grad.at[0], s.chunk_in.at[0], sibling)
    chunk(x, core, s.chunk_grad.at[1], "back3")
    over.wait_recv()
    for copy in crossing:
        copy.wait_recv()
    own = s.chunk_grad.at[1]
    own[...] += s.chunk_in[0]
    for i in range(1, grid.x):
        own[...] += s.cross_in[i - 1]
    load_tokens.wait()

    front_rows = s.front.reshape(width, columns)

    def collect(i, carry):
        rows = rows_at(i, block)
        unit, scale = normalise(s.tokens_v[rows])
        s.cot_v[rows] = unit
        s.scale2[rows] = jnp.broadcast_to(scale, (block, 128))
        s.norm_h[rows], s.norm_l[rows] = split(unit)
        total = None
        for k in range(2):
            cols = rows_at(k * blocks + i, block)
            grad = (s.accum[:head, cols] + s.accum[head:, cols]) * (head**-0.5)
            grad = cat([grad, grad], 0).T
            wide_part = spread(grad, s.routes[rows, k : k + 1], experts)
            total = wide_part if total is None else total + wide_part
        s.mixed_h[rows], s.mixed_l[rows] = split(total)
        sums = jnp.sum(total, axis=0, keepdims=True)
        s.sums[:, :wide] = jnp.where(i == 0, 0.0, s.sums[:, :wide]) + sums
        return carry

    def collect_rest(i, carry):
        rows = rows_at(i, block)
        lane = iota((block, 2 * head), 1)
        logits = jnp.zeros((block, 2 * head), f32)
        for k in range(2):
            logits = logits + jnp.where(lane == s.routes[rows, k : k + 1], s.gates[rows, k : k + 1], 0.0)
        total = cat([own[rows], logits], 1)
        s.rest_h[rows], s.rest_l[rows] = split(total)
        sums = jnp.sum(total, axis=0, keepdims=True)
        s.sums[:, wide:] = jnp.where(i == 0, 0.0, s.sums[:, wide:]) + sums
        return carry

    gain_c, shift_c = s.vectors[...].T[:, 0:1], s.vectors[...].T[:, 1:2]

    def front_grad(lo, hi, grads):
        base = dot_tn((s.norm_h[...], s.norm_l[...]), (grads[0][...], grads[1][...]))
        weight = s.front_h[:, lo:hi].astype(f32) + s.front_l[:, lo:hi].astype(f32)
        sums = s.sums[0:1, lo:hi]
        front_rows[:, lo:hi] = gain_c * base + shift_c * sums
        return jnp.sum(weight * base, axis=1, keepdims=True), jnp.sum(weight * sums, axis=1, keepdims=True)

    lax.fori_loop(0, blocks, collect, 0)
    gain_q, shift_q = front_grad(0, wide, (s.mixed_h, s.mixed_l))
    late = [r["query0"], r["query1"]]
    for item in late:
        item.start()
    lax.fori_loop(0, blocks, collect_rest, 0)
    gain_r, shift_r = front_grad(wide, columns, (s.rest_h, s.rest_l))
    lane = iota((width, 128), 1)
    others = cat([jnp.zeros((experts, width), f32), s.vector_grad[...], jnp.zeros((120 - experts, width), f32)], 0).T
    tail_grad = front_rows[:, wide + 2 * head :] + others
    tail_grad = jnp.where(
        lane == experts, gain_q + gain_r, jnp.where(lane == experts + 1, shift_q + shift_r, tail_grad)
    )
    front_rows[:, wide + 2 * head :] = tail_grad
    for q in range(ff // 128):
        both = s.bias_grad[0:1, q * 128 : (q + 1) * 128]
        for n, row in enumerate((pltpu.roll(both, piece, 1), both)):
            at = (per_tile * q + n) * plan.shard
            old = front_rows[at : at + 1, wide + 2 * head :]
            front_rows[at : at + 1, wide + 2 * head :] = jnp.where(lanes < piece, old, row)
    r["keys"].start()
    for item in late:
        item.step(0)

    def input_block(i, carry):
        rows = rows_at(i, block)
        parts = [cat([s.mixed_h[rows], s.rest_h[rows]], 1), cat([s.mixed_l[rows], s.rest_l[rows]], 1)]
        grad = dot_nt(parts, (s.front_h[...], s.front_l[...]))
        s.tokens_v[rows] = s.norm_grad[rows] + norm_back(grad, s.cot_v[rows], s.scale2[rows, 0:1], gain)
        return carry

    lax.fori_loop(0, blocks // 4, input_block, 0)
    r["keys"].step(0)
    lax.fori_loop(blocks // 4, blocks // 2, input_block, 0)
    for item in late:
        item.step(1)
    lax.fori_loop(blocks // 2, blocks, input_block, 0)
    store_input = pltpu.make_async_copy(s.tokens_v, input_grad, s.io_sems.at[4])
    store_input.start()
    r["keys"].step(1)
    for item in late:
        item.step(2)
    for j in range(chunks):
        up_sum[:, j * part : (j + 1) * part] = r["up%d" % j].result()
    for copy in down_last:
        copy.wait_recv()
    down_total = s.down[z, y, x, core]
    for i in range(grid.z - 1):
        down_total = down_total + s.down_z[i]
    down_sum[...] = down_total
    out_sum[...] = r["out"].result()
    r["keys"].step(2)
    for name, (lo, hi) in plan.pieces.items():
        front_sum[:, lo:hi] = r[name].result()
    store_input.wait()
    for item in r.values():
        item.finish()
    moves.finish()
    moves_back.finish()
    down_moves.finish()


def step_call(plan, lengths, small, big):
    span, width = big[0].shape
    shapes = [
        (span, width), (span, width), (plan.shard, plan.columns), (plan.shard, plan.ff), (plan.ff_shard, width),
        (plan.shard, width),
    ]
    named = plan.scratch()
    named["rest_h"] = pltpu.VMEM((span, plan.columns - plan.experts * plan.head), bf16)
    named["rest_l"] = pltpu.VMEM((span, plan.columns - plan.experts * plan.head), bf16)
    named["sums"] = pltpu.VMEM((1, plan.columns), f32)
    is_leaf = lambda item: not isinstance(item, (dict, list))
    scratch, tree = jax.tree.flatten(named, is_leaf=is_leaf)
    return pl.pallas_call(
        functools.partial(step_kernel, plan, tree),
        out_shape=[jax.ShapeDtypeStruct(shape, f32) for shape in shapes],
        in_specs=[pl.BlockSpec(memory_space=pltpu.SMEM)] + vmem_specs(len(small)) + any_specs(len(big)),
        out_specs=any_specs(2) + vmem_specs(4),
        scratch_shapes=scratch,
        compiler_params=pltpu.CompilerParams(
            collective_id=0, has_side_effects=True, vmem_limit_bytes=vmem_limit
        ),
        name="training_step",
    )(lengths, *small, *big)


def update_kernel(factor, head, *refs):
    raw_output, raw_input, front, up, down, out = refs[:6]
    weights, moments, averages = refs[6:14], refs[14:22], refs[22:30]
    output, input_grad = refs[30:32]
    new_weights, new_moments, new_averages = refs[32:40], refs[40:48], refs[48:56]
    held, load_sems, store_sems = refs[56:]
    rows = held.shape[1]
    count = held.shape[0] // 2
    moves = [
        (source.at[i * rows : (i + 1) * rows], target.at[i * rows : (i + 1) * rows])
        for source, target in ((raw_output, output), (raw_input, input_grad))
        for i in range(count)
    ]
    loads = [pltpu.make_async_copy(move[0], held.at[i], load_sems.at[i]) for i, move in enumerate(moves)]
    stores = [pltpu.make_async_copy(held.at[i], move[1], store_sems.at[i]) for i, move in enumerate(moves)]
    for load in loads:
        load.start()
    wide = out.shape[1]
    tail = front[:, wide + 2 * head :]
    experts = weights[0].shape[0]
    shard = tail.shape[0]
    square = cat([tail, jnp.zeros((128 - shard, 128), f32)], 0).T
    piece = weights[5].shape[1]
    gradients = [
        square[:experts, :shard],
        front[:, :wide],
        out[...],
        front[:, wide : wide + 2 * head],
        up[...],
        pltpu.roll(tail[0:8], piece, 1)[0:1, :piece],
        down[...],
        square[experts : experts + weights[7].shape[0], :shard],
    ]
    for load, store in zip(loads, stores):
        load.wait()
        store.start()
    for i, gradient in enumerate(gradients):
        scaled = gradient * factor
        moment = moment_decay * moments[i][...] + scaled
        weight = weights[i][...] - step_rate * (scaled + moment_decay * moment)
        new_moments[i][...] = moment
        new_weights[i][...] = weight
        new_averages[i][...] = average_decay * averages[i][...] + (1.0 - average_decay) * weight
    for store in stores:
        store.wait()


def update_all(factor, head, raw_output, raw_input, front, up, down, out, weights, moments, averages):
    def flat(arrays):
        return [arrays[0].T] + [a.reshape(1, -1) if a.ndim == 1 else a for a in arrays[1:]]

    shapes = [a.shape for a in weights]
    weights, moments, averages = flat(weights), flat(moments), flat(averages)
    results = pl.pallas_call(
        functools.partial(update_kernel, factor, head),
        out_shape=[jax.ShapeDtypeStruct(raw_output.shape, f32)] * 2
        + [jax.ShapeDtypeStruct(a.shape, f32) for a in weights] * 3,
        in_specs=any_specs(2) + vmem_specs(28),
        out_specs=any_specs(2) + vmem_specs(24),
        scratch_shapes=[
            pltpu.VMEM((8, raw_output.shape[0] // 4, raw_output.shape[1]), f32),
            pltpu.SemaphoreType.DMA((8,)),
            pltpu.SemaphoreType.DMA((8,)),
        ],
        compiler_params=pltpu.CompilerParams(vmem_limit_bytes=vmem_limit),
        name="update",
    )(raw_output, raw_input, front, up, down, out, *weights, *moments, *averages)
    updated = [a.T if i % 8 == 0 else a.reshape(shapes[i % 8]) for i, a in enumerate(results[2:])]
    return (results[0][None], results[1][None]) + tuple(updated)


def fused_step(grid, tokens, cotangent, lengths, routes, *params):
    weights, moments, averages = params[:8], params[8:16], params[16:24]
    router_weight, query_weight, out_weight, kv_weight, up_weight, up_bias, down_weight, vectors = weights
    experts = router_weight.shape[1]
    head = kv_weight.shape[1] // 2
    columns = query_weight.shape[1] + 2 * head + 128
    plan = Plan(grid, tokens.shape[1], tokens.shape[2], up_weight.shape[1], head, experts, columns)
    small = (query_weight, kv_weight, router_weight.T, vectors, up_bias[None], routes[0].T)
    big = (tokens[0], cotangent[0], out_weight, up_weight, down_weight)
    raw_output, raw_input, front, up, down, out = step_call(plan, lengths, small, big)
    factor = 1.0 / math.sqrt(tokens.shape[0] * tokens.shape[1] * grid.count)
    return update_all(factor, head, raw_output, raw_input, front, up, down, out, weights, moments, averages)


def step_for(mesh):
    grid = Grid(mesh)

    def step(*args):
        shard, span = args[4].shape[0], args[0].shape[1]
        if shard % 8 == 0 and span % 512 == 0 and grid.x > 1 and grid.z == 4 and args[9].shape[0] == 64:
            return fused_step(grid, *args)
        return general_step(*args)

    return step


def solution(mesh):
    in_specs = (
        P("dp", "seq", None),
        P("dp", "seq", None),
        P("dp", None),
        P("dp", "seq", None),
        P(("dp", "seq"), None),
        P(("dp", "seq"), None),
        P(("dp", "seq"), None),
        P(("dp", "seq"), None),
        P(("dp", "seq"), None),
        P(("dp", "seq")),
        P(("dp", "seq"), None),
        P(None, ("dp", "seq")),
        P(("dp", "seq"), None),
        P(("dp", "seq"), None),
        P(("dp", "seq"), None),
        P(("dp", "seq"), None),
        P(("dp", "seq"), None),
        P(("dp", "seq")),
        P(("dp", "seq"), None),
        P(None, ("dp", "seq")),
        P(("dp", "seq"), None),
        P(("dp", "seq"), None),
        P(("dp", "seq"), None),
        P(("dp", "seq"), None),
        P(("dp", "seq"), None),
        P(("dp", "seq")),
        P(("dp", "seq"), None),
        P(None, ("dp", "seq")),
    )
    out_specs = (
        P("dp", "seq", None),
        P("dp", "seq", None),
        P(("dp", "seq"), None),
        P(("dp", "seq"), None),
        P(("dp", "seq"), None),
        P(("dp", "seq"), None),
        P(("dp", "seq"), None),
        P(("dp", "seq")),
        P(("dp", "seq"), None),
        P(None, ("dp", "seq")),
        P(("dp", "seq"), None),
        P(("dp", "seq"), None),
        P(("dp", "seq"), None),
        P(("dp", "seq"), None),
        P(("dp", "seq"), None),
        P(("dp", "seq")),
        P(("dp", "seq"), None),
        P(None, ("dp", "seq")),
        P(("dp", "seq"), None),
        P(("dp", "seq"), None),
        P(("dp", "seq"), None),
        P(("dp", "seq"), None),
        P(("dp", "seq"), None),
        P(("dp", "seq")),
        P(("dp", "seq"), None),
        P(None, ("dp", "seq")),
    )
    return jax.shard_map(
        step_for(mesh), mesh=mesh, in_specs=in_specs, out_specs=out_specs, check_vma=False
    )
```

```python
import functools
import math
import types

import jax
import jax.numpy as jnp
from jax import lax
from jax.experimental import pallas as pl
from jax.experimental.pallas import tpu as pltpu
from jax.sharding import PartitionSpec as P

highest = lax.Precision.HIGHEST
norm_eps = 1e-05
step_rate = 0.02
moment_decay = 0.9
average_decay = 0.99


def matmul(left, right):
    return jnp.dot(left, right, precision=highest, preferred_element_type=jnp.float32)


def layer_norm(values, gain, shift):
    centre = values - jnp.mean(values, axis=-1, keepdims=True)
    spread = jnp.mean(centre * centre, axis=-1, keepdims=True)
    return centre * lax.rsqrt(spread + norm_eps) * gain + shift


def project_in(row_tokens, vectors, router_weight, query_weight, kv_weight, onehot):
    normed = layer_norm(row_tokens, vectors[0], vectors[1])
    logits = matmul(normed, router_weight)
    chosen = jnp.einsum("tke,te->tk", onehot, logits, precision=highest)
    gates = jax.nn.softmax(chosen, axis=-1)
    experts = onehot.shape[2]
    all_queries = matmul(normed, query_weight).reshape(normed.shape[0], experts, -1)
    queries = jnp.einsum("tke,ted->tkd", onehot, all_queries, precision=highest)
    keyval = matmul(normed, kv_weight)
    return (queries, keyval, gates)


def project_out(
    row_tokens, heads, gates, onehot, vectors, out_weight, up_weight, up_bias, down_weight
):
    mixed = jnp.einsum("tk,tke,tkd->ted", gates, onehot, heads, precision=highest)
    mixed = mixed.reshape(row_tokens.shape[0], -1)
    middle = row_tokens + matmul(mixed, out_weight)
    normed = layer_norm(middle, vectors[2], vectors[3])
    hidden = jax.nn.gelu(matmul(normed, up_weight) + up_bias)
    return middle + matmul(hidden, down_weight) + vectors[4]


def update(weight, gradient, moment, average, factor):
    scaled = gradient * factor
    moment_new = moment_decay * moment + scaled
    weight_new = weight - step_rate * (scaled + moment_decay * moment_new)
    average_new = average_decay * average + (1.0 - average_decay) * weight_new
    return (weight_new, moment_new, average_new)


def general_step(
    tokens,
    cotangent,
    lengths,
    routes,
    router_weight,
    query_weight,
    out_weight,
    kv_weight,
    up_weight,
    up_bias,
    down_weight,
    vectors,
    router_moment,
    query_moment,
    out_moment,
    kv_moment,
    up_moment,
    bias_moment,
    down_moment,
    vector_moment,
    router_average,
    query_average,
    out_average,
    kv_average,
    up_average,
    bias_average,
    down_average,
    vector_average,
):
    full_router, full_query, full_out, full_kv, full_up, full_bias, full_down, full_vectors = (
        lax.all_gather(router_weight, ("dp", "seq"), axis=0, tiled=True),
        lax.all_gather(query_weight, ("dp", "seq"), axis=0, tiled=True),
        lax.all_gather(out_weight, ("dp", "seq"), axis=0, tiled=True),
        lax.all_gather(kv_weight, ("dp", "seq"), axis=0, tiled=True),
        lax.all_gather(up_weight, ("dp", "seq"), axis=0, tiled=True),
        lax.all_gather(up_bias, ("dp", "seq"), axis=0, tiled=True),
        lax.all_gather(down_weight, ("dp", "seq"), axis=0, tiled=True),
        lax.all_gather(vectors, ("dp", "seq"), axis=1, tiled=True),
    )
    local_tokens = tokens[0]
    local_cotangent = cotangent[0]
    span = local_tokens.shape[0]
    row_length = span * lax.axis_size("seq")
    offset = lax.axis_index("seq") * span
    ends = jnp.cumsum(lengths[0])
    positions = jnp.arange(row_length, dtype=jnp.int32)
    segment_all = jnp.sum((positions[:, None] >= ends[None, :]).astype(jnp.int32), axis=1)
    segment_local = lax.dynamic_slice_in_dim(segment_all, offset, span)
    experts = full_router.shape[1]
    onehot = (routes[0][:, :, None] == jnp.arange(experts, dtype=jnp.int32)[None, None, :]).astype(
        jnp.float32
    )

    def front(tokens_in, vectors_in, router_in, query_in, kv_in):
        return project_in(tokens_in, vectors_in, router_in, query_in, kv_in, onehot)

    (queries, keyval, gates), front_pull = jax.vjp(
        front, local_tokens, full_vectors, full_router, full_query, full_kv
    )
    head_width = queries.shape[-1]
    choices_count = queries.shape[1]
    score_scale = head_width ** (-0.5)
    kv_piece = lax.all_gather(keyval, "seq", axis=0, tiled=True)
    best = jnp.full((span, choices_count), -1e30, jnp.float32)
    keys = kv_piece[:, :head_width]
    values = kv_piece[:, head_width:]
    key_segment = segment_all
    scores = jnp.einsum("tkd,sd->tks", queries, keys, precision=highest) * score_scale
    same_sent = segment_local[:, None, None] == key_segment[None, None, :]
    peak = jnp.maximum(best, jnp.max(jnp.where(same_sent, scores, -1e30), axis=-1))
    weights_soft = jnp.where(same_sent, jnp.exp(scores - peak[..., None]), 0.0)
    total = jnp.sum(weights_soft, axis=-1)
    accum = jnp.einsum("tks,sd->tkd", weights_soft, values, precision=highest)
    best, total, accum = (peak, total, accum)
    heads = accum / total[..., None]
    logsum = best + jnp.log(total)

    def tail(tokens_in, heads_in, gates_in, vectors_in, out_in, up_in, bias_in, down_in):
        return project_out(
            tokens_in, heads_in, gates_in, onehot, vectors_in, out_in, up_in, bias_in, down_in
        )

    output, tail_pull = jax.vjp(
        tail, local_tokens, heads, gates, full_vectors, full_out, full_up, full_bias, full_down
    )
    (
        tokens_grad_tail,
        heads_grad,
        gates_grad,
        vectors_grad_tail,
        out_grad,
        up_grad,
        bias_grad,
        down_grad,
    ) = tail_pull(local_cotangent)
    row_delta = jnp.sum(heads_grad * heads, axis=-1)
    kv_piece = lax.all_gather(keyval, "seq", axis=0, tiled=True)
    keys = kv_piece[:, :head_width]
    values = kv_piece[:, head_width:]
    key_segment = segment_all
    scores = jnp.einsum("tkd,sd->tks", queries, keys, precision=highest) * score_scale
    same_sent = segment_local[:, None, None] == key_segment[None, None, :]
    weights_soft = jnp.where(same_sent, jnp.exp(scores - logsum[..., None]), 0.0)
    weights_grad = jnp.einsum("tkd,sd->tks", heads_grad, values, precision=highest)
    scores_grad = weights_soft * (weights_grad - row_delta[..., None]) * score_scale
    query_grad = jnp.einsum("tks,sd->tkd", scores_grad, keys, precision=highest)
    keys_grad = jnp.einsum("tks,tkd->sd", scores_grad, queries, precision=highest)
    values_grad = jnp.einsum("tks,tkd->sd", weights_soft, heads_grad, precision=highest)
    joined = jnp.concatenate([keys_grad, values_grad], axis=1)
    keyval_grad = joined
    query_grad, keyval_partial = (query_grad, keyval_grad)
    keyval_grad = lax.psum_scatter(keyval_partial, "seq", scatter_dimension=0, tiled=True)
    tokens_grad_front, vectors_grad_front, router_grad, query_weight_grad, kv_grad = front_pull(
        (query_grad, keyval_grad, gates_grad)
    )
    input_grad = tokens_grad_tail + tokens_grad_front
    vectors_grad = vectors_grad_tail + vectors_grad_front
    shards = (
        router_weight,
        query_weight,
        out_weight,
        kv_weight,
        up_weight,
        up_bias,
        down_weight,
        vectors,
    )
    shard_dims = (0, 0, 0, 0, 0, 0, 0, 1)
    summed = lax.psum(
        (
            router_grad,
            query_weight_grad,
            out_grad,
            kv_grad,
            up_grad,
            bias_grad,
            down_grad,
            vectors_grad,
        ),
        ("dp", "seq"),
    )
    place = lax.axis_index(("dp", "seq"))
    reduced = tuple(
        (
            lax.dynamic_slice_in_dim(
                whole_grad, place * shard.shape[shard_dim], shard.shape[shard_dim], shard_dim
            )
            for whole_grad, shard, shard_dim in zip(summed, shards, shard_dims)
        )
    )
    all_tokens = span * lax.axis_size("seq") * tokens.shape[0] * lax.axis_size("dp")
    factor = 1.0 / math.sqrt(all_tokens)
    new_router, new_router_moment, new_router_average = update(
        router_weight, reduced[0], router_moment, router_average, factor
    )
    new_query, new_query_moment, new_query_average = update(
        query_weight, reduced[1], query_moment, query_average, factor
    )
    new_out, new_out_moment, new_out_average = update(
        out_weight, reduced[2], out_moment, out_average, factor
    )
    new_kv, new_kv_moment, new_kv_average = update(
        kv_weight, reduced[3], kv_moment, kv_average, factor
    )
    new_up, new_up_moment, new_up_average = update(
        up_weight, reduced[4], up_moment, up_average, factor
    )
    new_bias, new_bias_moment, new_bias_average = update(
        up_bias, reduced[5], bias_moment, bias_average, factor
    )
    new_down, new_down_moment, new_down_average = update(
        down_weight, reduced[6], down_moment, down_average, factor
    )
    new_vectors, new_vector_moment, new_vector_average = update(
        vectors, reduced[7], vector_moment, vector_average, factor
    )
    return (
        output[None],
        input_grad[None],
        new_router,
        new_query,
        new_out,
        new_kv,
        new_up,
        new_bias,
        new_down,
        new_vectors,
        new_router_moment,
        new_query_moment,
        new_out_moment,
        new_kv_moment,
        new_up_moment,
        new_bias_moment,
        new_down_moment,
        new_vector_moment,
        new_router_average,
        new_query_average,
        new_out_average,
        new_kv_average,
        new_up_average,
        new_bias_average,
        new_down_average,
        new_vector_average,
    )


f32 = jnp.float32
bf16 = jnp.bfloat16
MESH = pl.DeviceIdType.MESH
log2e = math.log2(math.e)
far = 2.0**100
vmem_limit = 62 * 2**20
NN = (((1,), (0,)), ((), ()))
NT = (((1,), (1,)), ((), ()))
TN = (((0,), (0,)), ((), ()))


def dot(left, right, dims=NN):
    return lax.dot_general(left, right, dims, preferred_element_type=f32)


def split(values):
    high = values.astype(bf16)
    return high, (values - high.astype(f32)).astype(bf16)


def split_wide(values):
    high = values.astype(bf16).astype(f32)
    return high, values - high


def cat(parts, axis):
    return jnp.concatenate(parts, axis=axis)


def dot_nn(left, right):
    return dot(cat([left[0], left[1], left[0]], 1), cat([right[0], right[0], right[1]], 0))


def dot_nt(left, right):
    return dot(cat([left[0], left[1], left[0]], 1), cat([right[0], right[0], right[1]], 1), NT)


def dot_tn(left, right):
    return dot(cat([left[0], left[1], left[0]], 0), cat([right[0], right[0], right[1]], 0), TN)


def iota(shape, dim):
    return lax.broadcasted_iota(jnp.int32, shape, dim)


def rows_at(index, count):
    return pl.ds(pl.multiple_of(index * count, count), count)


class Grid:
    def __init__(self, mesh):
        dp, seq = mesh.shape["dp"], mesh.shape["seq"]
        self.x = max(seq // 2, 1)
        self.y = self.x if dp % self.x == 0 else 1
        self.z = dp // self.y
        self.count = dp * seq
        self.lead = (self.z, self.y, self.x, 2)

    def here(self):
        dp, seq = lax.axis_index("dp"), lax.axis_index("seq")
        return dp // self.y, dp % self.y, seq // 2, seq % 2

    def device(self, z, y, x, core):
        return (z * self.y + y, x * 2 + core)

    def others(self, axis):
        z, y, x, core = self.here()
        if axis == "z":
            return [self.device((z + i) % self.z, y, x, core) for i in range(1, self.z)]
        if axis == "y":
            return [self.device(z, (y + i) % self.y, x, core) for i in range(1, self.y)]
        if axis == "x":
            return [self.device(z, y, (x + i) % self.x, core) for i in range(1, self.x)]
        return [self.device(z, y, x, 1 - core)]

    def copies(self):
        return self.z + self.y + self.x - 2

    def greet(self):
        barrier = pltpu.get_barrier_semaphore()
        for axis in "zyxc":
            for device in self.others(axis):
                pl.semaphore_signal(barrier, inc=1, device_id=device, device_id_type=MESH)

    def meet(self):
        pl.semaphore_wait(pltpu.get_barrier_semaphore(), sum(len(self.others(axis)) for axis in "zyxc"))


class Sends:
    def __init__(self, send, recv):
        self.send, self.recv, self.used, self.started = send, recv, 0, []

    def start(self, source, target, device):
        copy = pltpu.make_async_remote_copy(
            src_ref=source,
            dst_ref=target,
            send_sem=self.send.at[self.used],
            recv_sem=self.recv.at[self.used],
            device_id=device,
            device_id_type=MESH,
        )
        self.used += 1
        copy.start()
        self.started.append(copy)
        return copy

    def finish(self):
        for copy in self.started:
            copy.wait_send()


def vmem_specs(count):
    return [pl.BlockSpec(memory_space=pltpu.VMEM)] * count


def any_specs(count):
    return [pl.BlockSpec(memory_space=pl.ANY)] * count


def sentence_bounds(lengths, marks, first):
    start = jnp.zeros(marks.shape, jnp.int32)
    end = jnp.zeros(marks.shape, jnp.int32)
    at = jnp.int32(0)
    for e in range(lengths.shape[1]):
        after = at + lengths[0, e]
        start = jnp.where(marks == first + e, at, start)
        end = jnp.where(marks == first + e, after, end)
        at = after
    return start, end


def in_sentence(positions, start, end):
    return jnp.logical_and(positions >= start, positions < end).astype(f32)


def query_pack(transposed, extra):
    high, low = split(transposed[: transposed.shape[0] // 2])
    return cat([high, low, high, extra.astype(bf16)], 0)


def key_pack(doubled, extra):
    lanes = iota(doubled.shape, 1)
    half = doubled.shape[1] // 2
    high, low = split_wide(doubled)
    return cat([high.astype(bf16), jnp.where(lanes < half, low, extra).astype(bf16)], 1)


def half_split(doubled, axis):
    half = doubled.shape[axis] // 2
    high, low = split_wide(doubled)
    return jnp.where(iota(doubled.shape, axis) < half, high, low).astype(bf16)


def twice(pair):
    half = pair.shape[1] // 2
    turned = pltpu.roll(pair, half, 1)
    lanes = iota(pair.shape, 1)
    return jnp.where(lanes < half, pair, turned), jnp.where(lanes < half, turned, pair)


def pick(wide, route, head):
    lanes = iota((wide.shape[0], 2 * head), 1) // head
    total = None
    for group in range(wide.shape[1] // (2 * head)):
        part = jnp.where(lanes + 2 * group == route, wide[:, group * 2 * head : (group + 1) * 2 * head], 0.0)
        total = part if total is None else total + part
    return total + pltpu.roll(total, head, 1)


def spread(doubled, route, experts):
    head = doubled.shape[1] // 2
    lanes = iota(doubled.shape, 1) // head
    return cat([jnp.where(lanes + 2 * group == route, doubled, 0.0) for group in range(experts // 2)], 1)


def normalise(values):
    centre = values - jnp.mean(values, axis=-1, keepdims=True)
    scale = lax.rsqrt(jnp.mean(centre * centre, axis=-1, keepdims=True) + norm_eps)
    return centre * scale, scale


def norm_back(grad, unit, scale, gain):
    inner = grad * gain
    mean = jnp.mean(inner, axis=-1, keepdims=True)
    along = jnp.mean(inner * unit, axis=-1, keepdims=True)
    return scale * (inner - mean - unit * along)


class Gather:
    def __init__(self, grid, source, target, axes, order, sems):
        self.grid, self.source, self.target, self.axes, self.order = grid, source, target, axes, order
        self.sends, self.local = Sends(*sems[:2]), sems[2]
        self.current, self.own = [], None

    def view(self, **fixed):
        fixed["c"] = self.grid.here()[3]
        return self.target.at[tuple(fixed.get(axis, slice(None)) for axis in self.axes + "c")]

    def start(self):
        z, y, x, core = self.grid.here()
        mine = self.view(z=z, y=y, x=x)
        self.own = pltpu.make_async_copy(self.source, mine, self.local)
        self.own.start()
        self.current = [self.sends.start(self.source, mine, device) for device in self.grid.others("z")]

    def wait(self):
        for copy in self.current:
            copy.wait_recv()
        self.current = []
        if self.own is not None:
            self.own.wait()
            self.own = None

    def step(self, number):
        z, y, x, core = self.grid.here()
        self.wait()
        if number == 0:
            view = self.view(y=y, x=x)
        elif number == 1:
            view = self.view(x=x) if self.order[0] == "y" else self.view(y=y)
        else:
            view = self.view()
        axis = (self.order + "c")[number]
        self.current = [self.sends.start(view, view, device) for device in self.grid.others(axis)]

    def finish(self):
        self.wait()
        self.sends.finish()


class Reduce:
    def __init__(self, grid, source, axes, order, parts, sems):
        self.grid, self.source, self.axes, self.order, self.parts = grid, source, axes, order, parts
        self.sends, self.current, self.done = Sends(*sems[:2]), [], {}

    def view(self, core, **fixed):
        fixed["c"] = core
        return self.source.at[tuple(fixed.get(axis, slice(None)) for axis in self.axes + "c")]

    def start(self):
        core = self.grid.here()[3]
        self.send("c", [self.view(1 - core)], 0)

    def send(self, axis, views, part):
        devices = self.grid.others(axis)
        self.current = [
            self.sends.start(view, self.parts[part].at[i], device)
            for i, (view, device) in enumerate(zip(views, devices))
        ]
        self.part = part

    def take(self):
        core = self.grid.here()[3]
        view = self.view(core, **self.done)
        for copy in self.current:
            copy.wait_recv()
        for i in range(len(self.current)):
            view[...] += self.parts[self.part][i]
        self.current = []

    def step(self, number):
        z, y, x, core = self.grid.here()
        self.take()
        axis = (self.order + "z")[number]
        if axis not in self.axes:
            return
        size, at = {"z": (self.grid.z, z), "y": (self.grid.y, y), "x": (self.grid.x, x)}[axis]
        views = [
            self.view(core, **{**self.done, axis: (at + i) % size}) for i in range(1, size)
        ]
        self.send(axis, views, number + 1)
        self.done = {**self.done, axis: at}

    def result(self):
        self.take()
        return self.view(self.grid.here()[3], **self.done)[...]

    def finish(self):
        self.sends.finish()


def reduce_scratch(grid, shape, axes, order):
    size = {"z": grid.z, "y": grid.y, "x": grid.x}
    dims = lambda names: tuple(size[axis] for axis in axes if axis in names)
    parts = [
        pltpu.VMEM((1,) + dims(axes) + shape, f32),
        pltpu.VMEM((size[order[0]] - 1,) + dims(axes.replace(order[0], "")) + shape, f32),
        pltpu.VMEM((size[order[1]] - 1,) + dims(axes.replace("x", "").replace("y", "")) + shape, f32),
    ]
    if "z" in axes:
        parts.append(pltpu.VMEM((grid.z - 1,) + shape, f32))
    return parts


def copy_sems(count):
    return [pltpu.SemaphoreType.DMA((count,)), pltpu.SemaphoreType.DMA((count,)), pltpu.SemaphoreType.DMA]


gather_orders = (
    ("keys", "yx"),
    ("query0", "xy"),
    ("query1", "xy"),
    ("out", "xy"),
    ("up0", "yx"),
    ("up1", "xy"),
    ("up2", "yx"),
    ("up3", "xy"),
    ("down", "yx"),
    ("down0", "yx"),
    ("down1", "yx"),
    ("down2", "xy"),
    ("down3", "xy"),
)
reduce_orders = (
    ("up0", "yx"),
    ("up1", "xy"),
    ("up2", "xy"),
    ("up3", "xy"),
    ("down0", "yx"),
    ("down1", "xy"),
    ("down2", "yx"),
    ("down3", "yx"),
    ("out", "xy"),
    ("keys", "xy"),
    ("query0", "xy"),
    ("query1", "yx"),
)
moves_at = {
    "queries": "+out0",
    "split": "+up00",
    "own_mid": "+out1 +up01",
    "near_mid": "hand +down +down00 +up10",
    "near_end": "+down20",
    "far_mid": "+out2 +down10",
    "far_end": "+up02 +down01",
    "last_mid": "+up11 +down21 +down30",
    "last_end": "+down11 +up20",
    "mix": "+up30 +down02",
    "part00": "+up12 +down12 +up21 +down22 +up31 +down31",
    "part10": "+up22 -up00 -down00",
    "part11": "+up32 +down32",
    "part21": "-up01 -down01 -up10 -down10",
    "part31": "-up20 -down20",
    "heads_end": "-up02 -down02 -down21 -up30 -down30",
    "back0_mid": "-up11 -down11 -out0",
    "back0_end": "-down31",
    "back1_mid": "-up12 -down12 -up21 -down22",
    "back2_mid": "-up22 -up31 -down32 -out1 shards",
    "back3_mid": "-up32 -out2",
}


def plan_spills(chunks):
    return 6 * chunks


class Plan:
    def __init__(self, grid, span, width, ff, head, experts, columns):
        self.grid, self.span, self.width, self.ff = grid, span, width, ff
        self.head, self.experts, self.columns = head, experts, columns
        self.shard, self.ff_shard = width // grid.count, ff // grid.count
        self.chunks = grid.z
        self.part = ff // self.chunks
        self.pieces = {"keys": (experts * head, columns), "query0": (0, experts * head // 2)}
        self.pieces["query1"] = (experts * head // 2, experts * head)
        part, chunks = self.part, self.chunks
        shard = (self.shard, part)
        ff_shard = (self.ff_shard, width)
        self.gathers = [(name, "yx" if name[:-1] == "down" else "zyx", order) for name, order in gather_orders]
        shapes = {"out": (self.shard, width)}
        for name, (lo, hi) in self.pieces.items():
            shapes[name] = (self.shard, hi - lo)
        self.reduces = []
        for name, order in reduce_orders:
            shape = shapes.get(name, ff_shard if name.startswith("down") else shard)
            self.reduces.append((name, shape, "yx" if name.startswith("down") else "zyx", order))

    def scratch(self):
        grid, span, width, head = self.grid, self.span, self.width, self.head
        lead = grid.lead
        part = self.part
        b, f = lambda *shape: pltpu.VMEM(shape, bf16), lambda *shape: pltpu.VMEM(shape, f32)
        named = dict(
            tokens_v=f(span, width), cot_v=f(span, width), norm_grad=f(span, width),
            cot_h=b(span, width), cot_l=b(span, width), norm_h=b(span, width), norm_l=b(span, width),
            mixed_h=b(span, width), mixed_l=b(span, width), side=f(span, 128), heads=f(span, 2 * head),
            packed=f(self.shard, self.columns), square=f(128, 128),
            front=pltpu.VMEM(lead + (self.shard, self.columns), f32),
            front_h=b(width, self.columns), front_l=b(width, self.columns),
            vectors=f(8, width), vector_grad=f(8, width), bias=f(1, self.ff), bias_grad=f(1, self.ff),
            even=f(grid.count, 128), odd=f(grid.count, 128),
            query_t=b(4 * head, 2 * span), query_n=b(2 * span, 2 * head),
            grad_t=b(4 * head, 2 * span), grad_n=b(2 * span, 2 * head),
            keyval=f(grid.x, 2, span, 2 * head),
            key_p=b(span, 4 * head), value_p=b(span, 4 * head), turned=b(2 * head, span),
            accum=f(2 * head, 2 * span), peak=f(1, 2 * span), total=f(1, 2 * span), logsum=f(1, 2 * span),
            tile_k=f(min(512, span), 2 * head), tile_v=f(min(512, span), 2 * head),
            chunk_grad=f(2 * grid.x, span, 2 * head), chunk_in=f(grid.x, span, 2 * head),
            cross_in=f(max(grid.x - 1, 1), span, 2 * head),
            out=pltpu.VMEM(lead + (self.shard, width), f32), out_h=b(width, width), out_l=b(width, width),
            up=pltpu.VMEM(lead + (self.shard, self.ff), f32), down=pltpu.VMEM(lead + (self.ff_shard, width), f32),
            up_h=b(width, part), up_l=b(width, part), down_h=b(part, width), down_l=b(part, width),
            down_z=f(grid.z - 1, self.ff_shard, width),
            kv_sems=copy_sems(2 * grid.x - 1), chunk_sems=copy_sems(2 * grid.x - 1), down_sems=copy_sems(grid.z - 1),
            io_sems=pltpu.SemaphoreType.DMA((6,)), spill_sems=pltpu.SemaphoreType.DMA((plan_spills(self.chunks),)),
            fill_sems=pltpu.SemaphoreType.DMA((2, 4)),
        )
        copies = grid.z + grid.y + grid.x
        named["gather_sems"] = [copy_sems(copies) for _ in self.gathers]
        named["reduce_sems"] = [copy_sems(copies) for _ in self.reduces]
        named["reduce_parts"] = [
            reduce_scratch(grid, shape, axes, order) for _, shape, axes, order in self.reduces
        ]
        return named


def attention_sides(plan, lengths, at, count, offset):
    marks = iota((1, 2 * plan.head), 1) - plan.head
    start, end = sentence_bounds(lengths, marks, 0)
    positions = at + offset + iota((count, 1), 0)
    outside = (in_sentence(positions, start, end) - 1.0) * far
    return marks, jnp.where(jnp.logical_and(marks >= 0, marks < lengths.shape[1]), outside, 0.0)


def three(values):
    one = values.astype(bf16).astype(f32)
    two = (values - one).astype(bf16).astype(f32)
    return one, two, values - one - two


def step_kernel(plan, tree, lengths, query_w, kv_w, router_t, vectors_w, bias_w, routes_t,
                tokens, cotangent, out_w, up_w, down_w,
                output, input_grad, hidden_hh, hidden_hl, down_hh, down_hl, front_sum, up_sum, down_sum, out_sum,
                *scratch):
    s = types.SimpleNamespace(**jax.tree.unflatten(tree, scratch))
    grid, span, width, head, experts = plan.grid, plan.span, plan.width, plan.head, plan.experts
    ff, part, chunks, columns = plan.ff, plan.part, plan.chunks, plan.columns
    wide = experts * head
    z, y, x, core = grid.here()
    seq_at = (x * 2 + core) * span
    block = min(256, span)
    blocks = span // block

    load_tokens = pltpu.make_async_copy(tokens, s.tokens_v, s.io_sems.at[0])
    load_tokens.start()
    load_cot = pltpu.make_async_copy(cotangent, s.cot_v, s.io_sems.at[1])
    load_cot.start()

    grid.greet()
    s.square[...] = jnp.zeros_like(s.square)
    s.square[0:experts, 0 : plan.shard] = router_t[...]
    s.square[experts : experts + vectors_w.shape[0], 0 : plan.shard] = vectors_w[...]
    s.packed[:, :wide] = query_w[...]
    s.packed[:, wide : wide + 2 * head] = kv_w[...]
    s.packed[:, wide + 2 * head :] = s.square[...].T[: plan.shard]
    piece = ff // grid.count
    s.packed[0:1, columns - piece :] = bias_w[...]

    sources = {"out": (out_w, s.out), "down": (down_w, s.down)}
    for name, (lo, hi) in plan.pieces.items():
        sources[name] = (s.packed.at[:, lo:hi], s.front.at[:, :, :, :, :, lo:hi])
    for j in range(chunks):
        cols = slice(j * part, (j + 1) * part)
        sources["up%d" % j] = (up_w.at[:, cols], s.up.at[:, :, :, :, :, cols])
        sources["down%d" % j] = (None, s.down.at[j])
    g = {
        name: Gather(grid, *sources[name], axes, order, sems)
        for (name, axes, order), sems in zip(plan.gathers, s.gather_sems)
    }
    targets = {name: target for name, (_, target) in sources.items()}
    r = {
        name: Reduce(grid, targets[name], axes, order, parts, sems)
        for (name, _, axes, order), parts, sems in zip(plan.reduces, s.reduce_parts, s.reduce_sems)
    }

    grid.meet()
    g["keys"].start()

    def routes_block(i, carry):
        cols = rows_at(i, block)
        pair = routes_t[:, cols].astype(f32)
        tall = cat([pair, jnp.zeros((126, block), f32)], 0)
        s.side[cols] = tall.T
        return carry

    def unit_block(i, carry):
        rows = rows_at(i, block)
        s.norm_grad[rows] = normalise(s.tokens_v[rows])[0]
        return carry

    def cot_block(i, carry):
        rows = rows_at(i, block)
        s.cot_h[rows], s.cot_l[rows] = split(s.cot_v[rows])
        return carry

    keys, queries = g["keys"], [g["query0"], g["query1"]]
    lax.fori_loop(0, blocks, routes_block, 0)
    keys.step(0)
    for item in queries:
        item.start()
    load_tokens.wait()
    lax.fori_loop(0, blocks, unit_block, 0)
    keys.step(1)
    for item in queries:
        item.step(0)
    for name in ("out", "up0", "down"):
        g[name].start()
    load_cot.wait()
    lax.fori_loop(0, blocks, cot_block, 0)
    keys.step(2)
    for item in queries:
        item.step(1)
    keys.wait()

    def front_part(name):
        lo, hi = plan.pieces[name]
        part_w = s.front[:, :, :, :, :, lo:hi].reshape(width, hi - lo)
        s.front_h[:, lo:hi], s.front_l[:, lo:hi] = split(part_w)
        return part_w

    tail = front_part("keys")[:, 2 * head :]
    s.vectors[...] = tail.T[experts : experts + 8]
    gain, shift = s.vectors[0:1], s.vectors[1:2]

    def route_of(rows, k):
        return s.side[rows, k : k + 1].astype(jnp.int32)

    def project_keys(i, carry):
        rows = rows_at(i, block)
        normed_s = split(s.norm_grad[rows] * gain + shift)
        s.norm_h[rows], s.norm_l[rows] = normed_s
        result = dot_nn(normed_s, (s.front_h[:, wide:], s.front_l[:, wide:]))
        s.keyval[x, core, rows] = result[:, : 2 * head]
        lane = iota((block, 2 * head), 1)
        logits = result[:, 2 * head :]
        chosen = [
            jnp.sum(jnp.where(lane == route_of(rows, k), logits, 0.0), axis=1, keepdims=True) for k in range(2)
        ]
        top = jnp.maximum(chosen[0], chosen[1])
        raw = [jnp.exp(c - top) for c in chosen]
        norm = raw[0] + raw[1]
        s.side[rows, 2:4] = cat([raw[0] / norm, raw[1] / norm], 1)
        return carry

    lax.fori_loop(0, blocks, project_keys, 0, unroll=2)
    moves = Sends(*s.kv_sems[:2])
    mine = s.keyval.at[x, core]
    sibling = grid.others("c")[0]
    to_sibling = moves.start(mine, mine, sibling)
    across = [moves.start(mine, mine, device) for device in grid.others("x")]
    for item in queries:
        item.step(2)
    for j in range(1, chunks):
        g["up%d" % j].start()
    forwards = {}

    def hand_on(i):
        across[i - 1].wait_recv()
        view = s.keyval.at[(x - i + grid.x) % grid.x, core]
        forwards[i] = moves.start(view, view, sibling)

    down_moves = Sends(*s.down_sems[:2])
    down_last = []

    def tick(name):
        for move in moves_at.get(name, "").split():
            if move == "hand":
                hand_on(1)
            elif move == "+down":
                g["down"].wait()
            elif move == "shards":
                for i, device in enumerate(grid.others("z")):
                    source = s.down.at[(z + i + 1) % grid.z, y, x, core]
                    down_last.append(down_moves.start(source, s.down_z.at[i], device))
            else:
                (g if move[0] == "+" else r)[move[1:-1]].step(int(move[-1]))

    tick("queries")
    for item in queries:
        item.wait()
    front_part("query0")
    front_part("query1")
    lanes = iota((1, 128), 1)
    for p in range(grid.count):
        s.odd[p : p + 1] = tail[p * plan.shard : p * plan.shard + 1]
    s.even[...] = pltpu.roll(s.odd[...], piece, 1)
    per_tile = 128 // piece
    for q in range(ff // 128):
        s.bias[0:1, q * 128 : (q + 1) * 128] = jnp.where(
            lanes < piece, s.even[per_tile * q : per_tile * q + 1], s.odd[per_tile * q + 1 : per_tile * q + 2]
        )

    def project_queries(i, carry):
        rows = rows_at(i, block)
        result = dot_nn((s.norm_h[rows], s.norm_l[rows]), (s.front_h[:, :wide], s.front_l[:, :wide]))
        marks = iota((head, 1), 0)
        start, end = sentence_bounds(lengths, marks, 0)
        positions = seq_at + i * block + iota((1, block), 1)
        inside = in_sentence(positions, start, end)
        for k in range(2):
            query = pick(result, route_of(rows, k), head) * (log2e * head**-0.5)
            at = rows_at(k * blocks + i, block)
            s.query_n[at] = half_split(query, 1)
            s.query_t[:, at] = query_pack(query.T, inside)
        return carry

    tick("split")
    lax.fori_loop(0, blocks, project_queries, 0, unroll=2)
    for item in [keys] + queries:
        item.finish()

    s.accum[...] = jnp.zeros_like(s.accum)
    s.peak[...] = jnp.full_like(s.peak, -3e38)
    s.total[...] = jnp.zeros_like(s.total)
    t_tile = width
    t_count = 2 * span // t_tile

    def attend(chunk_x, chunk_core, name):
        at = (chunk_x * 2 + chunk_core) * span

        def prepare(i, carry):
            rows = rows_at(i, block)
            keys, values = twice(s.keyval[chunk_x, chunk_core, rows])
            _, outside = attention_sides(plan, lengths, at, block, i * block)
            s.key_p[rows] = key_pack(keys, outside)
            s.turned[:, rows] = half_split(values.T, 0)
            return carry

        lax.fori_loop(0, blocks, prepare, 0, unroll=2)

        def tile(i, carry):
            cols = rows_at(i, t_tile)
            s.norm_grad[...] = dot(s.key_p[...], s.query_t[:, cols])
            old = s.peak[0:1, cols]
            new = jnp.maximum(old, jnp.max(s.norm_grad[...], axis=0, keepdims=True))
            fade = jnp.exp2(old - new)
            probs = jnp.exp2(s.norm_grad[...] - new)
            high, low = split(probs)
            weights = s.turned[...]
            add = dot(cat([weights, weights], 1), cat([high, low], 0))
            s.total[0:1, cols] = s.total[0:1, cols] * fade + jnp.sum(probs, axis=0, keepdims=True)
            s.accum[:, cols] = s.accum[:, cols] * fade + add
            s.peak[0:1, cols] = new
            return carry

        lax.fori_loop(0, t_count // 2, tile, 0, unroll=2)
        tick(name + "_mid")
        lax.fori_loop(t_count // 2, t_count, tile, 0, unroll=2)
        tick(name + "_end")

    attend(x, core, "own")
    to_sibling.wait_recv()
    attend(x, 1 - core, "near")
    for i in range(1, grid.x):
        if i not in forwards:
            hand_on(i)
        attend((x - i + grid.x) % grid.x, core, "far" if i == 1 else "")
        forwards[i].wait_recv()
        attend((x - i + grid.x) % grid.x, 1 - core, "last" if i == 1 else "")

    def finish(i, carry):
        marks = iota((16, 1), 0)
        start, end = sentence_bounds(lengths, marks, 0)
        positions = seq_at + i * block + iota((1, block), 1)
        inside = in_sentence(positions, start, end)
        results = []
        for k in range(2):
            cols = rows_at(k * blocks + i, block)
            norm = s.total[0:1, cols]
            results.append((s.accum[:head, cols] + s.accum[head:, cols]) / norm)
            side = inside
            for n, term in enumerate(three(-(s.peak[0:1, cols] + jnp.log2(norm)))):
                side = jnp.where(marks == 8 + n, term, side)
            s.query_t[3 * head : 3 * head + 16, cols] = side.astype(bf16)
        s.heads[rows_at(i, block)] = cat(results, 0).T
        return carry

    lax.fori_loop(0, blocks, finish, 0, unroll=2)
    tick("finish")
    g["out"].finish()
    s.out_h[...], s.out_l[...] = split(s.out[...].reshape(width, width))
    gain2, shift2, last = s.vectors[2:3], s.vectors[3:4], s.vectors[4:5]

    def gate_pair(rows):
        return [s.side[rows, 2 + k : 3 + k] for k in range(2)]

    def mixed_heads(rows, gate):
        mixed = None
        for k, doubled in enumerate(twice(s.heads[rows])):
            own = gate[k] * doubled
            wide_part = spread(own, route_of(rows, k), experts)
            mixed = wide_part if mixed is None else mixed + wide_part
        return split(mixed)

    def mix(i, carry):
        rows = rows_at(i, block)
        mixed_s = mixed_heads(rows, gate_pair(rows))
        middle = s.tokens_v[rows] + dot_nn(mixed_s, (s.out_h[...], s.out_l[...]))
        unit, scale = normalise(middle)
        s.cot_v[rows] = unit
        s.side[rows, 6:7] = scale
        s.norm_h[rows], s.norm_l[rows] = split(unit * gain2 + shift2)
        s.tokens_v[rows] = middle + last
        s.norm_grad[rows] = jnp.zeros((block, width), f32)
        return carry

    lax.fori_loop(0, blocks, mix, 0, unroll=2)
    tick("mix")
    store_middle = pltpu.make_async_copy(s.tokens_v, output, s.io_sems.at[2])
    store_middle.start()

    up_rows, down_rows = s.up.reshape(width, ff), s.down.reshape(ff, width)
    row_block = min(512, span)

    def hidden_part(j, i):
        rows = slice(i * row_block, (i + 1) * row_block)
        cols = slice(j * part, (j + 1) * part)
        cot_s = (s.cot_h[rows], s.cot_l[rows])
        norm_s = (s.norm_h[rows], s.norm_l[rows])
        up_s = (s.up_h[...], s.up_l[...])
        down_s = (s.down_h[...], s.down_l[...])
        pre = dot_nn(norm_s, up_s) + s.bias[0:1, cols]
        back = dot_nt(cot_s, down_s)
        square = pre * pre
        wave = jnp.tanh(math.sqrt(2.0 / math.pi) * (pre + 0.044715 * (square * pre)))
        half_wave = 0.5 * (1.0 + wave)
        hidden_s = split(pre * half_wave)
        slope = half_wave + (0.5 * math.sqrt(2.0 / math.pi)) * pre * (1.0 - wave * wave) * (
            1.0 + (3.0 * 0.044715) * square
        )
        pre_grad = back * slope
        pre_s = split(pre_grad)
        s.mixed_h[rows], s.mixed_l[rows] = hidden_s
        s.norm_grad[rows] += dot_nt(pre_s, up_s)
        down_part = dot_tn(hidden_s, cot_s)
        up_part = dot_tn(norm_s, pre_s)
        bias_part = jnp.sum(pre_grad, axis=0, keepdims=True)
        if i == 0:
            down_rows[cols] = down_part
            up_rows[:, cols] = up_part
            s.bias_grad[0:1, cols] = bias_part
        else:
            down_rows[cols] += down_part
            up_rows[:, cols] += up_part
            s.bias_grad[0:1, cols] += bias_part

    spills, spill_count = {}, [0]

    def spill(*pairs):
        copies = []
        for source, target in pairs:
            copies.append(pltpu.make_async_copy(source, target, s.spill_sems.at[spill_count[0]]))
            copies[-1].start()
            spill_count[0] += 1
        return copies

    def fill(slot, j):
        pairs = zip((hidden_hh, hidden_hl, down_hh, down_hl), slots[slot])
        copies = [
            pltpu.make_async_copy(source.at[j], target, s.fill_sems.at[slot, n])
            for n, (source, target) in enumerate(pairs)
        ]
        for copy in copies:
            copy.start()
        return copies

    slots = [(s.cot_h, s.cot_l, s.down_h, s.down_l), (s.norm_h, s.norm_l, s.up_h, s.up_l)]

    for j in range(chunks):
        cols = slice(j * part, (j + 1) * part)
        if j == 0:
            g["down"].finish()
        g["up%d" % j].finish()
        g["down%d" % j].finish()
        s.up_h[...], s.up_l[...] = split(up_rows[:, cols])
        for copy in spills.pop("weights", []):
            copy.wait()
        s.down_h[...], s.down_l[...] = split(down_rows[cols])
        spills["weights"] = spill((s.down_h, down_hh.at[j]), (s.down_l, down_hl.at[j]))
        for i in range(span // row_block):
            for copy in spills.pop(i, []):
                copy.wait()
            hidden_part(j, i)
            rows = slice(i * row_block, (i + 1) * row_block)
            spills[i] = spill(
                (s.mixed_h.at[rows], hidden_hh.at[j, rows]), (s.mixed_l.at[rows], hidden_hl.at[j, rows])
            )
            if i + 1 == span // row_block:
                r["up%d" % j].start()
                r["down%d" % j].start()
            tick("part%d%d" % (j, i))

    store_middle.wait()
    load_tokens = pltpu.make_async_copy(tokens, s.tokens_v, s.io_sems.at[3])
    load_tokens.start()
    for copies in spills.values():
        for copy in copies:
            copy.wait()
    s.vector_grad[...] = jnp.zeros_like(s.vector_grad)
    out_rows = s.out.reshape(width, width)

    def heads_block(i, carry):
        rows = rows_at(i, block)
        grad = s.norm_grad[rows]
        unit = s.cot_v[rows]
        cot = s.cot_h[rows].astype(f32) + s.cot_l[rows].astype(f32)
        s.vector_grad[2:3] += jnp.sum(grad * unit, axis=0, keepdims=True)
        s.vector_grad[3:4] += jnp.sum(grad, axis=0, keepdims=True)
        s.vector_grad[4:5] += jnp.sum(cot, axis=0, keepdims=True)
        mid = cot + norm_back(grad, unit, s.side[rows, 6:7], gain2)
        s.norm_grad[rows] = mid
        mid_s = split(mid)
        s.norm_h[rows], s.norm_l[rows] = mid_s
        grad_mixed = dot_nt(mid_s, (s.out_h[...], s.out_l[...]))
        gate = gate_pair(rows)
        s.mixed_h[rows], s.mixed_l[rows] = mixed_heads(rows, gate)
        lane = iota((block, 2 * head), 1)
        marks = iota((head, 1), 0)
        gates_grad = []
        for k, doubled in enumerate(twice(s.heads[rows])):
            at = rows_at(k * blocks + i, block)
            picked = pick(grad_mixed, route_of(rows, k), head)
            gate_grad = jnp.sum(jnp.where(lane < head, picked * doubled, 0.0), axis=1, keepdims=True)
            gates_grad.append(gate_grad)
            own = gate[k] * picked
            s.grad_n[at] = half_split(own, 1)
            turned = jnp.where(lane < head, own, gate_grad * gate[k]).T
            side = jnp.zeros((head, block), f32)
            for n, term in enumerate(three(-turned[head : head + 1])):
                side = jnp.where(marks == n, term, side)
            s.grad_t[:, at] = query_pack(turned, side)
        both = gate[0] * gates_grad[0] + gate[1] * gates_grad[1]
        s.side[rows, 4:6] = cat([gate[k] * (gates_grad[k] - both) for k in range(2)], 1)
        return carry

    lax.fori_loop(0, blocks // 2, heads_block, 0, unroll=2)
    tick("heads_mid")
    lax.fori_loop(blocks // 2, blocks, heads_block, 0, unroll=2)
    out_rows[...] = dot_tn((s.mixed_h[...], s.mixed_l[...]), (s.norm_h[...], s.norm_l[...]))
    r["out"].start()
    tick("heads_end")
    filled = [fill(0, 0), None]

    s.accum[...] = jnp.zeros_like(s.accum)
    s_tile = min(512, span)

    def chunk(chunk_x, chunk_core, target, name):
        at = (chunk_x * 2 + chunk_core) * span

        def prepare(i, carry):
            rows = rows_at(i, block)
            keys, values = twice(s.keyval[chunk_x, chunk_core, rows])
            marks, outside = attention_sides(plan, lengths, at, block, i * block)
            ones = jnp.logical_and(marks >= 8, marks < 11)
            s.key_p[rows] = key_pack(keys, jnp.where(ones, 1.0, outside))
            few = jnp.logical_and(marks >= 0, marks < 3).astype(f32)
            s.value_p[rows] = key_pack(values, jnp.broadcast_to(few, values.shape))
            s.turned[:, rows] = half_split(keys.T, 0)
            return carry

        lax.fori_loop(0, blocks, prepare, 0, unroll=2)
        for i in range(span // s_tile):
            s_rows = slice(i * s_tile, (i + 1) * s_tile)
            s.tile_k[...] = jnp.zeros_like(s.tile_k)
            s.tile_v[...] = jnp.zeros_like(s.tile_v)

            def tile(j, carry):
                cols = rows_at(j, t_tile)
                probs = jnp.exp2(dot(s.key_p[s_rows], s.query_t[:, cols]))
                probs_h, probs_l = split(probs)
                grads = probs * dot(s.value_p[s_rows], s.grad_t[:, cols])
                grads_h, grads_l = split(grads)
                grad_rows, query_rows = s.grad_n[cols], s.query_n[cols]
                s.tile_v[...] += dot(cat([probs_h, probs_l], 1), cat([grad_rows, grad_rows], 0))
                s.tile_k[...] += dot(cat([grads_h, grads_l], 1), cat([query_rows, query_rows], 0))
                keys = s.turned[:, s_rows]
                s.accum[:, cols] += dot(cat([keys, keys], 1), cat([grads_h, grads_l], 0))
                return carry

            lax.fori_loop(0, t_count, tile, 0, unroll=2)
            lane = iota((s_tile, 2 * head), 1)
            k_part, v_part = s.tile_k[...], s.tile_v[...]
            target[s_rows] = jnp.where(
                lane < head,
                (k_part + pltpu.roll(k_part, head, 1)) * (1.0 / log2e),
                v_part + pltpu.roll(v_part, head, 1),
            )
            if i == 0:
                tick(name + "_mid")

    moves_back = Sends(*s.chunk_sems[:2])
    crossing = []
    for i in range(1, grid.x):
        there = (x + i) % grid.x
        chunk(there, 1 - core, s.chunk_grad.at[2 * i], "back0" if i == 1 else "")
        over = moves_back.start(s.chunk_grad.at[2 * i], s.chunk_in.at[i], sibling)
        if i == 1:
            tick("back0_end")
        chunk(there, core, s.chunk_grad.at[2 * i + 1], "back1" if i == 1 else "")
        over.wait_recv()
        s.chunk_grad[2 * i + 1] += s.chunk_in[i]
        crossing.append(
            moves_back.start(s.chunk_grad.at[2 * i + 1], s.cross_in.at[i - 1], grid.others("x")[i - 1])
        )
        if i == 1:
            tick("back1_end")
    chunk(x, 1 - core, s.chunk_grad.at[0], "back2")
    over = moves_back.start(s.chunk_grad.at[0], s.chunk_in.at[0], sibling)
    chunk(x, core, s.chunk_grad.at[1], "back3")
    over.wait_recv()
    for copy in crossing:
        copy.wait_recv()
    own = s.chunk_grad.at[1]
    own[...] += s.chunk_in[0]
    for i in range(1, grid.x):
        own[...] += s.cross_in[i - 1]
    load_tokens.wait()

    front_rows = s.front.reshape(width, columns)

    def collect(i, carry):
        rows = rows_at(i, block)
        unit, scale = normalise(s.tokens_v[rows])
        s.cot_v[rows] = unit
        s.side[rows, 6:7] = scale
        s.norm_h[rows], s.norm_l[rows] = split(unit)
        total = None
        for k in range(2):
            cols = rows_at(k * blocks + i, block)
            grad = (s.accum[:head, cols] + s.accum[head:, cols]) * (head**-0.5)
            grad = cat([grad, grad], 0).T
            wide_part = spread(grad, route_of(rows, k), experts)
            total = wide_part if total is None else total + wide_part
        s.mixed_h[rows], s.mixed_l[rows] = split(total)
        sums = jnp.sum(total, axis=0, keepdims=True)
        s.sums[:, :wide] = jnp.where(i == 0, 0.0, s.sums[:, :wide]) + sums
        return carry

    def collect_rest(i, carry):
        rows = rows_at(i, block)
        lane = iota((block, 2 * head), 1)
        logits = jnp.zeros((block, 2 * head), f32)
        for k in range(2):
            logits = logits + jnp.where(lane == route_of(rows, k), s.side[rows, 4 + k : 5 + k], 0.0)
        total = cat([own[rows], logits], 1)
        s.rest_h[rows], s.rest_l[rows] = split(total)
        sums = jnp.sum(total, axis=0, keepdims=True)
        s.sums[:, wide:] = jnp.where(i == 0, 0.0, s.sums[:, wide:]) + sums
        return carry

    gain_c, shift_c = s.vectors[...].T[:, 0:1], s.vectors[...].T[:, 1:2]

    def front_grad(lo, hi, grads):
        base = dot_tn((s.norm_h[...], s.norm_l[...]), (grads[0][...], grads[1][...]))
        weight = s.front_h[:, lo:hi].astype(f32) + s.front_l[:, lo:hi].astype(f32)
        sums = s.sums[0:1, lo:hi]
        front_rows[:, lo:hi] = gain_c * base + shift_c * sums
        return jnp.sum(weight * base, axis=1, keepdims=True), jnp.sum(weight * sums, axis=1, keepdims=True)

    lax.fori_loop(0, blocks, collect, 0, unroll=2)
    load_middle = pltpu.make_async_copy(output, s.tokens_v, s.io_sems.at[5])
    load_middle.start()
    gain_q, shift_q = front_grad(0, wide, (s.mixed_h, s.mixed_l))
    late = [r["query0"], r["query1"]]
    for item in late:
        item.start()
    lax.fori_loop(0, blocks, collect_rest, 0, unroll=2)
    gain_r, shift_r = front_grad(wide, columns, (s.rest_h, s.rest_l))
    filled[1] = fill(1, 1)
    lane = iota((width, 128), 1)
    others = cat([jnp.zeros((experts, width), f32), s.vector_grad[...], jnp.zeros((120 - experts, width), f32)], 0).T
    tail_grad = front_rows[:, wide + 2 * head :] + others
    tail_grad = jnp.where(
        lane == experts, gain_q + gain_r, jnp.where(lane == experts + 1, shift_q + shift_r, tail_grad)
    )
    front_rows[:, wide + 2 * head :] = tail_grad
    for q in range(ff // 128):
        both = s.bias_grad[0:1, q * 128 : (q + 1) * 128]
        for n, row in enumerate((pltpu.roll(both, piece, 1), both)):
            at = (per_tile * q + n) * plan.shard
            old = front_rows[at : at + 1, wide + 2 * head :]
            front_rows[at : at + 1, wide + 2 * head :] = jnp.where(lanes < piece, old, row)
    r["keys"].start()
    for item in late:
        item.step(0)

    def input_block(i, carry):
        rows = rows_at(i, block)
        parts = [cat([s.mixed_h[rows], s.rest_h[rows]], 1), cat([s.mixed_l[rows], s.rest_l[rows]], 1)]
        grad = dot_nt(parts, (s.front_h[...], s.front_l[...]))
        s.norm_grad[rows] += norm_back(grad, s.cot_v[rows], s.side[rows, 6:7], gain)
        return carry

    def output_part(j):
        slot = j % 2
        for copy in filled[slot]:
            copy.wait()
        hidden_h, hidden_l, weight_h, weight_l = slots[slot]

        def output_block(i, carry):
            rows = rows_at(i, block)
            s.tokens_v[rows] += dot_nn((hidden_h[rows], hidden_l[rows]), (weight_h[...], weight_l[...]))
            return carry

        lax.fori_loop(0, blocks, output_block, 0, unroll=2)
        if j + 2 < chunks:
            filled[slot] = fill(slot, j + 2)

    lax.fori_loop(0, blocks // 2, input_block, 0, unroll=2)
    r["keys"].step(0)
    lax.fori_loop(blocks // 2, blocks, input_block, 0, unroll=2)
    store_input = pltpu.make_async_copy(s.norm_grad, input_grad, s.io_sems.at[4])
    store_input.start()
    for item in late:
        item.step(1)
    load_middle.wait()
    output_part(0)
    r["keys"].step(1)
    output_part(1)
    for item in late:
        item.step(2)
    output_part(2)
    r["keys"].step(2)
    for j in range(3, chunks):
        output_part(j)
    store_output = pltpu.make_async_copy(s.tokens_v, output, s.io_sems.at[2])
    store_output.start()
    for j in range(chunks):
        up_sum[:, j * part : (j + 1) * part] = r["up%d" % j].result()
    for copy in down_last:
        copy.wait_recv()
    down_total = s.down[z, y, x, core]
    for i in range(grid.z - 1):
        down_total = down_total + s.down_z[i]
    down_sum[...] = down_total
    out_sum[...] = r["out"].result()
    for name, (lo, hi) in plan.pieces.items():
        front_sum[:, lo:hi] = r[name].result()
    store_input.wait()
    store_output.wait()
    for item in r.values():
        item.finish()
    moves.finish()
    moves_back.finish()
    down_moves.finish()


def step_call(plan, lengths, small, big):
    span, width = big[0].shape
    shapes = [(plan.shard, plan.columns), (plan.shard, plan.ff), (plan.ff_shard, width), (plan.shard, width)]
    spill = [(plan.chunks, span, plan.part)] * 2 + [(plan.chunks, plan.part, width)] * 2
    named = plan.scratch()
    named["rest_h"] = pltpu.VMEM((span, plan.columns - plan.experts * plan.head), bf16)
    named["rest_l"] = pltpu.VMEM((span, plan.columns - plan.experts * plan.head), bf16)
    named["sums"] = pltpu.VMEM((1, plan.columns), f32)
    is_leaf = lambda item: not isinstance(item, (dict, list))
    scratch, tree = jax.tree.flatten(named, is_leaf=is_leaf)
    return pl.pallas_call(
        functools.partial(step_kernel, plan, tree),
        out_shape=[jax.ShapeDtypeStruct((span, width), f32)] * 2
        + [jax.ShapeDtypeStruct(shape, bf16) for shape in spill]
        + [jax.ShapeDtypeStruct(shape, f32) for shape in shapes],
        in_specs=[pl.BlockSpec(memory_space=pltpu.SMEM)] + vmem_specs(len(small)) + any_specs(len(big)),
        out_specs=any_specs(6) + vmem_specs(4),
        scratch_shapes=scratch,
        compiler_params=pltpu.CompilerParams(
            collective_id=0, has_side_effects=True, vmem_limit_bytes=vmem_limit
        ),
        name="training_step",
    )(lengths, *small, *big)


def update_kernel(factor, head, *refs):
    raw, small, results = refs[:2], refs[2:30], refs[30:56]
    held_raw, held, made = refs[56], refs[57:85], refs[85:109]
    load_sems, store_sems, raw_load_sems, raw_store_sems = refs[109:]
    loads = [pltpu.make_async_copy(a, b, load_sems.at[i]) for i, (a, b) in enumerate(zip(small, held))]
    for load in loads:
        load.start()
    rows = held_raw.shape[1]
    count = held_raw.shape[0] // 2
    moves = [
        (source.at[i * rows : (i + 1) * rows], target.at[i * rows : (i + 1) * rows])
        for source, target in zip(raw, results[:2])
        for i in range(count)
    ]
    raw_loads = [pltpu.make_async_copy(m[0], held_raw.at[i], raw_load_sems.at[i]) for i, m in enumerate(moves)]
    raw_stores = [pltpu.make_async_copy(held_raw.at[i], m[1], raw_store_sems.at[i]) for i, m in enumerate(moves)]
    for load in raw_loads:
        load.start()
    for load in loads:
        load.wait()
    front, up, down, out = held[:4]
    weights, moments, averages = held[4:12], held[12:20], held[20:28]
    new_weights, new_moments, new_averages = made[:8], made[8:16], made[16:24]
    wide = out.shape[1]
    tail = front[:, wide + 2 * head :]
    experts = weights[0].shape[0]
    shard = tail.shape[0]
    square = cat([tail, jnp.zeros((128 - shard, 128), f32)], 0).T
    piece = weights[5].shape[1]
    gradients = [
        square[:experts, :shard],
        front[:, :wide],
        out[...],
        front[:, wide : wide + 2 * head],
        up[...],
        pltpu.roll(tail[0:8], piece, 1)[0:1, :piece],
        down[...],
        square[experts : experts + weights[7].shape[0], :shard],
    ]
    for i, gradient in enumerate(gradients):
        scaled = gradient * factor
        moment = moment_decay * moments[i][...] + scaled
        weight = weights[i][...] - step_rate * (scaled + moment_decay * moment)
        new_moments[i][...] = moment
        new_weights[i][...] = weight
        new_averages[i][...] = average_decay * averages[i][...] + (1.0 - average_decay) * weight
    stores = [pltpu.make_async_copy(a, b, store_sems.at[i]) for i, (a, b) in enumerate(zip(made, results[2:]))]
    for store in stores:
        store.start()
    for load, store in zip(raw_loads, raw_stores):
        load.wait()
        store.start()
    for store in stores + raw_stores:
        store.wait()


def update_all(factor, head, raw_output, raw_input, front, up, down, out, weights, moments, averages):
    def flat(arrays):
        return [arrays[0].T] + [a.reshape(1, -1) if a.ndim == 1 else a for a in arrays[1:]]

    shapes = [a.shape for a in weights]
    weights, moments, averages = flat(weights), flat(moments), flat(averages)
    small = [front, up, down, out, *weights, *moments, *averages]
    results = pl.pallas_call(
        functools.partial(update_kernel, factor, head),
        out_shape=[jax.ShapeDtypeStruct(raw_output.shape, f32)] * 2
        + [jax.ShapeDtypeStruct(a.shape, f32) for a in weights] * 3,
        in_specs=any_specs(30),
        out_specs=any_specs(26),
        scratch_shapes=[pltpu.VMEM((8, raw_output.shape[0] // 4, raw_output.shape[1]), f32)]
        + [pltpu.VMEM(a.shape, f32) for a in small]
        + [pltpu.VMEM(a.shape, f32) for a in weights] * 3
        + [pltpu.SemaphoreType.DMA((28,)), pltpu.SemaphoreType.DMA((24,))]
        + [pltpu.SemaphoreType.DMA((8,)), pltpu.SemaphoreType.DMA((8,))],
        compiler_params=pltpu.CompilerParams(vmem_limit_bytes=vmem_limit),
        name="update",
    )(raw_output, raw_input, *small)
    updated = [a.T if i % 8 == 0 else a.reshape(shapes[i % 8]) for i, a in enumerate(results[2:])]
    return (results[0][None], results[1][None]) + tuple(updated)


def fused_step(grid, tokens, cotangent, lengths, routes, *params):
    weights, moments, averages = params[:8], params[8:16], params[16:24]
    router_weight, query_weight, out_weight, kv_weight, up_weight, up_bias, down_weight, vectors = weights
    experts = router_weight.shape[1]
    head = kv_weight.shape[1] // 2
    columns = query_weight.shape[1] + 2 * head + 128
    plan = Plan(grid, tokens.shape[1], tokens.shape[2], up_weight.shape[1], head, experts, columns)
    small = (query_weight, kv_weight, router_weight.T, vectors, up_bias[None], routes[0].T)
    big = (tokens[0], cotangent[0], out_weight, up_weight, down_weight)
    raw_output, raw_input, _, _, _, _, front, up, down, out = step_call(plan, lengths, small, big)
    factor = 1.0 / math.sqrt(tokens.shape[0] * tokens.shape[1] * grid.count)
    return update_all(factor, head, raw_output, raw_input, front, up, down, out, weights, moments, averages)


def step_for(mesh):
    grid = Grid(mesh)

    def step(*args):
        shard, span = args[4].shape[0], args[0].shape[1]
        if shard % 8 == 0 and span % 512 == 0 and grid.x > 1 and grid.z == 4 and args[9].shape[0] == 64:
            return fused_step(grid, *args)
        return general_step(*args)

    return step


def solution(mesh):
    in_specs = (
        P("dp", "seq", None),
        P("dp", "seq", None),
        P("dp", None),
        P("dp", "seq", None),
        P(("dp", "seq"), None),
        P(("dp", "seq"), None),
        P(("dp", "seq"), None),
        P(("dp", "seq"), None),
        P(("dp", "seq"), None),
        P(("dp", "seq")),
        P(("dp", "seq"), None),
        P(None, ("dp", "seq")),
        P(("dp", "seq"), None),
        P(("dp", "seq"), None),
        P(("dp", "seq"), None),
        P(("dp", "seq"), None),
        P(("dp", "seq"), None),
        P(("dp", "seq")),
        P(("dp", "seq"), None),
        P(None, ("dp", "seq")),
        P(("dp", "seq"), None),
        P(("dp", "seq"), None),
        P(("dp", "seq"), None),
        P(("dp", "seq"), None),
        P(("dp", "seq"), None),
        P(("dp", "seq")),
        P(("dp", "seq"), None),
        P(None, ("dp", "seq")),
    )
    out_specs = (
        P("dp", "seq", None),
        P("dp", "seq", None),
        P(("dp", "seq"), None),
        P(("dp", "seq"), None),
        P(("dp", "seq"), None),
        P(("dp", "seq"), None),
        P(("dp", "seq"), None),
        P(("dp", "seq")),
        P(("dp", "seq"), None),
        P(None, ("dp", "seq")),
        P(("dp", "seq"), None),
        P(("dp", "seq"), None),
        P(("dp", "seq"), None),
        P(("dp", "seq"), None),
        P(("dp", "seq"), None),
        P(("dp", "seq")),
        P(("dp", "seq"), None),
        P(None, ("dp", "seq")),
        P(("dp", "seq"), None),
        P(("dp", "seq"), None),
        P(("dp", "seq"), None),
        P(("dp", "seq"), None),
        P(("dp", "seq"), None),
        P(("dp", "seq")),
        P(("dp", "seq"), None),
        P(None, ("dp", "seq")),
    )
    return jax.shard_map(
        step_for(mesh), mesh=mesh, in_specs=in_specs, out_specs=out_specs, check_vma=False
    )
```

```python
import functools
import math
import types

import jax
import jax.numpy as jnp
from jax import lax
from jax.experimental import pallas as pl
from jax.experimental.pallas import tpu as pltpu
from jax.sharding import PartitionSpec as P

highest = lax.Precision.HIGHEST
norm_eps = 1e-05
step_rate = 0.02
moment_decay = 0.9
average_decay = 0.99


def matmul(left, right):
    return jnp.dot(left, right, precision=highest, preferred_element_type=jnp.float32)


def layer_norm(values, gain, shift):
    centre = values - jnp.mean(values, axis=-1, keepdims=True)
    spread = jnp.mean(centre * centre, axis=-1, keepdims=True)
    return centre * lax.rsqrt(spread + norm_eps) * gain + shift


def project_in(row_tokens, vectors, router_weight, query_weight, kv_weight, onehot):
    normed = layer_norm(row_tokens, vectors[0], vectors[1])
    logits = matmul(normed, router_weight)
    chosen = jnp.einsum("tke,te->tk", onehot, logits, precision=highest)
    gates = jax.nn.softmax(chosen, axis=-1)
    experts = onehot.shape[2]
    all_queries = matmul(normed, query_weight).reshape(normed.shape[0], experts, -1)
    queries = jnp.einsum("tke,ted->tkd", onehot, all_queries, precision=highest)
    keyval = matmul(normed, kv_weight)
    return (queries, keyval, gates)


def project_out(
    row_tokens, heads, gates, onehot, vectors, out_weight, up_weight, up_bias, down_weight
):
    mixed = jnp.einsum("tk,tke,tkd->ted", gates, onehot, heads, precision=highest)
    mixed = mixed.reshape(row_tokens.shape[0], -1)
    middle = row_tokens + matmul(mixed, out_weight)
    normed = layer_norm(middle, vectors[2], vectors[3])
    hidden = jax.nn.gelu(matmul(normed, up_weight) + up_bias)
    return middle + matmul(hidden, down_weight) + vectors[4]


def update(weight, gradient, moment, average, factor):
    scaled = gradient * factor
    moment_new = moment_decay * moment + scaled
    weight_new = weight - step_rate * (scaled + moment_decay * moment_new)
    average_new = average_decay * average + (1.0 - average_decay) * weight_new
    return (weight_new, moment_new, average_new)


def general_step(
    tokens,
    cotangent,
    lengths,
    routes,
    router_weight,
    query_weight,
    out_weight,
    kv_weight,
    up_weight,
    up_bias,
    down_weight,
    vectors,
    router_moment,
    query_moment,
    out_moment,
    kv_moment,
    up_moment,
    bias_moment,
    down_moment,
    vector_moment,
    router_average,
    query_average,
    out_average,
    kv_average,
    up_average,
    bias_average,
    down_average,
    vector_average,
):
    full_router, full_query, full_out, full_kv, full_up, full_bias, full_down, full_vectors = (
        lax.all_gather(router_weight, ("dp", "seq"), axis=0, tiled=True),
        lax.all_gather(query_weight, ("dp", "seq"), axis=0, tiled=True),
        lax.all_gather(out_weight, ("dp", "seq"), axis=0, tiled=True),
        lax.all_gather(kv_weight, ("dp", "seq"), axis=0, tiled=True),
        lax.all_gather(up_weight, ("dp", "seq"), axis=0, tiled=True),
        lax.all_gather(up_bias, ("dp", "seq"), axis=0, tiled=True),
        lax.all_gather(down_weight, ("dp", "seq"), axis=0, tiled=True),
        lax.all_gather(vectors, ("dp", "seq"), axis=1, tiled=True),
    )
    local_tokens = tokens[0]
    local_cotangent = cotangent[0]
    span = local_tokens.shape[0]
    row_length = span * lax.axis_size("seq")
    offset = lax.axis_index("seq") * span
    ends = jnp.cumsum(lengths[0])
    positions = jnp.arange(row_length, dtype=jnp.int32)
    segment_all = jnp.sum((positions[:, None] >= ends[None, :]).astype(jnp.int32), axis=1)
    segment_local = lax.dynamic_slice_in_dim(segment_all, offset, span)
    experts = full_router.shape[1]
    onehot = (routes[0][:, :, None] == jnp.arange(experts, dtype=jnp.int32)[None, None, :]).astype(
        jnp.float32
    )

    def front(tokens_in, vectors_in, router_in, query_in, kv_in):
        return project_in(tokens_in, vectors_in, router_in, query_in, kv_in, onehot)

    (queries, keyval, gates), front_pull = jax.vjp(
        front, local_tokens, full_vectors, full_router, full_query, full_kv
    )
    head_width = queries.shape[-1]
    choices_count = queries.shape[1]
    score_scale = head_width ** (-0.5)
    kv_piece = lax.all_gather(keyval, "seq", axis=0, tiled=True)
    best = jnp.full((span, choices_count), -1e30, jnp.float32)
    keys = kv_piece[:, :head_width]
    values = kv_piece[:, head_width:]
    key_segment = segment_all
    scores = jnp.einsum("tkd,sd->tks", queries, keys, precision=highest) * score_scale
    same_sent = segment_local[:, None, None] == key_segment[None, None, :]
    peak = jnp.maximum(best, jnp.max(jnp.where(same_sent, scores, -1e30), axis=-1))
    weights_soft = jnp.where(same_sent, jnp.exp(scores - peak[..., None]), 0.0)
    total = jnp.sum(weights_soft, axis=-1)
    accum = jnp.einsum("tks,sd->tkd", weights_soft, values, precision=highest)
    best, total, accum = (peak, total, accum)
    heads = accum / total[..., None]
    logsum = best + jnp.log(total)

    def tail(tokens_in, heads_in, gates_in, vectors_in, out_in, up_in, bias_in, down_in):
        return project_out(
            tokens_in, heads_in, gates_in, onehot, vectors_in, out_in, up_in, bias_in, down_in
        )

    output, tail_pull = jax.vjp(
        tail, local_tokens, heads, gates, full_vectors, full_out, full_up, full_bias, full_down
    )
    (
        tokens_grad_tail,
        heads_grad,
        gates_grad,
        vectors_grad_tail,
        out_grad,
        up_grad,
        bias_grad,
        down_grad,
    ) = tail_pull(local_cotangent)
    row_delta = jnp.sum(heads_grad * heads, axis=-1)
    kv_piece = lax.all_gather(keyval, "seq", axis=0, tiled=True)
    keys = kv_piece[:, :head_width]
    values = kv_piece[:, head_width:]
    key_segment = segment_all
    scores = jnp.einsum("tkd,sd->tks", queries, keys, precision=highest) * score_scale
    same_sent = segment_local[:, None, None] == key_segment[None, None, :]
    weights_soft = jnp.where(same_sent, jnp.exp(scores - logsum[..., None]), 0.0)
    weights_grad = jnp.einsum("tkd,sd->tks", heads_grad, values, precision=highest)
    scores_grad = weights_soft * (weights_grad - row_delta[..., None]) * score_scale
    query_grad = jnp.einsum("tks,sd->tkd", scores_grad, keys, precision=highest)
    keys_grad = jnp.einsum("tks,tkd->sd", scores_grad, queries, precision=highest)
    values_grad = jnp.einsum("tks,tkd->sd", weights_soft, heads_grad, precision=highest)
    joined = jnp.concatenate([keys_grad, values_grad], axis=1)
    keyval_grad = joined
    query_grad, keyval_partial = (query_grad, keyval_grad)
    keyval_grad = lax.psum_scatter(keyval_partial, "seq", scatter_dimension=0, tiled=True)
    tokens_grad_front, vectors_grad_front, router_grad, query_weight_grad, kv_grad = front_pull(
        (query_grad, keyval_grad, gates_grad)
    )
    input_grad = tokens_grad_tail + tokens_grad_front
    vectors_grad = vectors_grad_tail + vectors_grad_front
    shards = (
        router_weight,
        query_weight,
        out_weight,
        kv_weight,
        up_weight,
        up_bias,
        down_weight,
        vectors,
    )
    shard_dims = (0, 0, 0, 0, 0, 0, 0, 1)
    summed = lax.psum(
        (
            router_grad,
            query_weight_grad,
            out_grad,
            kv_grad,
            up_grad,
            bias_grad,
            down_grad,
            vectors_grad,
        ),
        ("dp", "seq"),
    )
    place = lax.axis_index(("dp", "seq"))
    reduced = tuple(
        (
            lax.dynamic_slice_in_dim(
                whole_grad, place * shard.shape[shard_dim], shard.shape[shard_dim], shard_dim
            )
            for whole_grad, shard, shard_dim in zip(summed, shards, shard_dims)
        )
    )
    all_tokens = span * lax.axis_size("seq") * tokens.shape[0] * lax.axis_size("dp")
    factor = 1.0 / math.sqrt(all_tokens)
    new_router, new_router_moment, new_router_average = update(
        router_weight, reduced[0], router_moment, router_average, factor
    )
    new_query, new_query_moment, new_query_average = update(
        query_weight, reduced[1], query_moment, query_average, factor
    )
    new_out, new_out_moment, new_out_average = update(
        out_weight, reduced[2], out_moment, out_average, factor
    )
    new_kv, new_kv_moment, new_kv_average = update(
        kv_weight, reduced[3], kv_moment, kv_average, factor
    )
    new_up, new_up_moment, new_up_average = update(
        up_weight, reduced[4], up_moment, up_average, factor
    )
    new_bias, new_bias_moment, new_bias_average = update(
        up_bias, reduced[5], bias_moment, bias_average, factor
    )
    new_down, new_down_moment, new_down_average = update(
        down_weight, reduced[6], down_moment, down_average, factor
    )
    new_vectors, new_vector_moment, new_vector_average = update(
        vectors, reduced[7], vector_moment, vector_average, factor
    )
    return (
        output[None],
        input_grad[None],
        new_router,
        new_query,
        new_out,
        new_kv,
        new_up,
        new_bias,
        new_down,
        new_vectors,
        new_router_moment,
        new_query_moment,
        new_out_moment,
        new_kv_moment,
        new_up_moment,
        new_bias_moment,
        new_down_moment,
        new_vector_moment,
        new_router_average,
        new_query_average,
        new_out_average,
        new_kv_average,
        new_up_average,
        new_bias_average,
        new_down_average,
        new_vector_average,
    )


f32 = jnp.float32
bf16 = jnp.bfloat16
MESH = pl.DeviceIdType.MESH
log2e = math.log2(math.e)
far = 2.0**100
vmem_limit = 62 * 2**20
NN = (((1,), (0,)), ((), ()))
NT = (((1,), (1,)), ((), ()))
TN = (((0,), (0,)), ((), ()))


def dot(left, right, dims=NN):
    return lax.dot_general(left, right, dims, preferred_element_type=f32)


def split(values):
    high = values.astype(bf16)
    return high, (values - high.astype(f32)).astype(bf16)


def split_wide(values):
    high = values.astype(bf16).astype(f32)
    return high, values - high


def cat(parts, axis):
    return jnp.concatenate(parts, axis=axis)


def dot_nn(left, right):
    return dot(cat([left[0], left[1], left[0]], 1), cat([right[0], right[0], right[1]], 0))


def dot_nt(left, right):
    return dot(cat([left[0], left[1], left[0]], 1), cat([right[0], right[0], right[1]], 1), NT)


def dot_tn(left, right):
    return dot(cat([left[0], left[1], left[0]], 0), cat([right[0], right[0], right[1]], 0), TN)


def iota(shape, dim):
    return lax.broadcasted_iota(jnp.int32, shape, dim)


def rows_at(index, count):
    return pl.ds(pl.multiple_of(index * count, count), count)


class Grid:
    def __init__(self, mesh):
        dp, seq = mesh.shape["dp"], mesh.shape["seq"]
        self.x = max(seq // 2, 1)
        self.y = self.x if dp % self.x == 0 else 1
        self.z = dp // self.y
        self.count = dp * seq
        self.lead = (self.z, self.y, self.x, 2)

    def here(self):
        dp, seq = lax.axis_index("dp"), lax.axis_index("seq")
        return dp // self.y, dp % self.y, seq // 2, seq % 2

    def device(self, z, y, x, core):
        return (z * self.y + y, x * 2 + core)

    def others(self, axis):
        z, y, x, core = self.here()
        if axis == "z":
            return [self.device((z + i) % self.z, y, x, core) for i in range(1, self.z)]
        if axis == "y":
            return [self.device(z, (y + i) % self.y, x, core) for i in range(1, self.y)]
        if axis == "x":
            return [self.device(z, y, (x + i) % self.x, core) for i in range(1, self.x)]
        return [self.device(z, y, x, 1 - core)]

    def copies(self):
        return self.z + self.y + self.x - 2

    def greet(self):
        barrier = pltpu.get_barrier_semaphore()
        for axis in "zyxc":
            for device in self.others(axis):
                pl.semaphore_signal(barrier, inc=1, device_id=device, device_id_type=MESH)

    def meet(self):
        pl.semaphore_wait(pltpu.get_barrier_semaphore(), sum(len(self.others(axis)) for axis in "zyxc"))


class Sends:
    def __init__(self, send, recv):
        self.send, self.recv, self.used, self.started = send, recv, 0, []

    def start(self, source, target, device):
        copy = pltpu.make_async_remote_copy(
            src_ref=source,
            dst_ref=target,
            send_sem=self.send.at[self.used],
            recv_sem=self.recv.at[self.used],
            device_id=device,
            device_id_type=MESH,
        )
        self.used += 1
        copy.start()
        self.started.append(copy)
        return copy

    def finish(self):
        for copy in self.started:
            copy.wait_send()


def vmem_specs(count):
    return [pl.BlockSpec(memory_space=pltpu.VMEM)] * count


def any_specs(count):
    return [pl.BlockSpec(memory_space=pl.ANY)] * count


def sentence_bounds(lengths, marks, first):
    start = jnp.zeros(marks.shape, jnp.int32)
    end = jnp.zeros(marks.shape, jnp.int32)
    at = jnp.int32(0)
    for e in range(lengths.shape[1]):
        after = at + lengths[0, e]
        start = jnp.where(marks == first + e, at, start)
        end = jnp.where(marks == first + e, after, end)
        at = after
    return start, end


def in_sentence(positions, start, end):
    return jnp.logical_and(positions >= start, positions < end).astype(f32)


def query_pack(transposed, extra):
    high, low = split(transposed[: transposed.shape[0] // 2])
    return cat([high, low, high, extra.astype(bf16)], 0)


def key_pack(doubled, extra):
    lanes = iota(doubled.shape, 1)
    half = doubled.shape[1] // 2
    high, low = split_wide(doubled)
    return cat([high.astype(bf16), jnp.where(lanes < half, low, extra).astype(bf16)], 1)


def half_split(doubled, axis):
    half = doubled.shape[axis] // 2
    high, low = split_wide(doubled)
    return jnp.where(iota(doubled.shape, axis) < half, high, low).astype(bf16)


def twice(pair):
    half = pair.shape[1] // 2
    turned = pltpu.roll(pair, half, 1)
    lanes = iota(pair.shape, 1)
    return jnp.where(lanes < half, pair, turned), jnp.where(lanes < half, turned, pair)


def pick(wide, route, head):
    lanes = iota((wide.shape[0], 2 * head), 1) // head
    total = None
    for group in range(wide.shape[1] // (2 * head)):
        part = jnp.where(lanes + 2 * group == route, wide[:, group * 2 * head : (group + 1) * 2 * head], 0.0)
        total = part if total is None else total + part
    return total + pltpu.roll(total, head, 1)


def spread(doubled, route, experts):
    head = doubled.shape[1] // 2
    lanes = iota(doubled.shape, 1) // head
    return cat([jnp.where(lanes + 2 * group == route, doubled, 0.0) for group in range(experts // 2)], 1)


def normalise(values):
    centre = values - jnp.mean(values, axis=-1, keepdims=True)
    scale = lax.rsqrt(jnp.mean(centre * centre, axis=-1, keepdims=True) + norm_eps)
    return centre * scale, scale


def norm_back(grad, unit, scale, gain):
    inner = grad * gain
    mean = jnp.mean(inner, axis=-1, keepdims=True)
    along = jnp.mean(inner * unit, axis=-1, keepdims=True)
    return scale * (inner - mean - unit * along)


class Gather:
    def __init__(self, grid, source, target, axes, order, sems):
        self.grid, self.source, self.target, self.axes, self.order = grid, source, target, axes, order
        self.sends, self.local = Sends(*sems[:2]), sems[2]
        self.current, self.own = [], None

    def view(self, **fixed):
        fixed["c"] = self.grid.here()[3]
        return self.target.at[tuple(fixed.get(axis, slice(None)) for axis in self.axes + "c")]

    def start(self):
        z, y, x, core = self.grid.here()
        mine = self.view(z=z, y=y, x=x)
        self.own = pltpu.make_async_copy(self.source, mine, self.local)
        self.own.start()
        self.current = [self.sends.start(self.source, mine, device) for device in self.grid.others("z")]

    def wait(self):
        for copy in self.current:
            copy.wait_recv()
        self.current = []
        if self.own is not None:
            self.own.wait()
            self.own = None

    def step(self, number):
        z, y, x, core = self.grid.here()
        self.wait()
        if number == 0:
            view = self.view(y=y, x=x)
        elif number == 1:
            view = self.view(x=x) if self.order[0] == "y" else self.view(y=y)
        else:
            view = self.view()
        axis = (self.order + "c")[number]
        self.current = [self.sends.start(view, view, device) for device in self.grid.others(axis)]

    def finish(self):
        self.wait()
        self.sends.finish()


class Reduce:
    def __init__(self, grid, source, axes, order, parts, sems):
        self.grid, self.source, self.axes, self.order, self.parts = grid, source, axes, order, parts
        self.sends, self.current, self.done = Sends(*sems[:2]), [], {}

    def view(self, core, **fixed):
        fixed["c"] = core
        return self.source.at[tuple(fixed.get(axis, slice(None)) for axis in self.axes + "c")]

    def start(self):
        core = self.grid.here()[3]
        self.send("c", [self.view(1 - core)], 0)

    def send(self, axis, views, part):
        devices = self.grid.others(axis)
        self.current = [
            self.sends.start(view, self.parts[part].at[i], device)
            for i, (view, device) in enumerate(zip(views, devices))
        ]
        self.part = part

    def take(self):
        core = self.grid.here()[3]
        view = self.view(core, **self.done)
        for copy in self.current:
            copy.wait_recv()
        for i in range(len(self.current)):
            view[...] += self.parts[self.part][i]
        self.current = []

    def step(self, number):
        z, y, x, core = self.grid.here()
        self.take()
        axis = (self.order + "z")[number]
        if axis not in self.axes:
            return
        size, at = {"z": (self.grid.z, z), "y": (self.grid.y, y), "x": (self.grid.x, x)}[axis]
        views = [
            self.view(core, **{**self.done, axis: (at + i) % size}) for i in range(1, size)
        ]
        self.send(axis, views, number + 1)
        self.done = {**self.done, axis: at}

    def result(self):
        self.take()
        return self.view(self.grid.here()[3], **self.done)[...]

    def finish(self):
        self.sends.finish()


def reduce_scratch(grid, shape, axes, order):
    size = {"z": grid.z, "y": grid.y, "x": grid.x}
    dims = lambda names: tuple(size[axis] for axis in axes if axis in names)
    parts = [
        pltpu.VMEM((1,) + dims(axes) + shape, f32),
        pltpu.VMEM((size[order[0]] - 1,) + dims(axes.replace(order[0], "")) + shape, f32),
        pltpu.VMEM((size[order[1]] - 1,) + dims(axes.replace("x", "").replace("y", "")) + shape, f32),
    ]
    if "z" in axes:
        parts.append(pltpu.VMEM((grid.z - 1,) + shape, f32))
    return parts


def copy_sems(count):
    return [pltpu.SemaphoreType.DMA((count,)), pltpu.SemaphoreType.DMA((count,)), pltpu.SemaphoreType.DMA]


gather_orders = (
    ("keys", "yx"),
    ("query0", "xy"),
    ("query1", "xy"),
    ("out", "xy"),
    ("up0", "yx"),
    ("up1", "xy"),
    ("up2", "yx"),
    ("up3", "xy"),
    ("down", "yx"),
    ("down0", "yx"),
    ("down1", "yx"),
    ("down2", "xy"),
    ("down3", "xy"),
)
reduce_orders = (
    ("up0", "yx"),
    ("up1", "xy"),
    ("up2", "xy"),
    ("up3", "xy"),
    ("down0", "yx"),
    ("down1", "xy"),
    ("down2", "yx"),
    ("down3", "yx"),
    ("out", "xy"),
    ("keys", "xy"),
    ("query0", "xy"),
    ("query1", "yx"),
)
moves_at = {
    "queries": "+out0",
    "split": "+up00",
    "own_mid": "+out1 +up01",
    "near_mid": "hand +down +down00 +up10",
    "near_end": "+down20",
    "far_mid": "+out2 +down10",
    "far_end": "+up02 +down01",
    "last_mid": "+up11 +down21 +down30",
    "last_end": "+down11 +up20",
    "mix": "+up30 +down02",
    "part00": "+up12 +down12 +up21 +down22 +up31 +down31",
    "part10": "+up22 -up00 -down00",
    "part11": "+up32 +down32",
    "part21": "-up01 -down01 -up10 -down10",
    "part31": "-up20 -down20",
    "heads_end": "-up02 -down02 -down21 -up30 -down30",
    "back0_mid": "-up11 -down11 -out0",
    "back0_end": "-down31",
    "back1_mid": "-up12 -down12 -up21 -down22",
    "back2_mid": "-up22 -up31 -down32 -out1 shards",
    "back3_mid": "-up32 -out2",
}


def plan_spills(chunks):
    return 6 * chunks


class Plan:
    def __init__(self, grid, span, width, ff, head, experts, columns):
        self.grid, self.span, self.width, self.ff = grid, span, width, ff
        self.head, self.experts, self.columns = head, experts, columns
        self.shard, self.ff_shard = width // grid.count, ff // grid.count
        self.chunks = grid.z
        self.part = ff // self.chunks
        self.pieces = {"keys": (experts * head, columns), "query0": (0, experts * head // 2)}
        self.pieces["query1"] = (experts * head // 2, experts * head)
        part, chunks = self.part, self.chunks
        shard = (self.shard, part)
        ff_shard = (self.ff_shard, width)
        self.gathers = [(name, "yx" if name[:-1] == "down" else "zyx", order) for name, order in gather_orders]
        shapes = {"out": (self.shard, width)}
        for name, (lo, hi) in self.pieces.items():
            shapes[name] = (self.shard, hi - lo)
        self.reduces = []
        for name, order in reduce_orders:
            shape = shapes.get(name, ff_shard if name.startswith("down") else shard)
            self.reduces.append((name, shape, "yx" if name.startswith("down") else "zyx", order))

    def scratch(self):
        grid, span, width, head = self.grid, self.span, self.width, self.head
        lead = grid.lead
        part = self.part
        b, f = lambda *shape: pltpu.VMEM(shape, bf16), lambda *shape: pltpu.VMEM(shape, f32)
        named = dict(
            tokens_v=f(span, width), cot_v=f(span, width), norm_grad=f(span, width),
            cot_h=b(span, width), cot_l=b(span, width), norm_h=b(span, width), norm_l=b(span, width),
            mixed_h=b(span, width), mixed_l=b(span, width), side=f(span, 128), heads=f(span, 2 * head),
            packed=f(self.shard, self.columns), square=f(128, 128),
            front=pltpu.VMEM(lead + (self.shard, self.columns), f32),
            front_h=b(width, self.columns), front_l=b(width, self.columns),
            vectors=f(8, width), vector_grad=f(8, width), bias=f(1, self.ff), bias_grad=f(1, self.ff),
            even=f(grid.count, 128), odd=f(grid.count, 128),
            query_t=b(4 * head, 2 * span), query_n=b(2 * span, 2 * head),
            grad_t=b(4 * head, 2 * span), grad_n=b(2 * span, 2 * head),
            keyval=f(grid.x, 2, span, 2 * head),
            key_p=b(span, 4 * head), value_p=b(span, 4 * head), turned=b(2 * head, span),
            accum=f(2 * head, 2 * span), peak=f(1, 2 * span), total=f(1, 2 * span), logsum=f(1, 2 * span),
            tile_k=f(min(512, span), 2 * head), tile_v=f(min(512, span), 2 * head),
            chunk_grad=f(2 * grid.x, span, 2 * head), chunk_in=f(grid.x, span, 2 * head),
            cross_in=f(max(grid.x - 1, 1), span, 2 * head),
            out=pltpu.VMEM(lead + (self.shard, width), f32), out_h=b(width, width), out_l=b(width, width),
            up=pltpu.VMEM(lead + (self.shard, self.ff), f32), down=pltpu.VMEM(lead + (self.ff_shard, width), f32),
            up_h=b(width, part), up_l=b(width, part), down_h=b(part, width), down_l=b(part, width),
            down_z=f(grid.z - 1, self.ff_shard, width),
            kv_sems=copy_sems(2 * grid.x - 1), chunk_sems=copy_sems(2 * grid.x - 1), down_sems=copy_sems(grid.z - 1),
            io_sems=pltpu.SemaphoreType.DMA((6,)), spill_sems=pltpu.SemaphoreType.DMA((plan_spills(self.chunks),)),
            fill_sems=pltpu.SemaphoreType.DMA((2, 4)),
        )
        copies = grid.z + grid.y + grid.x
        named["gather_sems"] = [copy_sems(copies) for _ in self.gathers]
        named["reduce_sems"] = [copy_sems(copies) for _ in self.reduces]
        named["reduce_parts"] = [
            reduce_scratch(grid, shape, axes, order) for _, shape, axes, order in self.reduces
        ]
        return named


def attention_sides(plan, lengths, at, count, offset):
    marks = iota((1, 2 * plan.head), 1) - plan.head
    start, end = sentence_bounds(lengths, marks, 0)
    positions = at + offset + iota((count, 1), 0)
    outside = (in_sentence(positions, start, end) - 1.0) * far
    return marks, jnp.where(jnp.logical_and(marks >= 0, marks < lengths.shape[1]), outside, 0.0)


def three(values):
    one = values.astype(bf16).astype(f32)
    two = (values - one).astype(bf16).astype(f32)
    return one, two, values - one - two


def step_kernel(plan, tree, lengths, query_w, kv_w, router_t, vectors_w, bias_w, routes_t,
                tokens, cotangent, out_w, up_w, down_w,
                output, input_grad, hidden_hh, hidden_hl, down_hh, down_hl, front_sum, up_sum, down_sum, out_sum,
                *scratch):
    s = types.SimpleNamespace(**jax.tree.unflatten(tree, scratch))
    grid, span, width, head, experts = plan.grid, plan.span, plan.width, plan.head, plan.experts
    ff, part, chunks, columns = plan.ff, plan.part, plan.chunks, plan.columns
    wide = experts * head
    z, y, x, core = grid.here()
    seq_at = (x * 2 + core) * span
    block = min(256, span)
    blocks = span // block

    load_tokens = pltpu.make_async_copy(tokens, s.tokens_v, s.io_sems.at[0])
    load_tokens.start()
    load_cot = pltpu.make_async_copy(cotangent, s.cot_v, s.io_sems.at[1])
    load_cot.start()

    grid.greet()
    s.square[...] = jnp.zeros_like(s.square)
    s.square[0:experts, 0 : plan.shard] = router_t[...]
    s.square[experts : experts + vectors_w.shape[0], 0 : plan.shard] = vectors_w[...]
    s.packed[:, :wide] = query_w[...]
    s.packed[:, wide : wide + 2 * head] = kv_w[...]
    s.packed[:, wide + 2 * head :] = s.square[...].T[: plan.shard]
    piece = ff // grid.count
    s.packed[0:1, columns - piece :] = bias_w[...]

    sources = {"out": (out_w, s.out), "down": (down_w, s.down)}
    for name, (lo, hi) in plan.pieces.items():
        sources[name] = (s.packed.at[:, lo:hi], s.front.at[:, :, :, :, :, lo:hi])
    for j in range(chunks):
        cols = slice(j * part, (j + 1) * part)
        sources["up%d" % j] = (up_w.at[:, cols], s.up.at[:, :, :, :, :, cols])
        sources["down%d" % j] = (None, s.down.at[j])
    g = {
        name: Gather(grid, *sources[name], axes, order, sems)
        for (name, axes, order), sems in zip(plan.gathers, s.gather_sems)
    }
    targets = {name: target for name, (_, target) in sources.items()}
    r = {
        name: Reduce(grid, targets[name], axes, order, parts, sems)
        for (name, _, axes, order), parts, sems in zip(plan.reduces, s.reduce_parts, s.reduce_sems)
    }

    grid.meet()
    g["keys"].start()

    def routes_block(i, carry):
        cols = rows_at(i, block)
        pair = routes_t[:, cols].astype(f32)
        tall = cat([pair, jnp.zeros((126, block), f32)], 0)
        s.side[cols] = tall.T
        return carry

    def unit_block(i, carry):
        rows = rows_at(i, block)
        s.norm_grad[rows] = normalise(s.tokens_v[rows])[0]
        return carry

    def cot_block(i, carry):
        rows = rows_at(i, block)
        s.cot_h[rows], s.cot_l[rows] = split(s.cot_v[rows])
        return carry

    keys, queries = g["keys"], [g["query0"], g["query1"]]
    lax.fori_loop(0, blocks, routes_block, 0, unroll=2)
    keys.step(0)
    for item in queries:
        item.start()
    load_tokens.wait()
    lax.fori_loop(0, blocks // 2, unit_block, 0, unroll=2)
    keys.step(1)
    for item in queries:
        item.step(0)
    for name in ("out", "up0", "down"):
        g[name].start()
    lax.fori_loop(blocks // 2, blocks, unit_block, 0, unroll=2)
    keys.step(2)
    for item in queries:
        item.step(1)
    load_cot.wait()
    lax.fori_loop(0, blocks // 2, cot_block, 0, unroll=2)
    keys.wait()

    def front_part(name):
        lo, hi = plan.pieces[name]
        part_w = s.front[:, :, :, :, :, lo:hi].reshape(width, hi - lo)
        s.front_h[:, lo:hi], s.front_l[:, lo:hi] = split(part_w)
        return part_w

    tail = front_part("keys")[:, 2 * head :]
    s.vectors[...] = tail.T[experts : experts + 8]
    gain, shift = s.vectors[0:1], s.vectors[1:2]

    def route_of(rows, k):
        return s.side[rows, k : k + 1].astype(jnp.int32)

    def project_keys(i, carry):
        rows = rows_at(i, block)
        normed_s = split(s.norm_grad[rows] * gain + shift)
        s.norm_h[rows], s.norm_l[rows] = normed_s
        result = dot_nn(normed_s, (s.front_h[:, wide:], s.front_l[:, wide:]))
        s.keyval[x, core, rows] = result[:, : 2 * head]
        lane = iota((block, 2 * head), 1)
        logits = result[:, 2 * head :]
        chosen = [
            jnp.sum(jnp.where(lane == route_of(rows, k), logits, 0.0), axis=1, keepdims=True) for k in range(2)
        ]
        top = jnp.maximum(chosen[0], chosen[1])
        raw = [jnp.exp(c - top) for c in chosen]
        norm = raw[0] + raw[1]
        s.side[rows, 2:4] = cat([raw[0] / norm, raw[1] / norm], 1)
        return carry

    lax.fori_loop(0, blocks, project_keys, 0, unroll=2)
    moves = Sends(*s.kv_sems[:2])
    mine = s.keyval.at[x, core]
    sibling = grid.others("c")[0]
    to_sibling = moves.start(mine, mine, sibling)
    across = [moves.start(mine, mine, device) for device in grid.others("x")]
    for item in queries:
        item.step(2)
    for j in range(1, chunks):
        g["up%d" % j].start()
    forwards = {}

    def hand_on(i):
        across[i - 1].wait_recv()
        view = s.keyval.at[(x - i + grid.x) % grid.x, core]
        forwards[i] = moves.start(view, view, sibling)

    down_moves = Sends(*s.down_sems[:2])
    down_last = []

    def tick(name):
        for move in moves_at.get(name, "").split():
            if move == "hand":
                hand_on(1)
            elif move == "+down":
                g["down"].wait()
            elif move == "shards":
                for i, device in enumerate(grid.others("z")):
                    source = s.down.at[(z + i + 1) % grid.z, y, x, core]
                    down_last.append(down_moves.start(source, s.down_z.at[i], device))
            else:
                (g if move[0] == "+" else r)[move[1:-1]].step(int(move[-1]))

    tick("queries")
    lax.fori_loop(blocks // 2, blocks, cot_block, 0, unroll=2)
    for item in queries:
        item.wait()
    front_part("query0")
    front_part("query1")
    lanes = iota((1, 128), 1)
    for p in range(grid.count):
        s.odd[p : p + 1] = tail[p * plan.shard : p * plan.shard + 1]
    s.even[...] = pltpu.roll(s.odd[...], piece, 1)
    per_tile = 128 // piece
    for q in range(ff // 128):
        s.bias[0:1, q * 128 : (q + 1) * 128] = jnp.where(
            lanes < piece, s.even[per_tile * q : per_tile * q + 1], s.odd[per_tile * q + 1 : per_tile * q + 2]
        )

    def project_queries(i, carry):
        rows = rows_at(i, block)
        result = dot_nn((s.norm_h[rows], s.norm_l[rows]), (s.front_h[:, :wide], s.front_l[:, :wide]))
        marks = iota((head, 1), 0)
        start, end = sentence_bounds(lengths, marks, 0)
        positions = seq_at + i * block + iota((1, block), 1)
        inside = in_sentence(positions, start, end)
        for k in range(2):
            query = pick(result, route_of(rows, k), head) * (log2e * head**-0.5)
            at = rows_at(k * blocks + i, block)
            s.query_n[at] = half_split(query, 1)
            s.query_t[:, at] = query_pack(query.T, inside)
        return carry

    tick("split")
    lax.fori_loop(0, blocks, project_queries, 0, unroll=2)
    for item in [keys] + queries:
        item.finish()

    s.accum[...] = jnp.zeros_like(s.accum)
    s.peak[...] = jnp.full_like(s.peak, -3e38)
    s.total[...] = jnp.zeros_like(s.total)
    t_tile = width
    t_count = 2 * span // t_tile

    def attend(chunk_x, chunk_core, name):
        at = (chunk_x * 2 + chunk_core) * span

        def prepare(i, carry):
            rows = rows_at(i, block)
            keys, values = twice(s.keyval[chunk_x, chunk_core, rows])
            _, outside = attention_sides(plan, lengths, at, block, i * block)
            s.key_p[rows] = key_pack(keys, outside)
            s.turned[:, rows] = half_split(values.T, 0)
            return carry

        lax.fori_loop(0, blocks, prepare, 0, unroll=2)

        def tile(i, carry):
            cols = rows_at(i, t_tile)
            s.norm_grad[...] = dot(s.key_p[...], s.query_t[:, cols])
            old = s.peak[0:1, cols]
            new = jnp.maximum(old, jnp.max(s.norm_grad[...], axis=0, keepdims=True))
            fade = jnp.exp2(old - new)
            probs = jnp.exp2(s.norm_grad[...] - new)
            high, low = split(probs)
            weights = s.turned[...]
            add = dot(cat([weights, weights], 1), cat([high, low], 0))
            s.total[0:1, cols] = s.total[0:1, cols] * fade + jnp.sum(probs, axis=0, keepdims=True)
            s.accum[:, cols] = s.accum[:, cols] * fade + add
            s.peak[0:1, cols] = new
            return carry

        lax.fori_loop(0, t_count // 2, tile, 0, unroll=2)
        tick(name + "_mid")
        lax.fori_loop(t_count // 2, t_count, tile, 0, unroll=2)
        tick(name + "_end")

    attend(x, core, "own")
    to_sibling.wait_recv()
    attend(x, 1 - core, "near")
    for i in range(1, grid.x):
        if i not in forwards:
            hand_on(i)
        attend((x - i + grid.x) % grid.x, core, "far" if i == 1 else "")
        forwards[i].wait_recv()
        attend((x - i + grid.x) % grid.x, 1 - core, "last" if i == 1 else "")

    def finish(i, carry):
        marks = iota((16, 1), 0)
        start, end = sentence_bounds(lengths, marks, 0)
        positions = seq_at + i * block + iota((1, block), 1)
        inside = in_sentence(positions, start, end)
        results = []
        for k in range(2):
            cols = rows_at(k * blocks + i, block)
            norm = s.total[0:1, cols]
            results.append((s.accum[:head, cols] + s.accum[head:, cols]) / norm)
            side = inside
            for n, term in enumerate(three(-(s.peak[0:1, cols] + jnp.log2(norm)))):
                side = jnp.where(marks == 8 + n, term, side)
            s.query_t[3 * head : 3 * head + 16, cols] = side.astype(bf16)
        s.heads[rows_at(i, block)] = cat(results, 0).T
        return carry

    lax.fori_loop(0, blocks, finish, 0, unroll=2)
    tick("finish")
    g["out"].finish()
    s.out_h[...], s.out_l[...] = split(s.out[...].reshape(width, width))
    gain2, shift2, last = s.vectors[2:3], s.vectors[3:4], s.vectors[4:5]

    def gate_pair(rows):
        return [s.side[rows, 2 + k : 3 + k] for k in range(2)]

    def mixed_heads(rows, gate):
        mixed = None
        for k, doubled in enumerate(twice(s.heads[rows])):
            own = gate[k] * doubled
            wide_part = spread(own, route_of(rows, k), experts)
            mixed = wide_part if mixed is None else mixed + wide_part
        return split(mixed)

    def mix(i, carry):
        rows = rows_at(i, block)
        mixed_s = mixed_heads(rows, gate_pair(rows))
        middle = s.tokens_v[rows] + dot_nn(mixed_s, (s.out_h[...], s.out_l[...]))
        unit, scale = normalise(middle)
        s.cot_v[rows] = unit
        s.side[rows, 6:7] = scale
        s.norm_h[rows], s.norm_l[rows] = split(unit * gain2 + shift2)
        s.tokens_v[rows] = middle + last
        s.norm_grad[rows] = jnp.zeros((block, width), f32)
        return carry

    lax.fori_loop(0, blocks, mix, 0, unroll=2)
    tick("mix")
    store_middle = pltpu.make_async_copy(s.tokens_v, output, s.io_sems.at[2])
    store_middle.start()

    up_rows, down_rows = s.up.reshape(width, ff), s.down.reshape(ff, width)
    row_block = min(512, span)

    def hidden_part(j, i):
        rows = slice(i * row_block, (i + 1) * row_block)
        cols = slice(j * part, (j + 1) * part)
        cot_s = (s.cot_h[rows], s.cot_l[rows])
        norm_s = (s.norm_h[rows], s.norm_l[rows])
        up_s = (s.up_h[...], s.up_l[...])
        down_s = (s.down_h[...], s.down_l[...])
        pre = dot_nn(norm_s, up_s) + s.bias[0:1, cols]
        back = dot_nt(cot_s, down_s)
        square = pre * pre
        wave = jnp.tanh(math.sqrt(2.0 / math.pi) * (pre + 0.044715 * (square * pre)))
        half_wave = 0.5 * (1.0 + wave)
        hidden_s = split(pre * half_wave)
        slope = half_wave + (0.5 * math.sqrt(2.0 / math.pi)) * pre * (1.0 - wave * wave) * (
            1.0 + (3.0 * 0.044715) * square
        )
        pre_grad = back * slope
        pre_s = split(pre_grad)
        s.mixed_h[rows], s.mixed_l[rows] = hidden_s
        s.norm_grad[rows] += dot_nt(pre_s, up_s)
        down_part = dot_tn(hidden_s, cot_s)
        up_part = dot_tn(norm_s, pre_s)
        bias_part = jnp.sum(pre_grad, axis=0, keepdims=True)
        if i == 0:
            down_rows[cols] = down_part
            up_rows[:, cols] = up_part
            s.bias_grad[0:1, cols] = bias_part
        else:
            down_rows[cols] += down_part
            up_rows[:, cols] += up_part
            s.bias_grad[0:1, cols] += bias_part

    spills, spill_count = {}, [0]

    def spill(*pairs):
        copies = []
        for source, target in pairs:
            copies.append(pltpu.make_async_copy(source, target, s.spill_sems.at[spill_count[0]]))
            copies[-1].start()
            spill_count[0] += 1
        return copies

    def fill(slot, j):
        pairs = zip((hidden_hh, hidden_hl, down_hh, down_hl), slots[slot])
        copies = [
            pltpu.make_async_copy(source.at[j], target, s.fill_sems.at[slot, n])
            for n, (source, target) in enumerate(pairs)
        ]
        for copy in copies:
            copy.start()
        return copies

    slots = [(s.cot_h, s.cot_l, s.down_h, s.down_l), (s.norm_h, s.norm_l, s.up_h, s.up_l)]

    for j in range(chunks):
        cols = slice(j * part, (j + 1) * part)
        if j == 0:
            g["down"].finish()
        g["up%d" % j].finish()
        g["down%d" % j].finish()
        s.up_h[...], s.up_l[...] = split(up_rows[:, cols])
        for copy in spills.pop("weights", []):
            copy.wait()
        s.down_h[...], s.down_l[...] = split(down_rows[cols])
        spills["weights"] = spill((s.down_h, down_hh.at[j]), (s.down_l, down_hl.at[j]))
        for i in range(span // row_block):
            for copy in spills.pop(i, []):
                copy.wait()
            hidden_part(j, i)
            rows = slice(i * row_block, (i + 1) * row_block)
            spills[i] = spill(
                (s.mixed_h.at[rows], hidden_hh.at[j, rows]), (s.mixed_l.at[rows], hidden_hl.at[j, rows])
            )
            if i + 1 == span // row_block:
                r["up%d" % j].start()
                r["down%d" % j].start()
            tick("part%d%d" % (j, i))

    store_middle.wait()
    load_tokens = pltpu.make_async_copy(tokens, s.tokens_v, s.io_sems.at[3])
    load_tokens.start()
    for copies in spills.values():
        for copy in copies:
            copy.wait()
    s.vector_grad[...] = jnp.zeros_like(s.vector_grad)
    out_rows = s.out.reshape(width, width)

    def heads_block(i, carry):
        rows = rows_at(i, block)
        grad = s.norm_grad[rows]
        unit = s.cot_v[rows]
        cot = s.cot_h[rows].astype(f32) + s.cot_l[rows].astype(f32)
        s.vector_grad[2:3] += jnp.sum(grad * unit, axis=0, keepdims=True)
        s.vector_grad[3:4] += jnp.sum(grad, axis=0, keepdims=True)
        s.vector_grad[4:5] += jnp.sum(cot, axis=0, keepdims=True)
        mid = cot + norm_back(grad, unit, s.side[rows, 6:7], gain2)
        s.norm_grad[rows] = mid
        mid_s = split(mid)
        s.norm_h[rows], s.norm_l[rows] = mid_s
        grad_mixed = dot_nt(mid_s, (s.out_h[...], s.out_l[...]))
        gate = gate_pair(rows)
        s.mixed_h[rows], s.mixed_l[rows] = mixed_heads(rows, gate)
        lane = iota((block, 2 * head), 1)
        marks = iota((head, 1), 0)
        gates_grad = []
        for k, doubled in enumerate(twice(s.heads[rows])):
            at = rows_at(k * blocks + i, block)
            picked = pick(grad_mixed, route_of(rows, k), head)
            gate_grad = jnp.sum(jnp.where(lane < head, picked * doubled, 0.0), axis=1, keepdims=True)
            gates_grad.append(gate_grad)
            own = gate[k] * picked
            s.grad_n[at] = half_split(own, 1)
            turned = jnp.where(lane < head, own, gate_grad * gate[k]).T
            side = jnp.zeros((head, block), f32)
            for n, term in enumerate(three(-turned[head : head + 1])):
                side = jnp.where(marks == n, term, side)
            s.grad_t[:, at] = query_pack(turned, side)
        both = gate[0] * gates_grad[0] + gate[1] * gates_grad[1]
        s.side[rows, 4:6] = cat([gate[k] * (gates_grad[k] - both) for k in range(2)], 1)
        return carry

    lax.fori_loop(0, blocks // 2, heads_block, 0, unroll=2)
    tick("heads_mid")
    lax.fori_loop(blocks // 2, blocks, heads_block, 0, unroll=2)
    out_rows[...] = dot_tn((s.mixed_h[...], s.mixed_l[...]), (s.norm_h[...], s.norm_l[...]))
    r["out"].start()
    tick("heads_end")
    filled = [fill(0, 0), None]

    s.accum[...] = jnp.zeros_like(s.accum)
    s_tile = min(512, span)

    def chunk(chunk_x, chunk_core, target, name):
        at = (chunk_x * 2 + chunk_core) * span

        def prepare(i, carry):
            rows = rows_at(i, block)
            keys, values = twice(s.keyval[chunk_x, chunk_core, rows])
            marks, outside = attention_sides(plan, lengths, at, block, i * block)
            ones = jnp.logical_and(marks >= 8, marks < 11)
            s.key_p[rows] = key_pack(keys, jnp.where(ones, 1.0, outside))
            few = jnp.logical_and(marks >= 0, marks < 3).astype(f32)
            s.value_p[rows] = key_pack(values, jnp.broadcast_to(few, values.shape))
            s.turned[:, rows] = half_split(keys.T, 0)
            return carry

        lax.fori_loop(0, blocks, prepare, 0, unroll=2)
        for i in range(span // s_tile):
            s_rows = slice(i * s_tile, (i + 1) * s_tile)
            s.tile_k[...] = jnp.zeros_like(s.tile_k)
            s.tile_v[...] = jnp.zeros_like(s.tile_v)

            def tile(j, carry):
                cols = rows_at(j, t_tile)
                probs = jnp.exp2(dot(s.key_p[s_rows], s.query_t[:, cols]))
                probs_h, probs_l = split(probs)
                grads = probs * dot(s.value_p[s_rows], s.grad_t[:, cols])
                grads_h, grads_l = split(grads)
                grad_rows, query_rows = s.grad_n[cols], s.query_n[cols]
                s.tile_v[...] += dot(cat([probs_h, probs_l], 1), cat([grad_rows, grad_rows], 0))
                s.tile_k[...] += dot(cat([grads_h, grads_l], 1), cat([query_rows, query_rows], 0))
                keys = s.turned[:, s_rows]
                s.accum[:, cols] += dot(cat([keys, keys], 1), cat([grads_h, grads_l], 0))
                return carry

            lax.fori_loop(0, t_count, tile, 0, unroll=4)
            lane = iota((s_tile, 2 * head), 1)
            k_part, v_part = s.tile_k[...], s.tile_v[...]
            target[s_rows] = jnp.where(
                lane < head,
                (k_part + pltpu.roll(k_part, head, 1)) * (1.0 / log2e),
                v_part + pltpu.roll(v_part, head, 1),
            )
            if i == 0:
                tick(name + "_mid")

    moves_back = Sends(*s.chunk_sems[:2])
    crossing = []
    for i in range(1, grid.x):
        there = (x + i) % grid.x
        chunk(there, 1 - core, s.chunk_grad.at[2 * i], "back0" if i == 1 else "")
        over = moves_back.start(s.chunk_grad.at[2 * i], s.chunk_in.at[i], sibling)
        if i == 1:
            tick("back0_end")
        chunk(there, core, s.chunk_grad.at[2 * i + 1], "back1" if i == 1 else "")
        over.wait_recv()
        s.chunk_grad[2 * i + 1] += s.chunk_in[i]
        crossing.append(
            moves_back.start(s.chunk_grad.at[2 * i + 1], s.cross_in.at[i - 1], grid.others("x")[i - 1])
        )
        if i == 1:
            tick("back1_end")
    chunk(x, 1 - core, s.chunk_grad.at[0], "back2")
    over = moves_back.start(s.chunk_grad.at[0], s.chunk_in.at[0], sibling)
    chunk(x, core, s.chunk_grad.at[1], "back3")
    over.wait_recv()
    for copy in crossing:
        copy.wait_recv()
    own = s.chunk_grad.at[1]
    own[...] += s.chunk_in[0]
    for i in range(1, grid.x):
        own[...] += s.cross_in[i - 1]
    load_tokens.wait()

    front_rows = s.front.reshape(width, columns)

    def collect(i, carry):
        rows = rows_at(i, block)
        unit, scale = normalise(s.tokens_v[rows])
        s.cot_v[rows] = unit
        s.side[rows, 6:7] = scale
        s.norm_h[rows], s.norm_l[rows] = split(unit)
        total = None
        for k in range(2):
            cols = rows_at(k * blocks + i, block)
            grad = (s.accum[:head, cols] + s.accum[head:, cols]) * (head**-0.5)
            grad = cat([grad, grad], 0).T
            wide_part = spread(grad, route_of(rows, k), experts)
            total = wide_part if total is None else total + wide_part
        s.mixed_h[rows], s.mixed_l[rows] = split(total)
        sums = jnp.sum(total, axis=0, keepdims=True)
        s.sums[:, :wide] = jnp.where(i == 0, 0.0, s.sums[:, :wide]) + sums
        return carry

    def collect_rest(i, carry):
        rows = rows_at(i, block)
        lane = iota((block, 2 * head), 1)
        logits = jnp.zeros((block, 2 * head), f32)
        for k in range(2):
            logits = logits + jnp.where(lane == route_of(rows, k), s.side[rows, 4 + k : 5 + k], 0.0)
        total = cat([own[rows], logits], 1)
        s.rest_h[rows], s.rest_l[rows] = split(total)
        sums = jnp.sum(total, axis=0, keepdims=True)
        s.sums[:, wide:] = jnp.where(i == 0, 0.0, s.sums[:, wide:]) + sums
        return carry

    gain_c, shift_c = s.vectors[...].T[:, 0:1], s.vectors[...].T[:, 1:2]

    def front_grad(lo, hi, grads):
        base = dot_tn((s.norm_h[...], s.norm_l[...]), (grads[0][...], grads[1][...]))
        weight = s.front_h[:, lo:hi].astype(f32) + s.front_l[:, lo:hi].astype(f32)
        sums = s.sums[0:1, lo:hi]
        front_rows[:, lo:hi] = gain_c * base + shift_c * sums
        return jnp.sum(weight * base, axis=1, keepdims=True), jnp.sum(weight * sums, axis=1, keepdims=True)

    lax.fori_loop(0, blocks, collect, 0, unroll=2)
    load_middle = pltpu.make_async_copy(output, s.tokens_v, s.io_sems.at[5])
    load_middle.start()
    gain_q, shift_q = front_grad(0, wide, (s.mixed_h, s.mixed_l))
    late = [r["query0"], r["query1"]]
    for item in late:
        item.start()
    lax.fori_loop(0, blocks, collect_rest, 0, unroll=2)
    gain_r, shift_r = front_grad(wide, columns, (s.rest_h, s.rest_l))
    filled[1] = fill(1, 1)
    lane = iota((width, 128), 1)
    others = cat([jnp.zeros((experts, width), f32), s.vector_grad[...], jnp.zeros((120 - experts, width), f32)], 0).T
    tail_grad = front_rows[:, wide + 2 * head :] + others
    tail_grad = jnp.where(
        lane == experts, gain_q + gain_r, jnp.where(lane == experts + 1, shift_q + shift_r, tail_grad)
    )
    front_rows[:, wide + 2 * head :] = tail_grad
    for q in range(ff // 128):
        both = s.bias_grad[0:1, q * 128 : (q + 1) * 128]
        for n, row in enumerate((pltpu.roll(both, piece, 1), both)):
            at = (per_tile * q + n) * plan.shard
            old = front_rows[at : at + 1, wide + 2 * head :]
            front_rows[at : at + 1, wide + 2 * head :] = jnp.where(lanes < piece, old, row)
    r["keys"].start()
    for item in late:
        item.step(0)

    def input_block(i, carry):
        rows = rows_at(i, block)
        parts = [cat([s.mixed_h[rows], s.rest_h[rows]], 1), cat([s.mixed_l[rows], s.rest_l[rows]], 1)]
        grad = dot_nt(parts, (s.front_h[...], s.front_l[...]))
        s.norm_grad[rows] += norm_back(grad, s.cot_v[rows], s.side[rows, 6:7], gain)
        return carry

    def output_part(j):
        slot = j % 2
        for copy in filled[slot]:
            copy.wait()
        hidden_h, hidden_l, weight_h, weight_l = slots[slot]

        def output_block(i, carry):
            rows = rows_at(i, block)
            s.tokens_v[rows] += dot_nn((hidden_h[rows], hidden_l[rows]), (weight_h[...], weight_l[...]))
            return carry

        lax.fori_loop(0, blocks, output_block, 0, unroll=2)
        if j + 2 < chunks:
            filled[slot] = fill(slot, j + 2)

    lax.fori_loop(0, blocks // 2, input_block, 0, unroll=2)
    r["keys"].step(0)
    lax.fori_loop(blocks // 2, blocks, input_block, 0, unroll=2)
    store_input = pltpu.make_async_copy(s.norm_grad, input_grad, s.io_sems.at[4])
    store_input.start()
    for item in late:
        item.step(1)
    load_middle.wait()
    output_part(0)
    r["keys"].step(1)
    output_part(1)
    for item in late:
        item.step(2)
    output_part(2)
    r["keys"].step(2)
    for j in range(3, chunks):
        output_part(j)
    store_output = pltpu.make_async_copy(s.tokens_v, output, s.io_sems.at[2])
    store_output.start()
    for j in range(chunks):
        up_sum[:, j * part : (j + 1) * part] = r["up%d" % j].result()
    for copy in down_last:
        copy.wait_recv()
    down_total = s.down[z, y, x, core]
    for i in range(grid.z - 1):
        down_total = down_total + s.down_z[i]
    down_sum[...] = down_total
    out_sum[...] = r["out"].result()
    for name, (lo, hi) in plan.pieces.items():
        front_sum[:, lo:hi] = r[name].result()
    store_input.wait()
    store_output.wait()
    for item in r.values():
        item.finish()
    moves.finish()
    moves_back.finish()
    down_moves.finish()


def step_call(plan, lengths, small, big):
    span, width = big[0].shape
    shapes = [(plan.shard, plan.columns), (plan.shard, plan.ff), (plan.ff_shard, width), (plan.shard, width)]
    spill = [(plan.chunks, span, plan.part)] * 2 + [(plan.chunks, plan.part, width)] * 2
    named = plan.scratch()
    named["rest_h"] = pltpu.VMEM((span, plan.columns - plan.experts * plan.head), bf16)
    named["rest_l"] = pltpu.VMEM((span, plan.columns - plan.experts * plan.head), bf16)
    named["sums"] = pltpu.VMEM((1, plan.columns), f32)
    is_leaf = lambda item: not isinstance(item, (dict, list))
    scratch, tree = jax.tree.flatten(named, is_leaf=is_leaf)
    return pl.pallas_call(
        functools.partial(step_kernel, plan, tree),
        out_shape=[jax.ShapeDtypeStruct((span, width), f32)] * 2
        + [jax.ShapeDtypeStruct(shape, bf16) for shape in spill]
        + [jax.ShapeDtypeStruct(shape, f32) for shape in shapes],
        in_specs=[pl.BlockSpec(memory_space=pltpu.SMEM)] + vmem_specs(len(small)) + any_specs(len(big)),
        out_specs=any_specs(6) + vmem_specs(4),
        scratch_shapes=scratch,
        compiler_params=pltpu.CompilerParams(
            collective_id=0, has_side_effects=True, vmem_limit_bytes=vmem_limit
        ),
        name="training_step",
    )(lengths, *small, *big)


def update_kernel(factor, head, *refs):
    raw, small, results = refs[:2], refs[2:30], refs[30:56]
    held_raw, held, made = refs[56], refs[57:85], refs[85:109]
    load_sems, store_sems, raw_load_sems, raw_store_sems = refs[109:]
    loads = [pltpu.make_async_copy(a, b, load_sems.at[i]) for i, (a, b) in enumerate(zip(small, held))]
    rows = held_raw.shape[1]
    count = held_raw.shape[0] // 2
    moves = [
        (source.at[i * rows : (i + 1) * rows], target.at[i * rows : (i + 1) * rows])
        for source, target in zip(raw, results[:2])
        for i in range(count)
    ]
    raw_loads = [pltpu.make_async_copy(m[0], held_raw.at[i], raw_load_sems.at[i]) for i, m in enumerate(moves)]
    raw_stores = [pltpu.make_async_copy(held_raw.at[i], m[1], raw_store_sems.at[i]) for i, m in enumerate(moves)]
    for load in raw_loads + loads:
        load.start()
    for load, store in zip(raw_loads, raw_stores):
        load.wait()
        store.start()
    for load in loads:
        load.wait()
    front, up, down, out = held[:4]
    weights, moments, averages = held[4:12], held[12:20], held[20:28]
    new_weights, new_moments, new_averages = made[:8], made[8:16], made[16:24]
    wide = out.shape[1]
    tail = front[:, wide + 2 * head :]
    experts = weights[0].shape[0]
    shard = tail.shape[0]
    square = cat([tail, jnp.zeros((128 - shard, 128), f32)], 0).T
    piece = weights[5].shape[1]
    gradients = [
        square[:experts, :shard],
        front[:, :wide],
        out[...],
        front[:, wide : wide + 2 * head],
        up[...],
        pltpu.roll(tail[0:8], piece, 1)[0:1, :piece],
        down[...],
        square[experts : experts + weights[7].shape[0], :shard],
    ]
    for i, gradient in enumerate(gradients):
        scaled = gradient * factor
        moment = moment_decay * moments[i][...] + scaled
        weight = weights[i][...] - step_rate * (scaled + moment_decay * moment)
        new_moments[i][...] = moment
        new_weights[i][...] = weight
        new_averages[i][...] = average_decay * averages[i][...] + (1.0 - average_decay) * weight
    stores = [pltpu.make_async_copy(a, b, store_sems.at[i]) for i, (a, b) in enumerate(zip(made, results[2:]))]
    for store in stores:
        store.start()
    for store in stores + raw_stores:
        store.wait()


def update_all(factor, head, raw_output, raw_input, front, up, down, out, weights, moments, averages):
    def flat(arrays):
        return [arrays[0].T] + [a.reshape(1, -1) if a.ndim == 1 else a for a in arrays[1:]]

    shapes = [a.shape for a in weights]
    weights, moments, averages = flat(weights), flat(moments), flat(averages)
    small = [front, up, down, out, *weights, *moments, *averages]
    results = pl.pallas_call(
        functools.partial(update_kernel, factor, head),
        out_shape=[jax.ShapeDtypeStruct(raw_output.shape, f32)] * 2
        + [jax.ShapeDtypeStruct(a.shape, f32) for a in weights] * 3,
        in_specs=any_specs(30),
        out_specs=any_specs(26),
        scratch_shapes=[pltpu.VMEM((8, raw_output.shape[0] // 4, raw_output.shape[1]), f32)]
        + [pltpu.VMEM(a.shape, f32) for a in small]
        + [pltpu.VMEM(a.shape, f32) for a in weights] * 3
        + [pltpu.SemaphoreType.DMA((28,)), pltpu.SemaphoreType.DMA((24,))]
        + [pltpu.SemaphoreType.DMA((8,)), pltpu.SemaphoreType.DMA((8,))],
        compiler_params=pltpu.CompilerParams(vmem_limit_bytes=vmem_limit),
        name="update",
    )(raw_output, raw_input, *small)
    updated = [a.T if i % 8 == 0 else a.reshape(shapes[i % 8]) for i, a in enumerate(results[2:])]
    return (results[0][None], results[1][None]) + tuple(updated)


def fused_step(grid, tokens, cotangent, lengths, routes, *params):
    weights, moments, averages = params[:8], params[8:16], params[16:24]
    router_weight, query_weight, out_weight, kv_weight, up_weight, up_bias, down_weight, vectors = weights
    experts = router_weight.shape[1]
    head = kv_weight.shape[1] // 2
    columns = query_weight.shape[1] + 2 * head + 128
    plan = Plan(grid, tokens.shape[1], tokens.shape[2], up_weight.shape[1], head, experts, columns)
    small = (query_weight, kv_weight, router_weight.T, vectors, up_bias[None], routes[0].T)
    big = (tokens[0], cotangent[0], out_weight, up_weight, down_weight)
    raw_output, raw_input, _, _, _, _, front, up, down, out = step_call(plan, lengths, small, big)
    factor = 1.0 / math.sqrt(tokens.shape[0] * tokens.shape[1] * grid.count)
    return update_all(factor, head, raw_output, raw_input, front, up, down, out, weights, moments, averages)


def step_for(mesh):
    grid = Grid(mesh)

    def step(*args):
        shard, span = args[4].shape[0], args[0].shape[1]
        if shard % 8 == 0 and span % 512 == 0 and grid.x > 1 and grid.z == 4 and args[9].shape[0] == 64:
            return fused_step(grid, *args)
        return general_step(*args)

    return step


def solution(mesh):
    in_specs = (
        P("dp", "seq", None),
        P("dp", "seq", None),
        P("dp", None),
        P("dp", "seq", None),
        P(("dp", "seq"), None),
        P(("dp", "seq"), None),
        P(("dp", "seq"), None),
        P(("dp", "seq"), None),
        P(("dp", "seq"), None),
        P(("dp", "seq")),
        P(("dp", "seq"), None),
        P(None, ("dp", "seq")),
        P(("dp", "seq"), None),
        P(("dp", "seq"), None),
        P(("dp", "seq"), None),
        P(("dp", "seq"), None),
        P(("dp", "seq"), None),
        P(("dp", "seq")),
        P(("dp", "seq"), None),
        P(None, ("dp", "seq")),
        P(("dp", "seq"), None),
        P(("dp", "seq"), None),
        P(("dp", "seq"), None),
        P(("dp", "seq"), None),
        P(("dp", "seq"), None),
        P(("dp", "seq")),
        P(("dp", "seq"), None),
        P(None, ("dp", "seq")),
    )
    out_specs = (
        P("dp", "seq", None),
        P("dp", "seq", None),
        P(("dp", "seq"), None),
        P(("dp", "seq"), None),
        P(("dp", "seq"), None),
        P(("dp", "seq"), None),
        P(("dp", "seq"), None),
        P(("dp", "seq")),
        P(("dp", "seq"), None),
        P(None, ("dp", "seq")),
        P(("dp", "seq"), None),
        P(("dp", "seq"), None),
        P(("dp", "seq"), None),
        P(("dp", "seq"), None),
        P(("dp", "seq"), None),
        P(("dp", "seq")),
        P(("dp", "seq"), None),
        P(None, ("dp", "seq")),
        P(("dp", "seq"), None),
        P(("dp", "seq"), None),
        P(("dp", "seq"), None),
        P(("dp", "seq"), None),
        P(("dp", "seq"), None),
        P(("dp", "seq")),
        P(("dp", "seq"), None),
        P(None, ("dp", "seq")),
    )
    return jax.shard_map(
        step_for(mesh), mesh=mesh, in_specs=in_specs, out_specs=out_specs, check_vma=False
    )
```
